128 devices in a mesh: row: 8 (over x_lo, y), col: 16 (over z, x_hi, core).
Axes of the slice: x: 4 (x_hi: 2, x_lo: 2; x = x_hi * 2 + x_lo), y: 4, z: 4, core: 2. Of those that a mesh axis runs over, the one named last changes fastest.
Arguments:
- child_update_blocks: bfloat16 [8, 16, 128, 16, 8, 128], P('row', None, None, 'col'), may hold values from -4 to 4
- child_pivot_panel: bfloat16 [8, 16, 128, 16, 128], P('row', None, None, 'col'), may hold values from -1 to 1
- child_map: int32 [4, 64], replicated, may hold values from 0 to 127, as said below
- coupled: int32 [120], replicated, may hold values 0 or 1
- parent_front: bfloat16 [8, 16, 128, 16, 8, 128], P('row', None, None, 'col')
Outputs:
- factored: float32 [8, 16, 128, 16, 8, 128], P('row', None, None, 'col')
The draws below stay inside these ranges and needn't reach their ends.
Inputs may be any that keep to these rules, and one draw needn't show every extreme that they name: `child_map`: the 64 entries of one row are distinct. Each child names exactly 4 parent blocks of each value mod 16; rows 0 and 1 together name every parent block exactly once, and so do rows 2 and 3. For one child and one value of b mod 4, exactly 2 of its blocks b have an entry with each value mod 8; for one child and one value of b mod 8, at most 1 of its blocks b have an entry with one value mod 16, and some value has exactly 1.
All inputs are finite; a program needn't handle non-finite values.
Results may differ from the reference program's by a relative error of at most 0.0015.
The reference program's roundings to bfloat16 on the way count: a program that leaves them out, or rounds other values in their place, can miss the bound.
Values may be sent and summed in bfloat16 or wider, within the bound.
A program may use at most 192 MiB of HBM per device.

```python
import jax
import jax.numpy as jnp
from jax import lax

PARENT = 16384
FRONT_PIVOTS = 1024
BLOCK_ORDER = 128
NBP = 128
PPB = 8
CBB = 64
CHILD_GRID_COLS = 8
PLR = 16
PLC = 8
CHILD_LOCAL_ROWS = 16
CHILD_LOCAL_COLS = 8
N_ROW = 8
N_COL = 16


def draw_child_map(key, part):
    key = jax.random.fold_in(key, 41)
    order_key, parity_key, place_key = jax.random.split(key, 3)
    half_cols = N_COL // 2
    per_rank = CBB // half_cols
    cycles = per_rank // N_ROW
    order_keys = jax.random.split(order_key, 4 * half_cols * cycles)
    orders = jax.vmap(lambda one_key: jax.random.permutation(one_key, N_ROW))(order_keys).reshape(4, half_cols, cycles, N_ROW)
    parity_keys = jax.random.split(parity_key, 4 * N_ROW)
    ranking = jax.vmap(lambda one_key: jax.random.permutation(one_key, half_cols))(parity_keys).reshape(4, N_ROW, half_cols)
    parity = jnp.where(ranking < half_cols // 2, 1, 0).astype(jnp.int32)
    blocks = jnp.arange(CBB, dtype=jnp.int32)
    col_rank = blocks % half_cols
    within = blocks // half_cols
    cycle = within // N_ROW
    children = jnp.arange(4, dtype=jnp.int32)[:, None]
    lowpart = orders[children, col_rank[None, :], cycle[None, :], (within % N_ROW)[None, :]]
    flipped = parity[children, lowpart, col_rank[None, :]]
    residue = lowpart + N_ROW * ((cycle[None, :] + flipped) % 2)
    same = residue[:, :, None] == residue[:, None, :]
    earlier = blocks[None, :] < blocks[:, None]
    ordinal = jnp.sum(jnp.where(same & earlier[None], 1, 0), axis=2)
    local_count = NBP // N_COL
    place_keys = jax.random.split(place_key, 2 * N_COL)
    places = jax.vmap(lambda one_key: jax.random.permutation(one_key, local_count))(place_keys).reshape(2, N_COL, local_count)
    position = children % 2 * (CBB // N_COL) + ordinal
    local_index = places[children // 2, residue, position]
    return (residue + N_COL * local_index).astype(jnp.int32)


def draw_parent_front(key, part):
    key = jax.random.fold_in(key, 23)
    first_key, second_key = jax.random.split(key)
    dims_shape = (N_ROW, PLR, BLOCK_ORDER, N_COL, PLC, BLOCK_ORDER)
    scatter = 1.5 * jax.random.truncated_normal(first_key, -5.0, 5.0, dims_shape, jnp.float32)
    root_pivots = float(FRONT_PIVOTS) ** 0.5
    diagonal = jax.random.uniform(second_key, dims_shape, jnp.float32, 4.0 * root_pivots, 8.0 * root_pivots)
    row_index = (lax.broadcasted_iota(jnp.int32, dims_shape, 1) * N_ROW + lax.broadcasted_iota(jnp.int32, dims_shape, 0)) * BLOCK_ORDER + lax.broadcasted_iota(jnp.int32, dims_shape, 2)
    col_index = (lax.broadcasted_iota(jnp.int32, dims_shape, 4) * N_COL + lax.broadcasted_iota(jnp.int32, dims_shape, 3)) * BLOCK_ORDER + lax.broadcasted_iota(jnp.int32, dims_shape, 5)
    return jnp.where(row_index == col_index, diagonal, scatter).astype(jnp.bfloat16)


def plant(result, own_key, low, largest):
    index_at = [jax.random.randint(jax.random.fold_in(own_key, axis), (), 0, length) for axis, length in enumerate(result.shape)]
    main_axis = result.shape.index(max(result.shape))
    beside = index_at[:main_axis] + [(index_at[main_axis] + 1) % result.shape[main_axis]] + index_at[main_axis + 1:]
    return result.at[tuple(index_at)].set(low).at[tuple(beside)].set(largest)


def shard_levels(key, dims, cuts, low, top_value):
    def one(axis_at, blocks):
        heights = jax.random.uniform(jax.random.fold_in(jax.random.fold_in(key, 6), axis_at), (blocks,), jnp.float32, low / len(cuts), top_value / len(cuts))
        return jnp.repeat(jnp.exp(heights), dims[axis_at] // blocks).reshape((-1,) + (1,) * (len(dims) - axis_at - 1))

    factor_of = one(*cuts[0])
    for cut in cuts[1:]:
        factor_of = factor_of * one(*cut)
    return factor_of


def gaussian(rng, dims, width, bound, shards=(), kind=jnp.bfloat16):
    entries = jax.random.normal(rng, dims, jnp.float32) * width
    if len(shards) > 0:
        entries = shard_levels(rng, dims, shards, -0.22, 0.18) * entries
    return jnp.clip(entries, min=-bound, max=bound).astype(kind)


def setup_inputs(seed: int = 0) -> dict:
    keys = jax.random.split(jax.random.key(seed), 6)
    return {
        "child_update_blocks": gaussian(keys[0], (N_ROW, CHILD_LOCAL_ROWS, BLOCK_ORDER, N_COL, CHILD_LOCAL_COLS, BLOCK_ORDER), 0.3, 4.0, ((0, 8), (3, 16))),
        "child_pivot_panel": gaussian(keys[1], (N_ROW, CHILD_LOCAL_ROWS, BLOCK_ORDER, N_COL, FRONT_PIVOTS // CHILD_GRID_COLS), 0.07, 1.0, ((0, 8), (3, 16))),
        "child_map": draw_child_map(jax.random.fold_in(keys[5], 71), 0),
        "coupled": plant((jax.random.randint(keys[3], (NBP - PPB,), 0, 4) < 3).astype(jnp.int32), jax.random.fold_in(keys[3], 1), 0, 1),
        "parent_front": draw_parent_front(jax.random.fold_in(keys[5], 71), 0),
    }


def natural_order(blocks_array):
    moved = jnp.transpose(blocks_array, (1, 0, 2, 4, 3, 5))
    shape_in = moved.shape
    return moved.reshape(shape_in[0] * shape_in[1] * shape_in[2], shape_in[3] * shape_in[4] * shape_in[5])

def reference(child_update_blocks, child_pivot_panel, child_map, coupled, parent_front):
    half_rows = N_ROW // 2
    half_cols = N_COL // 2
    blocks = natural_order(parent_front).astype(jnp.float32).reshape(NBP, BLOCK_ORDER, NBP, BLOCK_ORDER)
    for row_half in range(2):
        for col_half in range(2):
            update_block = natural_order(child_update_blocks[row_half * half_rows:(row_half + 1) * half_rows, :, :, col_half * half_cols:(col_half + 1) * half_cols])
            portion = child_pivot_panel[row_half * half_rows:(row_half + 1) * half_rows, :, :, col_half * half_cols:(col_half + 1) * half_cols]
            child_cols = jnp.transpose(portion, (1, 0, 2, 3, 4)).reshape(CBB * BLOCK_ORDER, FRONT_PIVOTS)
            product = jnp.dot(child_cols.astype(jnp.float32), child_cols.T.astype(jnp.float32), preferred_element_type=jnp.float32)
            contribution = (update_block.astype(jnp.float32) - product).astype(jnp.bfloat16)
            targets = child_map[2 * row_half + col_half]
            moved = jnp.transpose(contribution.reshape(CBB, BLOCK_ORDER, CBB, BLOCK_ORDER), (0, 2, 1, 3)).astype(jnp.float32)
            blocks = blocks.at[targets[:, None], :, targets[None, :], :].add(moved)
    assembled = blocks.reshape(PARENT, PARENT)
    panel_cols = assembled[:, :FRONT_PIVOTS].astype(jnp.bfloat16)
    pivot_square = panel_cols[:FRONT_PIVOTS].astype(jnp.float32)
    lower_factor = jnp.linalg.cholesky(0.5 * (pivot_square + pivot_square.T))
    inverse = jax.scipy.linalg.solve_triangular(lower_factor, jnp.eye(FRONT_PIVOTS, dtype=jnp.float32), lower=True)
    inverse_factor = inverse.T.astype(jnp.bfloat16)
    kept_blocks = jnp.concatenate([jnp.ones((PPB,), jnp.float32), coupled.astype(jnp.float32)])
    kept_rows = jnp.repeat(kept_blocks, BLOCK_ORDER)[FRONT_PIVOTS:]
    below = jnp.dot(panel_cols[FRONT_PIVOTS:].astype(jnp.float32), inverse_factor.astype(jnp.float32), preferred_element_type=jnp.float32) * kept_rows[:, None]
    below_half = below.astype(jnp.bfloat16)
    schur_part = assembled[FRONT_PIVOTS:, FRONT_PIVOTS:] - jnp.dot(below_half.astype(jnp.float32), below_half.T.astype(jnp.float32), preferred_element_type=jnp.float32)
    upper_rows = jnp.concatenate([jnp.tril(lower_factor), jnp.zeros((FRONT_PIVOTS, PARENT - FRONT_PIVOTS), jnp.float32)], axis=1)
    bottom_rows = jnp.concatenate([below, schur_part], axis=1)
    factored = jnp.concatenate([upper_rows, bottom_rows], axis=0)
    return jnp.transpose(factored.reshape(PLR, N_ROW, BLOCK_ORDER, PLC, N_COL, BLOCK_ORDER), (1, 0, 2, 4, 3, 5))
```

```python
import functools

import jax
import jax.numpy as jnp
from jax import lax
from jax.experimental import pallas as pl
from jax.experimental.pallas import tpu as pltpu
from jax.sharding import PartitionSpec as P

B = 128
NB = 8
N = NB * B
F32 = jnp.float32
BF = jnp.bfloat16
MESH = pl.DeviceIdType.MESH
ANY = pl.BlockSpec(memory_space=pl.ANY)
VM = pl.BlockSpec(memory_space=pltpu.VMEM)
SM = pl.BlockSpec(memory_space=pltpu.SMEM)
LIMIT = 56 * 1024 * 1024


def params(**kw):
    return pltpu.CompilerParams(vmem_limit_bytes=LIMIT, **kw)


N_TAB = 128
AT_ROW, AT_COL, AT_RSRC, AT_RCH, AT_CSRC, AT_CCH = 0, 16, 32, 64, 96, 112


def tables_kernel(map_ref, tab_ref, count):
    my_row, my_col = lax.axis_index("row"), lax.axis_index("col")
    row_rank, col_rank = my_row % 4, my_col % 8
    child = 2 * (my_row // 4) + my_col // 8

    def clear(i, _):
        count[i] = 0
        return 0

    lax.fori_loop(0, 24, clear, 0)

    def out_row(l, _):
        owner = map_ref[child, l * 4 + row_rank] % 8
        tab_ref[AT_ROW + owner * 2 + count[owner]] = l
        count[owner] = count[owner] + 1
        return 0

    lax.fori_loop(0, 16, out_row, 0)

    def out_col(m, _):
        tab_ref[AT_COL + m] = map_ref[child, m * 8 + col_rank] % 16
        return 0

    lax.fori_loop(0, 8, out_col, 0)

    def arrive(q, _):
        h, g = q // 2, q % 2

        def one(b, _):
            target = map_ref[q, b]

            @pl.when(target % 8 == my_row)
            def _():
                slot = 8 + q * 4 + b % 4
                at = h * 16 + target // 8
                tab_ref[AT_RSRC + at] = (h * 4 + b % 4) * 32 + count[slot]
                tab_ref[AT_RCH + at] = g
                count[slot] = count[slot] + 1

            @pl.when(target % 16 == my_col)
            def _():
                at = h * 8 + target // 16
                tab_ref[AT_CSRC + at] = (g * 8 + b % 8) * 2
                tab_ref[AT_CCH + at] = g

            return 0

        lax.fori_loop(0, 64, one, 0)
        return 0

    lax.fori_loop(0, 4, arrive, 0)


def tables(child_map):
    return pl.pallas_call(
        tables_kernel,
        out_shape=jax.ShapeDtypeStruct((N_TAB,), jnp.int32),
        in_specs=[SM],
        out_specs=SM,
        scratch_shapes=[pltpu.SMEM((24,), jnp.int32)],
    )(child_map)


def place(row, col):
    return row // 4, row % 4, col // 4, col // 2 % 2, col % 2


def panel_gather_kernel(p_ref, row_ref, col_ref, local, send, rrow, rcol):
    my_row, my_col = lax.axis_index("row"), lax.axis_index("col")
    half_row, y = my_row // 4 * 4, my_row % 4
    half_col, cc = my_col // 8 * 8, my_col % 8
    core, pair = cc % 2, cc // 2
    sibling = half_col + pair * 2 + 1 - core
    barrier = pltpu.get_barrier_semaphore()

    def greet(row, col):
        pl.semaphore_signal(barrier, inc=1, device_id=(row, col), device_id_type=MESH)

    others = [half_col + (pair + d) % 4 * 2 + core for d in (1, 2, 3)]
    for col in others:
        greet(my_row, col)
    greet(my_row, sibling)
    source_row = half_row + cc % 4
    own = y == cc % 4
    for j in range(8):

        @pl.when(jnp.logical_not(own & (cc == j)))
        def _():
            greet(source_row, half_col + j)

    pl.semaphore_wait(barrier, jnp.where(own, 11, 12))

    def remote(src, dst, s, r, row, col):
        return pltpu.make_async_remote_copy(
            src_ref=src, dst_ref=dst, send_sem=s, recv_sem=r, device_id=(row, col), device_id_type=MESH
        )

    mine = pltpu.make_async_copy(p_ref, row_ref.at[cc], local.at[0])
    mine.start()
    copies = []
    for i, col in enumerate(others):
        copies.append(remote(p_ref, row_ref.at[cc], send.at[i], rrow.at[cc], my_row, col))
        copies[-1].start()
    for d in range(4):
        for parity in range(2):
            row, col = half_row + (y + d) % 4, half_col + parity * 4 + y
            i = 4 + d * 2 + parity
            c = remote(p_ref.at[:, parity], col_ref.at[cc], send.at[i], rcol.at[cc], row, col)
            if d:
                c.start()
            else:
                self_copy = pltpu.make_async_copy(p_ref.at[:, parity], col_ref.at[cc], local.at[1])
                is_self = cc == parity * 4 + y

                @pl.when(is_self)
                def _():
                    self_copy.start()

                @pl.when(jnp.logical_not(is_self))
                def _():
                    c.start()

    sib = remote(p_ref, row_ref.at[cc], send.at[3], rrow.at[cc], my_row, sibling)
    sib.start()
    forwards = []
    for i in range(3):
        k = (pair + 3 - i) % 4 * 2 + core
        remote(p_ref, row_ref.at[k], send.at[0], rrow.at[k], my_row, sibling).wait_recv()
        f = remote(row_ref.at[k], row_ref.at[k], send.at[12 + i], rrow.at[k], my_row, sibling)
        f.start()
        forwards.append(f)
    for c in copies + forwards + [sib]:
        c.wait_send()
    for d in range(4):
        for parity in range(2):
            c = remote(p_ref.at[:, parity], col_ref.at[cc], send.at[4 + d * 2 + parity], rcol.at[cc], my_row, my_col)
            if d:
                c.wait_send()
            else:
                is_self = cc == parity * 4 + y

                @pl.when(is_self)
                def _():
                    pltpu.make_async_copy(p_ref.at[:, parity], col_ref.at[cc], local.at[1]).wait()

                @pl.when(jnp.logical_not(is_self))
                def _():
                    c.wait_send()

    mine.wait()
    for i in range(4):
        k = i * 2 + 1 - core
        remote(p_ref, row_ref.at[k], send.at[0], rrow.at[k], my_row, sibling).wait_recv()
    for j in range(8):

        @pl.when(jnp.logical_not(own & (cc == j)))
        def _():
            remote(p_ref.at[:, 0], col_ref.at[j], send.at[0], rcol.at[j], my_row, sibling).wait_recv()


def panel_gather(piece):
    return pl.pallas_call(
        panel_gather_kernel,
        out_shape=(
            jax.ShapeDtypeStruct((8, 8, 2, B, B), BF),
            jax.ShapeDtypeStruct((8, 8, B, B), BF),
        ),
        in_specs=[ANY],
        out_specs=(ANY, ANY),
        scratch_shapes=[
            pltpu.SemaphoreType.DMA((2,)),
            pltpu.SemaphoreType.DMA((15,)),
            pltpu.SemaphoreType.DMA((8,)),
            pltpu.SemaphoreType.DMA((8,)),
        ],
        compiler_params=params(collective_id=1, has_side_effects=True),
    )(piece)


def contribution_kernel(tab, u0, u1, row_ref, col_ref, out_ref, wide):
    owner = pl.program_id(0)
    left = []
    for s, u in enumerate((u0, u1)):
        wide[s] = u[0].astype(F32)
        l = tab[AT_ROW + owner * 2 + s]
        left.append(jnp.concatenate([row_ref[k, l] for k in range(8)], axis=1))
    left = jnp.concatenate(left, axis=0)
    for m in range(0, 8, 2):
        right = jnp.concatenate(
            [jnp.concatenate([col_ref[k, m + t] for k in range(8)], axis=1) for t in range(2)], axis=0
        )
        product = lax.dot_general(left, right, (((1,), (1,)), ((), ())), preferred_element_type=F32)
        for t in range(2):
            c = tab[AT_COL + m + t]
            for s in range(2):
                value = wide[s, :, m + t, :] - product[s * B : (s + 1) * B, t * B : (t + 1) * B]
                out_ref[c, s * B : (s + 1) * B, :] = value.astype(BF)


def contributions(tab, update, row_op, col_op):
    full = lambda shape: pl.BlockSpec(shape, lambda i, t: (0,) * len(shape))
    u_spec = lambda s: pl.BlockSpec((1, B, 8, B), lambda i, t: (t[AT_ROW + 2 * i + s], 0, 0, 0))
    return pl.pallas_call(
        contribution_kernel,
        out_shape=jax.ShapeDtypeStruct((128, 2 * B, B), BF),
        grid_spec=pltpu.PrefetchScalarGridSpec(
            num_scalar_prefetch=1,
            grid=(8,),
            in_specs=[u_spec(0), u_spec(1), full((8, 16, B, B)), full((8, 8, B, B))],
            out_specs=pl.BlockSpec((16, 2 * B, B), lambda i, t: (i, 0, 0)),
            scratch_shapes=[pltpu.VMEM((2, B, 8, B), F32)],
        ),
        compiler_params=params(),
    )(tab, update, update, row_op, col_op)


def pivot_kernel(tab, c0, c1, front, out_ref):
    l = pl.program_id(0)
    value = front[0].astype(F32)
    for h, c in enumerate((c0, c1)):
        valid = tab[AT_RCH + h * 16 + l] == tab[AT_CCH + h * 8]
        value = value + jnp.where(valid, c[0].astype(F32), 0.0)
    out_ref[0] = value.astype(BF)


def pivot_columns(tab, arrived, front):
    def spec(h):
        return pl.BlockSpec((1, B, B), lambda l, t: (t[AT_RSRC + h * 16 + l] + t[AT_CSRC + h * 8], 0, 0))

    one = pl.BlockSpec((1, B, B), lambda l, t: (l, 0, 0))
    return pl.pallas_call(
        pivot_kernel,
        out_shape=jax.ShapeDtypeStruct((16, B, B), BF),
        grid_spec=pltpu.PrefetchScalarGridSpec(
            num_scalar_prefetch=1, grid=(16,), in_specs=[spec(0), spec(1), one], out_specs=one
        ),
        compiler_params=params(),
    )(tab, arrived, arrived, front)


def remote(src, dst, s, r, row, col):
    return pltpu.make_async_remote_copy(
        src_ref=src, dst_ref=dst, send_sem=s, recv_sem=r, device_id=(row, col), device_id_type=MESH
    )


class Gather:
    def __init__(self, p_ref, sq_ref, por_ref, cols_ref, local, s_row, s_sq, s_por, s_cols, s_fsq, s_fpor, r_row, r_sq, r_por, r_cols):
        self.__dict__.update(locals())
        self.row, self.col = lax.axis_index("row"), lax.axis_index("col")
        self.core, self.chip = self.col % 2, self.col // 2
        self.sibling = self.chip * 2 + 1 - self.core
        self.owner = self.col < 8
        self.diagonal = self.row == self.col

    def chips(self):
        return [(self.chip + d) % 8 * 2 + self.core for d in (4, 1, 7, 2, 6, 3, 5)]

    def enter(self):
        barrier = pltpu.get_barrier_semaphore()

        def greet(row, col):
            pl.semaphore_signal(barrier, inc=1, device_id=(row, col), device_id_type=MESH)

        greet(self.row, self.sibling)

        @pl.when(self.owner)
        def _():
            for d in range(1, 8):
                greet((self.row + d) % 8, self.col)

        for i in range(4):
            j = 2 * i + self.core

            @pl.when(j != self.col)
            def _():
                greet(self.row, j)

        for j in range(8):
            source = self.col % 8

            @pl.when(jnp.logical_not((source == self.row) & (self.col == j)))
            def _():
                greet(source, j)

        pl.semaphore_wait(barrier, jnp.where(self.owner, jnp.where(self.diagonal, 30, 31), 1))

    def row_sends(self):
        out = []
        for d in range(1, 8):
            dst = self.sq_ref.at[self.col, self.row]
            out.append(remote(self.p_ref.at[0, 0], dst, self.s_row.at[d - 1], self.r_row.at[self.row], (self.row + d) % 8, self.col))
        return out

    def sq_sends(self):
        return [
            remote(self.sq_ref.at[self.col], self.sq_ref.at[self.col], self.s_sq.at[i], self.r_sq.at[self.col], self.row, c)
            for i, c in enumerate(self.chips())
        ]

    def por_sends(self):
        return [
            remote(self.p_ref, self.por_ref.at[self.col], self.s_por.at[i], self.r_por.at[self.col], self.row, c)
            for i, c in enumerate(self.chips())
        ]

    def cols_sends(self):
        out = []
        for d in (4, 1, 3, 5, 7, 2, 6, 0):
            for half in range(2):
                c = remote(
                    self.p_ref.at[:, half], self.cols_ref.at[self.col], self.s_cols.at[d * 2 + half], self.r_cols.at[self.col],
                    (self.row + d) % 8, self.row + 8 * half,
                )
                out.append((c, d == 0 and half == 0))
        return out

    def local_copies(self):
        a = pltpu.make_async_copy(self.p_ref.at[0, 0], self.sq_ref.at[self.col, self.row], self.local.at[0])
        b = pltpu.make_async_copy(self.p_ref, self.por_ref.at[self.col], self.local.at[1])
        c = pltpu.make_async_copy(self.p_ref.at[:, 0], self.cols_ref.at[self.col], self.local.at[2])
        return a, b, c

    def start(self):
        @pl.when(self.owner)
        def _():
            a, b, c = self.local_copies()
            a.start()
            for s in self.row_sends():
                s.start()
            b.start()

            @pl.when(self.diagonal)
            def _():
                c.start()

            a.wait()
            for d in range(1, 8):
                i = (self.row + d) % 8
                remote(self.p_ref.at[0, 0], self.sq_ref.at[self.col, i], self.s_row.at[0], self.r_row.at[i], self.row, self.sibling).wait_recv()
            for s in self.sq_sends():
                s.start()
            for s in self.por_sends():
                s.start()
            for s, maybe_self in self.cols_sends():
                if maybe_self:

                    @pl.when(jnp.logical_not(self.diagonal))
                    def _():
                        s.start()

                else:
                    s.start()
            b.wait()

            @pl.when(self.diagonal)
            def _():
                c.wait()

    def share(self, ref, send, recv):
        for i in range(4):
            j = 2 * i + self.core

            @pl.when(j != self.col)
            def _():
                remote(ref.at[j], ref.at[j], send.at[i], recv.at[j], self.row, self.sibling).wait_recv()

            remote(ref.at[j], ref.at[j], send.at[i], recv.at[j], self.row, self.sibling).start()

    def shared(self, ref, send, recv):
        for i in range(4):
            j = 2 * i + 1 - self.core
            remote(ref.at[j], ref.at[j], send.at[i], recv.at[j], self.row, self.sibling).wait_recv()

    def share_square(self):
        self.share(self.sq_ref, self.s_fsq, self.r_sq)

    def wait_square(self):
        self.shared(self.sq_ref, self.s_fsq, self.r_sq)

    def share_portion(self):
        self.share(self.por_ref, self.s_fpor, self.r_por)

    def wait_rest(self):
        self.shared(self.por_ref, self.s_fpor, self.r_por)
        for j in range(8):

            @pl.when(jnp.logical_not(self.diagonal & (self.col == j)))
            def _():
                remote(self.cols_ref.at[j], self.cols_ref.at[j], self.s_cols.at[0], self.r_cols.at[j], self.row, self.sibling).wait_recv()

    def finish(self):
        for ref, send, recv in ((self.sq_ref, self.s_fsq, self.r_sq), (self.por_ref, self.s_fpor, self.r_por)):
            for i in range(4):
                j = 2 * i + self.core
                remote(ref.at[j], ref.at[j], send.at[i], recv.at[j], self.row, self.sibling).wait_send()

        @pl.when(self.owner)
        def _():
            for s in self.row_sends() + self.sq_sends() + self.por_sends():
                s.wait_send()
            for s, maybe_self in self.cols_sends():
                if maybe_self:

                    @pl.when(jnp.logical_not(self.diagonal))
                    def _():
                        s.wait_send()

                else:
                    s.wait_send()


GATHER_SEMS = (3, 7, 7, 7, 16, 4, 4, 8, 8, 8, 8)


def pivot_gather_kernel(p_ref, sq_ref, por_ref, cols_ref, *sems):
    g = Gather(p_ref, sq_ref, por_ref, cols_ref, *sems)
    g.enter()
    g.start()
    g.share_square()
    g.wait_square()
    g.share_portion()
    g.wait_rest()
    g.finish()


def pivot_gather(piece):
    return pl.pallas_call(
        pivot_gather_kernel,
        out_shape=(
            jax.ShapeDtypeStruct((8, 8, B, B), BF),
            jax.ShapeDtypeStruct((8, 8, 2, B, B), BF),
            jax.ShapeDtypeStruct((8, 8, B, B), BF),
        ),
        in_specs=[ANY],
        out_specs=(ANY, ANY, ANY),
        scratch_shapes=[pltpu.SemaphoreType.DMA((n,)) for n in GATHER_SEMS],
        compiler_params=params(collective_id=2, has_side_effects=True),
    )(piece)


def splits(a):
    parts = []
    for i in range(3):
        h = a.astype(BF)
        parts.append(h)
        if i < 2:
            a = a - h.astype(F32)
    return parts


LEFT = (0, 0, 1, 1, 0, 2)
RIGHT = (0, 1, 0, 1, 2, 0)


def dot_f32(a, b, dims):
    sa, sb = splits(a), splits(b)
    left = jnp.concatenate([sa[i] for i in LEFT], axis=dims[0][0])
    right = jnp.concatenate([sb[i] for i in RIGHT], axis=dims[1][0])
    return lax.dot_general(left, right, (dims, ((), ())), preferred_element_type=F32)


def diagonal_factor(square):
    group = 16
    lane = lax.broadcasted_iota(jnp.int32, (8, B), 1)
    sub = lax.broadcasted_iota(jnp.int32, (8, B), 0)
    spread = lambda x, s: jnp.broadcast_to(x[s : s + 1, :], (8, B))
    rest, upper, lower = square, [], []
    for g in range(B // group):
        r0 = group * g
        p = [rest[8 * v : 8 * v + 8, :] for v in range(2)]
        column = [[jnp.broadcast_to(p[v][:, r0 + j : r0 + j + 1], (8, B)) for v in range(2)] for j in range(group)]
        root = [jnp.zeros((8, B), F32) for _ in range(2)]
        for k in range(group):
            at, s = divmod(k, 8)
            r = lax.rsqrt(spread(column[k][at], s))
            root[at] = jnp.where(sub == s, r, root[at])
            if k == group - 1:
                break
            here = lane == r0 + k
            row = jnp.where(here, 1.0, spread(p[at], s))
            for v in range(at, 2):
                if v == at and s == 7:
                    continue
                factor = column[k][v] * (r * r)
                if v == at:
                    factor = jnp.where(sub > s, factor, 0.0)
                    p[v] = jnp.where(here & (sub > s), 0.0, p[v]) - factor * row
                else:
                    p[v] = jnp.where(here, 0.0, p[v]) - factor * row
                for j in range(k + 1, group):
                    column[j][v] = column[j][v] - factor * spread(column[j][at], s)
        panel = jnp.concatenate([p[v] * root[v] for v in range(2)], axis=0)
        roots = jnp.concatenate(root, axis=0)
        ln = lax.broadcasted_iota(jnp.int32, (group, B), 1) - r0
        sb = lax.broadcasted_iota(jnp.int32, (group, B), 0)
        eliminated = jnp.where(ln == sb, roots, jnp.where((ln > sb) & (ln < group), 0.0, panel))
        upper.append(panel)
        lower.append(jnp.where(ln > sb, 0.0, eliminated))
        if g < B // group - 1:
            change = dot_f32(jnp.where(ln >= group, panel, 0.0), eliminated, ((0,), (0,)))
            lt = lax.broadcasted_iota(jnp.int32, (B - r0 - group, B), 1)
            rest = jnp.where((lt >= r0) & (lt < r0 + group), 0.0, rest[group:, :]) - change[r0 + group :, :]
    return jnp.concatenate(upper, axis=0), jnp.concatenate(lower, axis=0)


def factor_start(sq_ref, lower_ref, work):
    for i in range(NB):
        for j in range(NB):
            at = (slice(i * B, (i + 1) * B), slice(j * B, (j + 1) * B))
            if j < i:
                work[at] = jnp.zeros((B, B), F32)
            else:
                work[at] = 0.5 * (sq_ref[j, i].astype(F32) + sq_ref[i, j].astype(F32).T)
    lower_ref[...] = jnp.zeros((B, B), F32)


def factor_step(kb, my_row, my_col, inv_ref, lower_ref, work, left, right):
    lane = lax.broadcasted_iota(jnp.int32, (B, B), 1)
    sub = lax.broadcasted_iota(jnp.int32, (B, B), 0)
    d0 = pl.multiple_of(kb * B, B)
    upper, lower = diagonal_factor(work[pl.ds(d0, B), pl.ds(d0, B)])
    work[pl.ds(d0, B), pl.ds(d0, B)] = jnp.where(lane == sub, 1.0, 0.0)
    panel = dot_f32(lower, work[pl.ds(d0, B), :], ((1,), (0,)))
    col = lax.broadcasted_iota(jnp.int32, (B, N), 1)
    inv_ref[pl.ds(d0, B), :] = jnp.where(col < d0 + B, panel, 0.0).astype(BF)

    @pl.when(kb == my_col)
    def _():
        @pl.when(kb == my_row)
        def _():
            lower_ref[...] = jnp.where(lane >= sub, upper, 0.0).T

        @pl.when(kb < my_row)
        def _():
            work[pl.ds(d0, B), :] = panel
            lower_ref[...] = work[pl.ds(d0, B), pl.ds(pl.multiple_of(my_row * B, B), B)].T

    parts = splits(panel)
    for t in range(6):
        left[t * B : (t + 1) * B, :] = parts[LEFT[t]]
        right[t * B : (t + 1) * B, :] = parts[RIGHT[t]]

    def trailing(i, _):
        i0 = pl.multiple_of(i * B, B)
        work[pl.ds(i0, B), pl.ds(d0, B)] = jnp.zeros((B, B), F32)
        work[pl.ds(i0, B), :] = work[pl.ds(i0, B), :] - lax.dot_general(
            left[:, pl.ds(i0, B)], right[...], (((0,), (0,)), ((), ())), preferred_element_type=F32
        )
        return 0

    lax.fori_loop(kb + 1, NB, trailing, 0)


def below_rows(por_ref, cols_ref, inv_ref, lower_ref, keep_ref, my_col, below_ref, panel_ref, first_ref):
    safe = jnp.minimum(my_col, NB - 1)
    dims = (((1,), (1,)), ((), ()))

    def rows(i, _):
        for t in range(2):
            l = 2 * i + t
            a = jnp.concatenate([por_ref[k, l] for k in range(8)], axis=1)
            out = lax.dot_general(a, inv_ref[...], dims, preferred_element_type=F32) * keep_ref[l]
            below_ref[pl.ds(pl.multiple_of(l * B, B), B), :] = out.astype(BF)
            mine = inv_ref[pl.ds(pl.multiple_of(safe * B, B), B), :]
            first_ref[l] = lax.dot_general(a, mine, dims, preferred_element_type=F32) * keep_ref[l]
        return 0

    lax.fori_loop(0, 8, rows, 0)
    first_ref[0] = lower_ref[...]

    def cols(m, _):
        a = jnp.concatenate([cols_ref[k, m] for k in range(8)], axis=1)
        out = lax.dot_general(a, inv_ref[...], dims, preferred_element_type=F32) * keep_ref[16 + m]
        panel_ref[pl.ds(pl.multiple_of(m * B, B), B), :] = out.astype(BF)
        return 0

    lax.fori_loop(0, 8, cols, 0)


def factor_kernel(sq_ref, por_ref, cols_ref, keep_ref, below_ref, panel_ref, first_ref, inv_ref, lower_ref, work, left, right):
    my_row, my_col = lax.axis_index("row"), lax.axis_index("col")
    factor_start(sq_ref, lower_ref, work)

    def step(kb, _):
        factor_step(kb, my_row, my_col, inv_ref, lower_ref, work, left, right)
        return 0

    lax.fori_loop(0, NB, step, 0)
    below_rows(por_ref, cols_ref, inv_ref, lower_ref, keep_ref, my_col, below_ref, panel_ref, first_ref)


FACTOR_OUT = (
    jax.ShapeDtypeStruct((16 * B, N), BF),
    jax.ShapeDtypeStruct((8 * B, N), BF),
    jax.ShapeDtypeStruct((16, B, B), F32),
)
FACTOR_SCRATCH = (
    ((N, N), BF),
    ((B, B), F32),
    ((N, N), F32),
    ((6 * B, N), BF),
    ((6 * B, N), BF),
)


def factor(square, portion, cols, keep):
    return pl.pallas_call(
        factor_kernel,
        out_shape=FACTOR_OUT,
        in_specs=[VM, VM, VM, SM],
        out_specs=(VM, VM, VM),
        scratch_shapes=[pltpu.VMEM(s, d) for s, d in FACTOR_SCRATCH],
        compiler_params=params(),
    )(square, portion, cols, keep)


def schur_kernel(tab, front, arrived, below, panel, first, out_ref, wide):
    i = pl.program_id(0)
    my_col = lax.axis_index("col")
    product = lax.dot_general(below[...], panel[...], (((1,), (1,)), ((), ())), preferred_element_type=F32)
    for s in range(2):
        l = 2 * i + s
        wide[...] = front[s].astype(F32)
        for m in range(8):
            value = wide[:, m, :]
            for h in range(2):
                valid = tab[AT_RCH + h * 16 + l] == tab[AT_CCH + h * 8 + m]
                at = jnp.where(valid, tab[AT_RSRC + h * 16 + l] + tab[AT_CSRC + h * 8 + m], 0)
                value = value + jnp.where(valid, arrived[at].astype(F32), 0.0)
            value = value - product[s * B : (s + 1) * B, m * B : (m + 1) * B]
            if s == 0:
                value = jnp.where(l == 0, 0.0, value)
            if m == 0:
                value = jnp.where(my_col < NB, first[s], value)
            out_ref[s, :, m, :] = value


def schur(tab, front, arrived, below, panel, first):
    full = lambda shape: pl.BlockSpec(shape, lambda i, t: (0,) * len(shape))
    return pl.pallas_call(
        schur_kernel,
        out_shape=jax.ShapeDtypeStruct((16, B, 8, B), F32),
        grid_spec=pltpu.PrefetchScalarGridSpec(
            num_scalar_prefetch=1,
            grid=(8,),
            in_specs=[
                pl.BlockSpec((2, B, 8, B), lambda i, t: (i, 0, 0, 0)),
                full((256, B, B)),
                pl.BlockSpec((2 * B, N), lambda i, t: (i, 0)),
                full((N, N)),
                pl.BlockSpec((2, B, B), lambda i, t: (i, 0, 0)),
            ],
            out_specs=pl.BlockSpec((2, B, 8, B), lambda i, t: (i, 0, 0, 0)),
            scratch_shapes=[pltpu.VMEM((B, 8, B), F32)],
        ),
        compiler_params=params(),
    )(tab, front, arrived, below, panel, first)


def per_device(child_update_blocks, child_pivot_panel, child_map, coupled, parent_front):
    my_row, my_col = lax.axis_index("row"), lax.axis_index("col")
    front = parent_front.reshape(16, B, 8, B)
    tab = tables(child_map)
    row_op, col_op = panel_gather(child_pivot_panel.reshape(8, 2, B, B))
    outgoing = contributions(tab, child_update_blocks.reshape(16, B, 8, B), row_op.reshape(8, 16, B, B), col_op)
    incoming = lax.all_to_all(outgoing, ("row", "col"), split_axis=0, concat_axis=0, tiled=True)
    arrived = incoming.reshape(256, B, B)
    kept = jnp.concatenate([jnp.ones((NB,), F32), coupled.astype(F32)])
    keep = jnp.concatenate(
        [
            lax.dynamic_index_in_dim(kept.reshape(16, 8), my_row, 1, keepdims=False),
            lax.dynamic_index_in_dim(kept.reshape(8, 16), my_col, 1, keepdims=False),
        ]
    )
    pivots = pivot_columns(tab, arrived, front[:, :, 0, :])
    square, portion, cols = pivot_gather(pivots.reshape(8, 2, B, B))
    below, panel, first = factor(square, portion.reshape(8, 16, B, B), cols, keep)
    out = schur(tab, front, arrived, below, panel, first)
    return out.reshape(1, 16, B, 1, 8, B)


def solution(mesh):
    in_specs = (
        P("row", None, None, "col", None, None),
        P("row", None, None, "col", None),
        P(),
        P(),
        P("row", None, None, "col", None, None),
    )
    out_specs = P("row", None, None, "col", None, None)
    return jax.shard_map(per_device, mesh=mesh, in_specs=in_specs, out_specs=out_specs, check_vma=False)
```

```python
import functools

import jax
import jax.numpy as jnp
from jax import lax
from jax.experimental import pallas as pl
from jax.experimental.pallas import tpu as pltpu
from jax.sharding import PartitionSpec as P

B = 128
NB = 8
N = NB * B
F32 = jnp.float32
BF = jnp.bfloat16
MESH = pl.DeviceIdType.MESH
ANY = pl.BlockSpec(memory_space=pl.ANY)
VM = pl.BlockSpec(memory_space=pltpu.VMEM)
SM = pl.BlockSpec(memory_space=pltpu.SMEM)
LIMIT = 56 * 1024 * 1024


def params(**kw):
    return pltpu.CompilerParams(vmem_limit_bytes=LIMIT, **kw)


OUT_ROW, OUT_COL = 0, 16
AT_RSRC, AT_RCH, AT_CSRC, AT_CCH = 0, 32, 64, 80


def clear(count):
    def one(i, _):
        count[i] = 0
        return 0

    lax.fori_loop(0, 16, one, 0)


def outgoing_kernel(map_ref, tab_ref, count):
    my_row, my_col = lax.axis_index("row"), lax.axis_index("col")
    row_rank, col_rank = my_row % 4, my_col % 8
    child = 2 * (my_row // 4) + my_col // 8
    clear(count)
    for l in range(16):
        owner = map_ref[child, l * 4 + row_rank] % 8
        tab_ref[OUT_ROW + owner * 2 + count[owner]] = l
        count[owner] = count[owner] + 1
    for m in range(8):
        tab_ref[OUT_COL + m] = map_ref[child, m * 8 + col_rank] % 16


def incoming_kernel(map_ref, tab_ref, count):
    my_row, my_col = lax.axis_index("row"), lax.axis_index("col")
    clear(count)

    def arrive(q, _):
        h, g = q // 2, q % 2

        def one(b, _):
            target = map_ref[q, b]

            @pl.when(target % 8 == my_row)
            def _():
                slot = q * 4 + b % 4
                at = h * 16 + target // 8
                tab_ref[AT_RSRC + at] = (h * 4 + b % 4) * 32 + count[slot]
                tab_ref[AT_RCH + at] = g
                count[slot] = count[slot] + 1

            @pl.when(target % 16 == my_col)
            def _():
                at = h * 8 + target // 16
                tab_ref[AT_CSRC + at] = (g * 8 + b % 8) * 2
                tab_ref[AT_CCH + at] = g

            return 0

        lax.fori_loop(0, 64, one, 0)
        return 0

    lax.fori_loop(0, 4, arrive, 0)


def table(kernel, size, child_map):
    return pl.pallas_call(
        kernel,
        out_shape=jax.ShapeDtypeStruct((size,), jnp.int32),
        in_specs=[SM],
        out_specs=SM,
        scratch_shapes=[pltpu.SMEM((16,), jnp.int32)],
        cost_estimate=pl.CostEstimate(flops=20000, bytes_accessed=2048, transcendentals=0),
    )(child_map)


def remote(src, dst, s, r, row, col):
    return pltpu.make_async_remote_copy(
        src_ref=src, dst_ref=dst, send_sem=s, recv_sem=r, device_id=(row, col), device_id_type=MESH
    )


def panel_gather_kernel(p_ref, row_ref, col_ref, local, s_chip, s_sib, s_col, r_row, r_col):
    my_row, my_col = lax.axis_index("row"), lax.axis_index("col")
    base, y = my_row // 4 * 4, my_row % 4
    half, cc = my_col // 8 * 8, my_col % 8
    core, pair, parity = cc % 2, cc // 2, cc // 4
    sibling = half + pair * 2 + 1 - core
    y0 = cc % 4
    step = jnp.where(y0 % 2 == 0, 3, 1)
    outer = (y0 + step) % 4
    inner = y0 + 1 - 2 * (y0 % 2)
    last = outer + 1 - 2 * (outer % 2)
    is_source, is_relay = y == y0, y == outer
    barrier = pltpu.get_barrier_semaphore()

    def greet(row, col):
        pl.semaphore_signal(barrier, inc=1, device_id=(row, col), device_id_type=MESH)

    others = [half + (pair + d) % 4 * 2 + core for d in (2, 1, 3)]
    for col in others:
        greet(my_row, col)
    greet(my_row, sibling)

    @pl.when(jnp.logical_not(is_source))
    def _():
        greet(base + jnp.where(y == last, outer, y0), my_col)

    pl.semaphore_wait(barrier, 4 + jnp.where(is_source, 2, jnp.where(is_relay, 1, 0)))

    order = [cc, pair * 2 + 1 - core] + [(pair + d) % 4 * 2 + core for d in (2, 1, 3)]
    order += [(pair + d) % 4 * 2 + 1 - core for d in (2, 1, 3)]

    def own():
        return pltpu.make_async_copy(p_ref, row_ref.at[cc], local.at[8])

    def chip_send(i):
        return remote(p_ref, row_ref.at[cc], s_chip.at[i], r_row.at[cc], my_row, others[i])

    def sib_send(e):
        src = p_ref if e == 0 else row_ref.at[order[e]]
        return remote(src, row_ref.at[order[e]], s_sib.at[max(e - 1, 0)], r_row.at[order[e]], my_row, sibling)

    def part(e):
        return p_ref.at[:, parity] if e == 0 else row_ref.at[order[e], :, parity]

    def keep(e):
        return pltpu.make_async_copy(part(e), col_ref.at[order[e]], local.at[e])

    def col_send(e, t):
        return remote(part(e), col_ref.at[order[e]], s_col.at[e, t], r_col.at[order[e]], base + (outer, inner)[t], my_col)

    def pass_on(e):
        j = order[e]
        return remote(col_ref.at[j], col_ref.at[j], s_col.at[e, 0], r_col.at[j], base + last, my_col)

    own().start()
    for i in range(3):
        chip_send(i).start()
    sib_send(0).start()
    for e in range(9):
        if e < 8:
            if e:
                remote(p_ref, row_ref.at[order[e]], s_sib.at[0], r_row.at[order[e]], my_row, sibling).wait_recv()
            if 2 <= e < 5:
                sib_send(e).start()

            @pl.when(is_source)
            def _():
                col_send(e, 0).start()
                col_send(e, 1).start()
                keep(e).start()

        if e:

            @pl.when(is_relay)
            def _():
                pass_on(e - 1).wait_recv()
                pass_on(e - 1).start()

    @pl.when(jnp.logical_not(is_source | is_relay))
    def _():
        for e in range(8):
            pass_on(e).wait_recv()

    own().wait()
    for i in range(3):
        chip_send(i).wait_send()
    for e in (0, 2, 3, 4):
        sib_send(e).wait_send()

    @pl.when(is_source)
    def _():
        for e in range(8):
            keep(e).wait()
            col_send(e, 0).wait_send()
            col_send(e, 1).wait_send()

    @pl.when(is_relay)
    def _():
        for e in range(8):
            pass_on(e).wait_send()


def panel_gather(piece):
    return pl.pallas_call(
        panel_gather_kernel,
        out_shape=(
            jax.ShapeDtypeStruct((8, 8, 2, B, B), BF),
            jax.ShapeDtypeStruct((8, 8, B, B), BF),
        ),
        in_specs=[ANY],
        out_specs=(ANY, ANY),
        scratch_shapes=[
            pltpu.SemaphoreType.DMA((9,)),
            pltpu.SemaphoreType.DMA((3,)),
            pltpu.SemaphoreType.DMA((4,)),
            pltpu.SemaphoreType.DMA((8, 2)),
            pltpu.SemaphoreType.DMA((8,)),
            pltpu.SemaphoreType.DMA((8,)),
        ],
        compiler_params=params(collective_id=1, has_side_effects=True),
    )(piece)


def contribution_kernel(tab, u0, u1, row_ref, col_ref, out_ref, right):
    owner = pl.program_id(0)

    @pl.when(owner == 0)
    def _():
        for k in range(8):
            for m in range(8):
                right[m * B : (m + 1) * B, k * B : (k + 1) * B] = col_ref[k, m]

    left = []
    for s in range(2):
        l = tab[OUT_ROW + owner * 2 + s]
        left.append(jnp.concatenate([row_ref[k, l] for k in range(8)], axis=1))
    left = jnp.concatenate(left, axis=0)
    product = lax.dot_general(left, right[...], (((1,), (1,)), ((), ())), preferred_element_type=F32)
    for s, u in enumerate((u0, u1)):
        update = jnp.swapaxes(u[0], 0, 1)
        for m in range(8):
            value = update[m].astype(F32) - product[s * B : (s + 1) * B, m * B : (m + 1) * B]
            out_ref[tab[OUT_COL + m], s * B : (s + 1) * B, :] = value.astype(BF)


def contributions(tab, update, row_op, col_op):
    full = lambda shape: pl.BlockSpec(shape, lambda i, t: (0,) * len(shape))
    u_spec = lambda s: pl.BlockSpec((1, B, 8, B), lambda i, t: (t[OUT_ROW + 2 * i + s], 0, 0, 0))
    return pl.pallas_call(
        contribution_kernel,
        out_shape=jax.ShapeDtypeStruct((128, 2 * B, B), BF),
        grid_spec=pltpu.PrefetchScalarGridSpec(
            num_scalar_prefetch=1,
            grid=(8,),
            in_specs=[u_spec(0), u_spec(1), full((8, 16, B, B)), full((8, 8, B, B))],
            out_specs=pl.BlockSpec((16, 2 * B, B), lambda i, t: (i, 0, 0)),
            scratch_shapes=[pltpu.VMEM((N, N), BF)],
        ),
        compiler_params=params(),
    )(tab, update, update, row_op, col_op)


def pivot_kernel(tab, arrived, front, out_ref, block, sem):
    def fits(l, h):
        return tab[AT_RCH + h * 16 + l] == tab[AT_CCH + h * 8]

    def fetch(l, h):
        at = jnp.where(fits(l, h), tab[AT_RSRC + h * 16 + l] + tab[AT_CSRC + h * 8], 0)
        return pltpu.make_async_copy(arrived.at[at], block.at[h, l], sem.at[h, l])

    for l in range(16):
        for h in range(2):
            fetch(l, h).start()
    for l in range(16):
        value = front[l].astype(F32)
        for h in range(2):
            valid = fits(l, h)
            fetch(l, h).wait()
            value = value + jnp.where(valid, block[h, l].astype(F32), 0.0)
        out_ref[l] = value.astype(BF)


def pivot_columns(tab, arrived, front):
    return pl.pallas_call(
        pivot_kernel,
        out_shape=jax.ShapeDtypeStruct((16, B, B), BF),
        in_specs=[SM, ANY, VM],
        out_specs=VM,
        scratch_shapes=[pltpu.VMEM((2, 16, B, B), BF), pltpu.SemaphoreType.DMA((2, 16))],
        compiler_params=params(),
    )(tab, arrived, front)


class Gather:
    SEMS = (2, 7, 7, 4, 3, 2, 4, 8, 8, 8, 8, 8)

    def __init__(self, piece, sq, portion, cols, sems):
        self.piece, self.sq, self.portion, self.cols = piece, sq, portion, cols
        (self.local, self.s_row, self.s_sq, self.s_sqf, self.s_z, self.s_x, self.s_sib, self.s_cols) = sems[:8]
        self.r_row, self.r_sq, self.r_por, self.r_cols = sems[8:]
        self.row, self.col = lax.axis_index("row"), lax.axis_index("col")
        col = self.col
        self.z, self.xh, self.core = col // 4, col // 2 % 2, col % 2
        self.zh = self.z // 2
        self.chip = col // 2
        self.sibling = self.chip * 2 + 1 - self.core
        self.across = self.z * 4 + (1 - self.xh) * 2 + self.core
        self.owner = col < 8
        self.same = col % 8 == self.row

    def chips(self):
        return [(self.chip + d) % 8 * 2 + self.core for d in (4, 1, 7, 2, 6, 3, 5)]

    def enter(self):
        barrier = pltpu.get_barrier_semaphore()

        def greet(row, col):
            pl.semaphore_signal(barrier, inc=1, device_id=(row, col), device_id_type=MESH)

        greet(self.row, self.sibling)
        greet(self.row, self.across)

        @pl.when(self.owner)
        def _():
            for d in range(1, 8):
                greet((self.row + d) % 8, self.col)

        for i in range(4):
            j = 2 * i + self.core

            @pl.when(j != self.col)
            def _():
                greet(self.row, j)

        for d in range(8):
            j = (self.col + d) % 8
            if d:
                greet(self.col % 8, self.zh * 8 + j)
            else:

                @pl.when(jnp.logical_not(self.same))
                def _():
                    greet(self.col % 8, self.zh * 8 + j)

        pl.semaphore_wait(barrier, 10 + jnp.where(self.owner, 14, 0) - jnp.where(self.same, 1, 0))

    def row_sends(self):
        dst = self.sq.at[self.col, self.row]
        return [
            remote(self.piece.at[0, 0], dst, self.s_row.at[d - 1], self.r_row.at[self.row], (self.row + d) % 8, self.col)
            for d in range(1, 8)
        ]

    def sq_sends(self):
        c = self.sq.at[self.col]
        return [
            remote(c, c, self.s_sq.at[i], self.r_sq.at[self.col], self.row, t) for i, t in enumerate(self.chips())
        ]

    def z_sends(self):
        c = self.portion.at[self.col]
        return [
            remote(self.piece, c, self.s_z.at[d - 1], self.r_por.at[self.col], self.row, (self.col + 4 * d) % 16)
            for d in (2, 1, 3)
        ]

    def x_sends(self):
        out = []
        for zp in range(2):
            j = zp * 4 + self.xh * 2 + self.core
            out.append(remote(self.portion.at[j], self.portion.at[j], self.s_x.at[zp], self.r_por.at[j], self.row, self.across))
        return out

    def sib_sends(self):
        out = []
        for i in range(4):
            j = 2 * i + self.core
            out.append(remote(self.portion.at[j], self.portion.at[j], self.s_sib.at[i], self.r_por.at[j], self.row, self.sibling))
        return out

    def cols_send(self, d):
        j = self.col % 8
        src = self.portion.at[j, :, self.zh]
        return remote(
            src, self.cols.at[j], self.s_cols.at[d], self.r_cols.at[j], (self.row + d) % 8, self.row + 8 * self.zh
        )

    def cols_sends(self):
        return [self.cols_send(d) for d in (4, 1, 3, 5, 7, 2, 6)]

    def arrived(self, ref, sem):
        remote(ref, ref, self.s_row.at[0], sem, self.row, self.sibling).wait_recv()

    def square(self):
        @pl.when(self.owner)
        def _():
            first = pltpu.make_async_copy(self.piece.at[0, 0], self.sq.at[self.col, self.row], self.local.at[0])
            whole = pltpu.make_async_copy(self.piece, self.portion.at[self.col], self.local.at[1])
            first.start()
            for s in self.row_sends():
                s.start()
            whole.start()
            first.wait()
            for d in range(1, 8):
                i = (self.row + d) % 8
                self.arrived(self.sq.at[self.col, i], self.r_row.at[i])
            for s in self.sq_sends():
                s.start()
            whole.wait()

        for i in range(4):
            j = 2 * i + self.core

            @pl.when(j != self.col)
            def _():
                self.arrived(self.sq.at[j], self.r_sq.at[j])

            c = self.sq.at[j]
            remote(c, c, self.s_sqf.at[i], self.r_sq.at[j], self.row, self.sibling).start()
        for i in range(4):
            j = 2 * i + 1 - self.core
            self.arrived(self.sq.at[j], self.r_sq.at[j])

    def cols_start(self):
        for s in self.cols_sends():
            s.start()

        @pl.when(jnp.logical_not(self.same))
        def _():
            self.cols_send(0).start()

    def keep_cols(self):
        j = self.col % 8
        return pltpu.make_async_copy(self.portion.at[j, :, self.zh], self.cols.at[j], self.local.at[0])

    def first(self):
        @pl.when(self.owner)
        def _():
            for s in self.z_sends():
                s.start()
            self.cols_start()

    def second(self):
        for zp in range(2):
            j = zp * 4 + self.xh * 2 + self.core

            @pl.when(j != self.col)
            def _():
                self.arrived(self.portion.at[j], self.r_por.at[j])

        for s in self.x_sends():
            s.start()

        @pl.when(jnp.logical_not(self.owner))
        def _():
            self.cols_start()

        @pl.when(self.same)
        def _():
            self.keep_cols().start()

    def third(self):
        for zp in range(2):
            j = zp * 4 + (1 - self.xh) * 2 + self.core
            self.arrived(self.portion.at[j], self.r_por.at[j])
        for s in self.sib_sends():
            s.start()

    def last(self):
        for i in range(4):
            j = 2 * i + 1 - self.core
            self.arrived(self.portion.at[j], self.r_por.at[j])
        for d in range(1, 8):
            j = (self.col + d) % 8
            self.arrived(self.cols.at[j], self.r_cols.at[j])

        @pl.when(self.same)
        def _():
            self.keep_cols().wait()

        @pl.when(jnp.logical_not(self.same))
        def _():
            j = self.col % 8
            self.arrived(self.cols.at[j], self.r_cols.at[j])

    def finish(self):
        for i in range(4):
            c = self.sq.at[2 * i + self.core]
            remote(c, c, self.s_sqf.at[i], self.r_sq.at[0], self.row, self.sibling).wait_send()
        for s in self.x_sends() + self.sib_sends() + self.cols_sends():
            s.wait_send()

        @pl.when(jnp.logical_not(self.same))
        def _():
            self.cols_send(0).wait_send()

        @pl.when(self.owner)
        def _():
            for s in self.row_sends() + self.sq_sends() + self.z_sends():
                s.wait_send()


def splits(a):
    parts = []
    for i in range(3):
        h = a.astype(BF)
        parts.append(h)
        if i < 2:
            a = a - h.astype(F32)
    return parts


LEFT = (0, 0, 1, 1, 0, 2)
RIGHT = (0, 1, 0, 1, 2, 0)


def dot_f32(a, b, dims):
    sa, sb = splits(a), splits(b)
    left = jnp.concatenate([sa[i] for i in LEFT], axis=dims[0][0])
    right = jnp.concatenate([sb[i] for i in RIGHT], axis=dims[1][0])
    return lax.dot_general(left, right, (dims, ((), ())), preferred_element_type=F32)


def diagonal_factor(square):
    group = 16
    lane = lax.broadcasted_iota(jnp.int32, (8, B), 1)
    sub = lax.broadcasted_iota(jnp.int32, (8, B), 0)
    spread = lambda x, s: jnp.broadcast_to(x[s : s + 1, :], (8, B))
    rest, upper, lower = square, [], []
    for g in range(B // group):
        r0 = group * g
        p = [rest[8 * v : 8 * v + 8, :] for v in range(2)]
        column = [[jnp.broadcast_to(p[v][:, r0 + j : r0 + j + 1], (8, B)) for v in range(2)] for j in range(group)]
        root = [jnp.zeros((8, B), F32) for _ in range(2)]
        for k in range(group):
            at, s = divmod(k, 8)
            r = lax.rsqrt(spread(column[k][at], s))
            root[at] = jnp.where(sub == s, r, root[at])
            if k == group - 1:
                break
            here = lane == r0 + k
            row = jnp.where(here, 1.0, spread(p[at], s))
            for v in range(at, 2):
                if v == at and s == 7:
                    continue
                factor = column[k][v] * (r * r)
                if v == at:
                    factor = jnp.where(sub > s, factor, 0.0)
                    p[v] = jnp.where(here & (sub > s), 0.0, p[v]) - factor * row
                else:
                    p[v] = jnp.where(here, 0.0, p[v]) - factor * row
                for j in range(k + 1, group):
                    column[j][v] = column[j][v] - factor * spread(column[j][at], s)
        panel = jnp.concatenate([p[v] * root[v] for v in range(2)], axis=0)
        roots = jnp.concatenate(root, axis=0)
        ln = lax.broadcasted_iota(jnp.int32, (group, B), 1) - r0
        sb = lax.broadcasted_iota(jnp.int32, (group, B), 0)
        eliminated = jnp.where(ln == sb, roots, jnp.where((ln > sb) & (ln < group), 0.0, panel))
        upper.append(panel)
        lower.append(jnp.where(ln > sb, 0.0, eliminated))
        if g < B // group - 1:
            change = dot_f32(jnp.where(ln >= group, panel, 0.0), eliminated, ((0,), (0,)))
            lt = lax.broadcasted_iota(jnp.int32, (B - r0 - group, B), 1)
            rest = jnp.where((lt >= r0) & (lt < r0 + group), 0.0, rest[group:, :]) - change[r0 + group :, :]
    return jnp.concatenate(upper, axis=0), jnp.concatenate(lower, axis=0)


def factor_start(sq_ref, lower_ref, work):
    for i in range(NB):
        for j in range(NB):
            at = (slice(i * B, (i + 1) * B), slice(j * B, (j + 1) * B))
            if j < i:
                work[at] = jnp.zeros((B, B), F32)
            else:
                work[at] = 0.5 * (sq_ref[j, i].astype(F32) + sq_ref[i, j].astype(F32).T)
    lower_ref[...] = jnp.zeros((B, B), F32)


def factor_step(kb, my_row, my_col, inv_ref, lower_ref, work, left, right):
    lane = lax.broadcasted_iota(jnp.int32, (B, B), 1)
    sub = lax.broadcasted_iota(jnp.int32, (B, B), 0)
    d0 = pl.multiple_of(kb * B, B)
    upper, lower = diagonal_factor(work[pl.ds(d0, B), pl.ds(d0, B)])
    work[pl.ds(d0, B), pl.ds(d0, B)] = jnp.where(lane == sub, 1.0, 0.0)
    panel = dot_f32(lower, work[pl.ds(d0, B), :], ((1,), (0,)))
    col = lax.broadcasted_iota(jnp.int32, (B, N), 1)
    inv_ref[pl.ds(d0, B), :] = jnp.where(col < d0 + B, panel, 0.0).astype(BF)

    @pl.when(kb == my_col)
    def _():
        @pl.when(kb == my_row)
        def _():
            lower_ref[...] = jnp.where(lane >= sub, upper, 0.0).T

        @pl.when(kb < my_row)
        def _():
            work[pl.ds(d0, B), :] = panel
            lower_ref[...] = work[pl.ds(d0, B), pl.ds(pl.multiple_of(my_row * B, B), B)].T

    parts = splits(panel)
    for t in range(6):
        left[t * B : (t + 1) * B, :] = parts[LEFT[t]]
        right[t * B : (t + 1) * B, :] = parts[RIGHT[t]]

    def trailing(i, _):
        i0 = pl.multiple_of(i * B, B)
        work[pl.ds(i0, B), pl.ds(d0, B)] = jnp.zeros((B, B), F32)
        work[pl.ds(i0, B), :] = work[pl.ds(i0, B), :] - lax.dot_general(
            left[:, pl.ds(i0, B)], right[...], (((0,), (0,)), ((), ())), preferred_element_type=F32
        )
        return 0

    lax.fori_loop(kb + 1, NB, trailing, 0)


def below_rows(portion, cols, inv_ref, lower_ref, keep_ref, my_col, below_ref, panel_ref, first_ref, wide):
    safe = jnp.minimum(my_col, NB - 1)
    dims = (((1,), (1,)), ((), ()))

    def rows(i, _):
        a = jnp.concatenate(
            [jnp.concatenate([portion[k, 2 * i + t // 2, t % 2] for k in range(8)], axis=1) for t in range(4)], axis=0
        )
        out = lax.dot_general(a, inv_ref[...], dims, preferred_element_type=F32)
        for t in range(4):
            l = 4 * i + t
            kept = out[t * B : (t + 1) * B, :] * keep_ref[l]
            wide[t * B : (t + 1) * B, :] = kept
            below_ref[pl.ds(pl.multiple_of(l * B, B), B), :] = kept.astype(BF)
        for t in range(4):
            first_ref[4 * i + t] = wide[t * B : (t + 1) * B, pl.ds(pl.multiple_of(safe * B, B), B)]
        return 0

    lax.fori_loop(0, 4, rows, 0)
    first_ref[0] = lower_ref[...]

    def more(i, _):
        a = jnp.concatenate(
            [jnp.concatenate([cols[k, 4 * i + t] for k in range(8)], axis=1) for t in range(4)], axis=0
        )
        out = lax.dot_general(a, inv_ref[...], dims, preferred_element_type=F32)
        for t in range(4):
            m = 4 * i + t
            kept = out[t * B : (t + 1) * B, :] * keep_ref[16 + m]
            panel_ref[pl.ds(pl.multiple_of(m * B, B), B), :] = kept.astype(BF)
        return 0

    lax.fori_loop(0, 2, more, 0)


def factor_kernel(piece, keep_ref, below_ref, panel_ref, first_ref, sq, portion, cols, inv_ref, lower_ref, work, left, right, wide, *sems):
    my_row, my_col = lax.axis_index("row"), lax.axis_index("col")
    gather = Gather(piece, sq, portion, cols, sems)
    gather.enter()
    gather.square()
    gather.first()
    factor_start(sq, lower_ref, work)

    def step(kb, _):
        @pl.when(kb == 3)
        def _():
            gather.second()

        @pl.when(kb == 7)
        def _():
            gather.third()

        factor_step(kb, my_row, my_col, inv_ref, lower_ref, work, left, right)
        return 0

    lax.fori_loop(0, NB, step, 0)
    gather.last()
    below_rows(portion, cols, inv_ref, lower_ref, keep_ref, my_col, below_ref, panel_ref, first_ref, wide)
    gather.finish()


FACTOR_OUT = (
    jax.ShapeDtypeStruct((16 * B, N), BF),
    jax.ShapeDtypeStruct((8 * B, N), BF),
    jax.ShapeDtypeStruct((16, B, B), F32),
)
FACTOR_SCRATCH = (
    ((8, 8, B, B), BF),
    ((8, 8, 2, B, B), BF),
    ((8, 8, B, B), BF),
    ((N, N), BF),
    ((B, B), F32),
    ((N, N), F32),
    ((6 * B, N), BF),
    ((6 * B, N), BF),
    ((4 * B, N), F32),
)


def factor(piece, keep):
    return pl.pallas_call(
        factor_kernel,
        out_shape=FACTOR_OUT,
        in_specs=[ANY, SM],
        out_specs=(VM, VM, VM),
        scratch_shapes=[pltpu.VMEM(s, d) for s, d in FACTOR_SCRATCH]
        + [pltpu.SemaphoreType.DMA((n,)) for n in Gather.SEMS],
        compiler_params=params(collective_id=2, has_side_effects=True),
    )(piece, keep)


def schur_kernel(tab, front, arrived, below, panel, first, out_ref):
    i = pl.program_id(0)
    my_col = lax.axis_index("col")
    product = lax.dot_general(below[...], panel[...], (((1,), (1,)), ((), ())), preferred_element_type=F32)
    for s in range(2):
        l = 2 * i + s
        initial = jnp.swapaxes(front[s], 0, 1)
        values = []
        for m in range(8):
            value = initial[m].astype(F32)
            for h in range(2):
                valid = tab[AT_RCH + h * 16 + l] == tab[AT_CCH + h * 8 + m]
                at = jnp.where(valid, tab[AT_RSRC + h * 16 + l] + tab[AT_CSRC + h * 8 + m], 0)
                value = value + jnp.where(valid, arrived[at].astype(F32), 0.0)
            value = value - product[s * B : (s + 1) * B, m * B : (m + 1) * B]
            if s == 0:
                value = jnp.where(l == 0, 0.0, value)
            if m == 0:
                value = jnp.where(my_col < NB, first[s], value)
            values.append(value)
        out_ref[s] = jnp.swapaxes(jnp.stack(values), 0, 1)


def schur(tab, front, arrived, below, panel, first):
    full = lambda shape: pl.BlockSpec(shape, lambda i, t: (0,) * len(shape))
    return pl.pallas_call(
        schur_kernel,
        out_shape=jax.ShapeDtypeStruct((16, B, 8, B), F32),
        grid_spec=pltpu.PrefetchScalarGridSpec(
            num_scalar_prefetch=1,
            grid=(8,),
            in_specs=[
                pl.BlockSpec((2, B, 8, B), lambda i, t: (i, 0, 0, 0)),
                full((256, B, B)),
                pl.BlockSpec((2 * B, N), lambda i, t: (i, 0)),
                full((N, N)),
                pl.BlockSpec((2, B, B), lambda i, t: (i, 0, 0)),
            ],
            out_specs=pl.BlockSpec((2, B, 8, B), lambda i, t: (i, 0, 0, 0)),
        ),
        compiler_params=params(),
    )(tab, front, arrived, below, panel, first)


def per_device(child_update_blocks, child_pivot_panel, child_map, coupled, parent_front):
    my_row, my_col = lax.axis_index("row"), lax.axis_index("col")
    front = parent_front.reshape(16, B, 8, B)
    out_tab = table(outgoing_kernel, 24, child_map)
    row_op, col_op = panel_gather(child_pivot_panel.reshape(8, 2, B, B))
    outgoing = contributions(out_tab, child_update_blocks.reshape(16, B, 8, B), row_op.reshape(8, 16, B, B), col_op)
    incoming = lax.all_to_all(outgoing, ("row", "col"), split_axis=0, concat_axis=0, tiled=True)
    arrived = incoming.reshape(256, B, B)
    later_map, later_coupled, _ = lax.optimization_barrier((child_map, coupled, outgoing))
    in_tab = table(incoming_kernel, 96, later_map)
    kept = jnp.concatenate([jnp.ones((NB,), F32), later_coupled.astype(F32)])
    keep = jnp.concatenate(
        [
            lax.dynamic_index_in_dim(kept.reshape(16, 8), my_row, 1, keepdims=False),
            lax.dynamic_index_in_dim(kept.reshape(8, 16), my_col, 1, keepdims=False),
        ]
    )
    pivots = pivot_columns(in_tab, arrived, front[:, :, 0, :])
    below, panel, first = factor(pivots.reshape(8, 2, B, B), keep)
    out = schur(in_tab, front, arrived, below, panel, first)
    return out.reshape(1, 16, B, 1, 8, B)


def solution(mesh):
    in_specs = (
        P("row", None, None, "col", None, None),
        P("row", None, None, "col", None),
        P(),
        P(),
        P("row", None, None, "col", None, None),
    )
    out_specs = P("row", None, None, "col", None, None)
    return jax.shard_map(per_device, mesh=mesh, in_specs=in_specs, out_specs=out_specs, check_vma=False)
```

```python
import functools

import jax
import jax.numpy as jnp
from jax import lax
from jax.experimental import pallas as pl
from jax.experimental.pallas import tpu as pltpu
from jax.sharding import PartitionSpec as P

B = 128
NB = 8
N = NB * B
F32 = jnp.float32
BF = jnp.bfloat16
MESH = pl.DeviceIdType.MESH
ANY = pl.BlockSpec(memory_space=pl.ANY)
VM = pl.BlockSpec(memory_space=pltpu.VMEM)
SM = pl.BlockSpec(memory_space=pltpu.SMEM)
LIMIT = 56 * 1024 * 1024


def params(**kw):
    return pltpu.CompilerParams(vmem_limit_bytes=LIMIT, **kw)


OUT_ROW, OUT_COL = 0, 16
AT_RSRC, AT_RCH, AT_CSRC, AT_CCH = 0, 32, 64, 80


def clear(count):
    def one(i, _):
        count[i] = 0
        return 0

    lax.fori_loop(0, 16, one, 0)


def outgoing_kernel(map_ref, tab_ref, count):
    my_row, my_col = lax.axis_index("row"), lax.axis_index("col")
    row_rank, col_rank = my_row % 4, my_col % 8
    child = 2 * (my_row // 4) + my_col // 8
    clear(count)
    for l in range(16):
        owner = map_ref[child, l * 4 + row_rank] % 8
        tab_ref[OUT_ROW + owner * 2 + count[owner]] = l
        count[owner] = count[owner] + 1
    for c in range(16):
        tab_ref[OUT_COL + c] = 0
    for m in range(8):
        tab_ref[OUT_COL + map_ref[child, m * 8 + col_rank] % 16] = m


def incoming_kernel(map_ref, tab_ref, count):
    my_row, my_col = lax.axis_index("row"), lax.axis_index("col")
    clear(count)

    def arrive(q, _):
        h, g = q // 2, q % 2

        def one(b, _):
            target = map_ref[q, b]

            @pl.when(target % 8 == my_row)
            def _():
                slot = q * 4 + b % 4
                at = h * 16 + target // 8
                tab_ref[AT_RSRC + at] = (h * 4 + b % 4) * 32 + count[slot]
                tab_ref[AT_RCH + at] = g
                count[slot] = count[slot] + 1

            @pl.when(target % 16 == my_col)
            def _():
                at = h * 8 + target // 16
                tab_ref[AT_CSRC + at] = (g * 8 + b % 8) * 2
                tab_ref[AT_CCH + at] = g

            return 0

        lax.fori_loop(0, 64, one, 0)
        return 0

    lax.fori_loop(0, 4, arrive, 0)


def table(kernel, size, child_map):
    return pl.pallas_call(
        kernel,
        out_shape=jax.ShapeDtypeStruct((size,), jnp.int32),
        in_specs=[SM],
        out_specs=SM,
        scratch_shapes=[pltpu.SMEM((16,), jnp.int32)],
        cost_estimate=pl.CostEstimate(flops=20000, bytes_accessed=2048, transcendentals=0),
    )(child_map)


def remote(src, dst, s, r, row, col):
    return pltpu.make_async_remote_copy(
        src_ref=src, dst_ref=dst, send_sem=s, recv_sem=r, device_id=(row, col), device_id_type=MESH
    )


def contribution_kernel(tab, p_ref, u_hbm, out_hbm, row_ref, col_ref, total, u_ref, block, slots, local, s_chip, s_sib, s_col, r_row, r_col):
    my_row, my_col = lax.axis_index("row"), lax.axis_index("col")
    base, y = my_row // 4 * 4, my_row % 4
    half, cc = my_col // 8 * 8, my_col % 8
    core, pair, parity = cc % 2, cc // 2, cc // 4
    sibling = half + pair * 2 + 1 - core
    y0 = cc % 4
    step = jnp.where(y0 % 2 == 0, 3, 1)
    outer = (y0 + step) % 4
    inner = y0 + 1 - 2 * (y0 % 2)
    last = outer + 1 - 2 * (outer % 2)
    is_source, is_relay = y == y0, y == outer
    fetch = pltpu.make_async_copy(u_hbm, u_ref, local.at[2])
    fetch.start()
    barrier = pltpu.get_barrier_semaphore()

    def greet(row, col):
        pl.semaphore_signal(barrier, inc=1, device_id=(row, col), device_id_type=MESH)

    others = [half + (pair + d) % 4 * 2 + core for d in (2, 1, 3)]
    for col in others:
        greet(my_row, col)
    greet(my_row, sibling)

    @pl.when(jnp.logical_not(is_source))
    def _():
        greet(base + jnp.where(y == last, outer, y0), my_col)

    pl.semaphore_wait(barrier, 4 + jnp.where(is_source, 2, jnp.where(is_relay, 1, 0)))

    order = [cc, pair * 2 + 1 - core] + [(pair + d) % 4 * 2 + core for d in (2, 1, 3)]
    order += [(pair + d) % 4 * 2 + 1 - core for d in (2, 1, 3)]

    def chip_send(i):
        return remote(p_ref, row_ref.at[cc], s_chip.at[i], r_row.at[cc], my_row, others[i])

    def sib_send(e):
        src = p_ref if e == 0 else row_ref.at[order[e]]
        return remote(src, row_ref.at[order[e]], s_sib.at[max(e - 1, 0)], r_row.at[order[e]], my_row, sibling)

    def col_send(e, t):
        src = p_ref.at[:, parity] if e == 0 else row_ref.at[order[e], :, parity]
        return remote(src, col_ref.at[order[e]], s_col.at[e, t], r_col.at[order[e]], base + (outer, inner)[t], my_col)

    def pass_on(e):
        j = order[e]
        return remote(col_ref.at[j], col_ref.at[j], s_col.at[e, 0], r_col.at[j], base + last, my_col)

    for i in range(3):
        chip_send(i).start()
    sib_send(0).start()

    @pl.when(is_source)
    def _():
        col_send(0, 0).start()
        col_send(0, 1).start()

    row_ref[cc] = p_ref[...]

    for e in range(8):
        j = order[e]
        if e:
            remote(p_ref, row_ref.at[j], s_sib.at[0], r_row.at[j], my_row, sibling).wait_recv()
            if 2 <= e < 5:
                sib_send(e).start()

            @pl.when(is_source)
            def _():
                col_send(e, 0).start()
                col_send(e, 1).start()

        if e % 2 == 0:
            continue

        @pl.when(is_source)
        def _():
            for i in (order[e - 1], j):
                col_ref[i] = row_ref[i, :, parity]

        @pl.when(jnp.logical_not(is_source))
        def _():
            for f in (e - 1, e):
                pass_on(f).wait_recv()

                @pl.when(is_relay)
                def _():
                    pass_on(f).start()

        def product(i, _):
            left = [row_ref[f, pl.ds(2 * i, 2)].reshape(4 * B, B) for f in (order[e - 1], j)]
            right = [col_ref[f].reshape(8 * B, B) for f in (order[e - 1], j)]
            more = lax.dot_general(
                jnp.concatenate(left, axis=1), jnp.concatenate(right, axis=1), (((1,), (1,)), ((), ())),
                preferred_element_type=F32,
            )
            for m in range(8):
                part = more[:, m * B : (m + 1) * B].reshape(4, B, B)
                at = pl.ds(4 * i, 4)
                total[m, at] = part if e == 1 else total[m, at] + part
            return 0

        lax.fori_loop(0, 4, product, 0)

    fetch.wait()

    def emit(owner, slot):
        return pltpu.make_async_copy(slots.at[slot], out_hbm.at[pl.ds(owner * 16, 16)], local.at[slot])

    def lay_out(owner, _):
        slot = owner % 2

        @pl.when(owner >= 2)
        def _():
            emit(owner - 2, slot).wait()

        for s in range(2):
            l = tab[OUT_ROW + owner * 2 + s]
            update = jnp.swapaxes(u_ref[l], 0, 1)
            for m in range(8):
                block[m] = (update[m].astype(F32) - total[m, l]).astype(BF)
            for c in range(16):
                slots[slot, c, s * B : (s + 1) * B, :] = block[tab[OUT_COL + c]]
        emit(owner, slot).start()
        return 0

    lax.fori_loop(0, 8, lay_out, 0)
    for slot in range(2):
        emit(6 + slot, slot).wait()
    for i in range(3):
        chip_send(i).wait_send()
    for e in (0, 2, 3, 4):
        sib_send(e).wait_send()

    @pl.when(is_source)
    def _():
        for e in range(8):
            col_send(e, 0).wait_send()
            col_send(e, 1).wait_send()

    @pl.when(is_relay)
    def _():
        for e in range(8):
            pass_on(e).wait_send()


def contributions(tab, piece, update):
    dma = pltpu.SemaphoreType.DMA
    return pl.pallas_call(
        contribution_kernel,
        out_shape=jax.ShapeDtypeStruct((128, 2 * B, B), BF),
        in_specs=[SM, VM, ANY],
        out_specs=ANY,
        scratch_shapes=[
            pltpu.VMEM((8, 8, 2, B, B), BF),
            pltpu.VMEM((8, 8, B, B), BF),
            pltpu.VMEM((8, 16, B, B), F32),
            pltpu.VMEM((16, B, 8, B), BF),
            pltpu.VMEM((8, B, B), BF),
            pltpu.VMEM((2, 16, 2 * B, B), BF),
            dma((3,)),
            dma((3,)),
            dma((4,)),
            dma((8, 2)),
            dma((8,)),
            dma((8,)),
        ],
        compiler_params=params(collective_id=1, has_side_effects=True),
    )(tab, piece, update)


def pivot_kernel(tab, arrived, front, out_ref, block, sem):
    def fits(l, h):
        return tab[AT_RCH + h * 16 + l] == tab[AT_CCH + h * 8]

    def fetch(l, h):
        at = jnp.where(fits(l, h), tab[AT_RSRC + h * 16 + l] + tab[AT_CSRC + h * 8], 0)
        return pltpu.make_async_copy(arrived.at[at], block.at[h, l], sem.at[h, l])

    for l in range(16):
        for h in range(2):
            fetch(l, h).start()
    for l in range(16):
        value = front[l].astype(F32)
        for h in range(2):
            valid = fits(l, h)
            fetch(l, h).wait()
            value = value + jnp.where(valid, block[h, l].astype(F32), 0.0)
        out_ref[l] = value.astype(BF)


def pivot_columns(tab, arrived, front):
    return pl.pallas_call(
        pivot_kernel,
        out_shape=jax.ShapeDtypeStruct((16, B, B), BF),
        in_specs=[SM, ANY, VM],
        out_specs=VM,
        scratch_shapes=[pltpu.VMEM((2, 16, B, B), BF), pltpu.SemaphoreType.DMA((2, 16))],
        compiler_params=params(),
    )(tab, arrived, front)


class Gather:
    SEMS = (2, 7, 7, 4, 3, 2, 4, 8, 8, 8, 8, 8)

    def __init__(self, piece, sq, portion, cols, sems):
        self.piece, self.sq, self.portion, self.cols = piece, sq, portion, cols
        (self.local, self.s_row, self.s_sq, self.s_sqf, self.s_z, self.s_x, self.s_sib, self.s_cols) = sems[:8]
        self.r_row, self.r_sq, self.r_por, self.r_cols = sems[8:]
        self.row, self.col = lax.axis_index("row"), lax.axis_index("col")
        col = self.col
        self.z, self.xh, self.core = col // 4, col // 2 % 2, col % 2
        self.zh = self.z // 2
        self.chip = col // 2
        self.sibling = self.chip * 2 + 1 - self.core
        self.across = self.z * 4 + (1 - self.xh) * 2 + self.core
        self.owner = col < 8
        self.same = col % 8 == self.row

    def chips(self):
        return [(self.chip + d) % 8 * 2 + self.core for d in (4, 1, 7, 2, 6, 3, 5)]

    def enter(self):
        barrier = pltpu.get_barrier_semaphore()

        def greet(row, col):
            pl.semaphore_signal(barrier, inc=1, device_id=(row, col), device_id_type=MESH)

        greet(self.row, self.sibling)
        greet(self.row, self.across)

        @pl.when(self.owner)
        def _():
            for d in range(1, 8):
                greet((self.row + d) % 8, self.col)

        for i in range(4):
            j = 2 * i + self.core

            @pl.when(j != self.col)
            def _():
                greet(self.row, j)

        for d in range(8):
            j = (self.col + d) % 8
            if d:
                greet(self.col % 8, self.zh * 8 + j)
            else:

                @pl.when(jnp.logical_not(self.same))
                def _():
                    greet(self.col % 8, self.zh * 8 + j)

        pl.semaphore_wait(barrier, 10 + jnp.where(self.owner, 14, 0) - jnp.where(self.same, 1, 0))

    def row_sends(self):
        dst = self.sq.at[self.col, self.row]
        return [
            remote(self.piece.at[0, 0], dst, self.s_row.at[d - 1], self.r_row.at[self.row], (self.row + d) % 8, self.col)
            for d in range(1, 8)
        ]

    def sq_sends(self):
        c = self.sq.at[self.col]
        return [
            remote(c, c, self.s_sq.at[i], self.r_sq.at[self.col], self.row, t) for i, t in enumerate(self.chips())
        ]

    def z_sends(self):
        c = self.portion.at[self.col]
        return [
            remote(self.piece, c, self.s_z.at[d - 1], self.r_por.at[self.col], self.row, (self.col + 4 * d) % 16)
            for d in (2, 1, 3)
        ]

    def x_sends(self):
        out = []
        for zp in range(2):
            j = zp * 4 + self.xh * 2 + self.core
            out.append(remote(self.portion.at[j], self.portion.at[j], self.s_x.at[zp], self.r_por.at[j], self.row, self.across))
        return out

    def sib_sends(self):
        out = []
        for i in range(4):
            j = 2 * i + self.core
            out.append(remote(self.portion.at[j], self.portion.at[j], self.s_sib.at[i], self.r_por.at[j], self.row, self.sibling))
        return out

    def cols_send(self, d):
        j = self.col % 8
        src = self.portion.at[j, :, self.zh]
        return remote(
            src, self.cols.at[j], self.s_cols.at[d], self.r_cols.at[j], (self.row + d) % 8, self.row + 8 * self.zh
        )

    def cols_sends(self):
        return [self.cols_send(d) for d in (4, 1, 3, 5, 7, 2, 6)]

    def arrived(self, ref, sem):
        remote(ref, ref, self.s_row.at[0], sem, self.row, self.sibling).wait_recv()

    def square(self):
        @pl.when(self.owner)
        def _():
            first = pltpu.make_async_copy(self.piece.at[0, 0], self.sq.at[self.col, self.row], self.local.at[0])
            whole = pltpu.make_async_copy(self.piece, self.portion.at[self.col], self.local.at[1])
            first.start()
            for s in self.row_sends():
                s.start()
            whole.start()
            first.wait()
            for d in range(1, 8):
                i = (self.row + d) % 8
                self.arrived(self.sq.at[self.col, i], self.r_row.at[i])
            for s in self.sq_sends():
                s.start()
            whole.wait()
            for s in self.z_sends():
                s.start()

        for i in range(4):
            j = 2 * i + self.core

            @pl.when(j != self.col)
            def _():
                self.arrived(self.sq.at[j], self.r_sq.at[j])

            c = self.sq.at[j]
            remote(c, c, self.s_sqf.at[i], self.r_sq.at[j], self.row, self.sibling).start()
        for i in range(4):
            j = 2 * i + 1 - self.core
            self.arrived(self.sq.at[j], self.r_sq.at[j])

    def cols_start(self):
        for s in self.cols_sends():
            s.start()

        @pl.when(jnp.logical_not(self.same))
        def _():
            self.cols_send(0).start()

    def second(self):
        for zp in range(2):
            j = zp * 4 + self.xh * 2 + self.core

            @pl.when(j != self.col)
            def _():
                self.arrived(self.portion.at[j], self.r_por.at[j])

        for s in self.x_sends():
            s.start()
        self.cols_start()

        @pl.when(self.same)
        def _():
            self.cols[self.col % 8] = self.portion[self.col % 8, :, self.zh]

    def third(self):
        for zp in range(2):
            j = zp * 4 + (1 - self.xh) * 2 + self.core
            self.arrived(self.portion.at[j], self.r_por.at[j])
        for s in self.sib_sends():
            s.start()

    def last(self):
        for i in range(4):
            j = 2 * i + 1 - self.core
            self.arrived(self.portion.at[j], self.r_por.at[j])
        for d in range(1, 8):
            j = (self.col + d) % 8
            self.arrived(self.cols.at[j], self.r_cols.at[j])

        @pl.when(jnp.logical_not(self.same))
        def _():
            j = self.col % 8
            self.arrived(self.cols.at[j], self.r_cols.at[j])

    def finish(self):
        for i in range(4):
            c = self.sq.at[2 * i + self.core]
            remote(c, c, self.s_sqf.at[i], self.r_sq.at[0], self.row, self.sibling).wait_send()
        for s in self.x_sends() + self.sib_sends() + self.cols_sends():
            s.wait_send()

        @pl.when(jnp.logical_not(self.same))
        def _():
            self.cols_send(0).wait_send()

        @pl.when(self.owner)
        def _():
            for s in self.row_sends() + self.sq_sends() + self.z_sends():
                s.wait_send()


def splits(a):
    parts = []
    for i in range(3):
        h = a.astype(BF)
        parts.append(h)
        if i < 2:
            a = a - h.astype(F32)
    return parts


LEFT = (0, 0, 1, 1, 0, 2)
RIGHT = (0, 1, 0, 1, 2, 0)


def dot_f32(a, b, dims):
    sa, sb = splits(a), splits(b)
    left = jnp.concatenate([sa[i] for i in LEFT], axis=dims[0][0])
    right = jnp.concatenate([sb[i] for i in RIGHT], axis=dims[1][0])
    return lax.dot_general(left, right, (dims, ((), ())), preferred_element_type=F32)


def diagonal_factor(square):
    group = 16
    lane = lax.broadcasted_iota(jnp.int32, (8, B), 1)
    sub = lax.broadcasted_iota(jnp.int32, (8, B), 0)
    spread = lambda x, s: jnp.broadcast_to(x[s : s + 1, :], (8, B))
    rest, upper, lower = square, [], []
    for g in range(B // group):
        r0 = group * g
        p = [rest[8 * v : 8 * v + 8, :] for v in range(2)]
        column = [[jnp.broadcast_to(p[v][:, r0 + j : r0 + j + 1], (8, B)) for v in range(2)] for j in range(group)]
        root = [jnp.zeros((8, B), F32) for _ in range(2)]
        for k in range(group):
            at, s = divmod(k, 8)
            r = lax.rsqrt(spread(column[k][at], s))
            root[at] = jnp.where(sub == s, r, root[at])
            if k == group - 1:
                break
            here = lane == r0 + k
            row = jnp.where(here, 1.0, spread(p[at], s))
            for v in range(at, 2):
                if v == at and s == 7:
                    continue
                factor = column[k][v] * (r * r)
                if v == at:
                    factor = jnp.where(sub > s, factor, 0.0)
                    p[v] = jnp.where(here & (sub > s), 0.0, p[v]) - factor * row
                else:
                    p[v] = jnp.where(here, 0.0, p[v]) - factor * row
                for j in range(k + 1, group):
                    column[j][v] = column[j][v] - factor * spread(column[j][at], s)
        panel = jnp.concatenate([p[v] * root[v] for v in range(2)], axis=0)
        roots = jnp.concatenate(root, axis=0)
        ln = lax.broadcasted_iota(jnp.int32, (group, B), 1) - r0
        sb = lax.broadcasted_iota(jnp.int32, (group, B), 0)
        eliminated = jnp.where(ln == sb, roots, jnp.where((ln > sb) & (ln < group), 0.0, panel))
        upper.append(panel)
        lower.append(jnp.where(ln > sb, 0.0, eliminated))
        if g < B // group - 1:
            change = dot_f32(jnp.where(ln >= group, panel, 0.0), eliminated, ((0,), (0,)))
            lt = lax.broadcasted_iota(jnp.int32, (B - r0 - group, B), 1)
            rest = jnp.where((lt >= r0) & (lt < r0 + group), 0.0, rest[group:, :]) - change[r0 + group :, :]
    return jnp.concatenate(upper, axis=0), jnp.concatenate(lower, axis=0)


def factor_start(sq_ref, lower_ref, work):
    for i in range(NB):
        for j in range(NB):
            at = (slice(i * B, (i + 1) * B), slice(j * B, (j + 1) * B))
            if j < i:
                work[at] = jnp.zeros((B, B), F32)
            else:
                work[at] = 0.5 * (sq_ref[j, i].astype(F32) + sq_ref[i, j].astype(F32).T)
    lower_ref[...] = jnp.zeros((B, B), F32)


def factor_step(kb, my_row, my_col, inv_ref, lower_ref, work, left, right):
    lane = lax.broadcasted_iota(jnp.int32, (B, B), 1)
    sub = lax.broadcasted_iota(jnp.int32, (B, B), 0)
    d0 = pl.multiple_of(kb * B, B)
    upper, lower = diagonal_factor(work[pl.ds(d0, B), pl.ds(d0, B)])
    work[pl.ds(d0, B), pl.ds(d0, B)] = jnp.where(lane == sub, 1.0, 0.0)
    panel = dot_f32(lower, work[pl.ds(d0, B), :], ((1,), (0,)))
    col = lax.broadcasted_iota(jnp.int32, (B, N), 1)
    inv_ref[pl.ds(d0, B), :] = jnp.where(col < d0 + B, panel, 0.0).astype(BF)

    @pl.when(kb == my_col)
    def _():
        @pl.when(kb == my_row)
        def _():
            lower_ref[...] = jnp.where(lane >= sub, upper, 0.0).T

        @pl.when(kb < my_row)
        def _():
            work[pl.ds(d0, B), :] = panel
            lower_ref[...] = work[pl.ds(d0, B), pl.ds(pl.multiple_of(my_row * B, B), B)].T

    parts = splits(panel)
    for t in range(6):
        left[t * B : (t + 1) * B, :] = parts[LEFT[t]]
        right[t * B : (t + 1) * B, :] = parts[RIGHT[t]]

    def trailing(i, _):
        i0 = pl.multiple_of(i * B, B)
        work[pl.ds(i0, B), pl.ds(d0, B)] = jnp.zeros((B, B), F32)
        work[pl.ds(i0, B), :] = work[pl.ds(i0, B), :] - lax.dot_general(
            left[:, pl.ds(i0, B)], right[...], (((0,), (0,)), ((), ())), preferred_element_type=F32
        )
        return 0

    lax.fori_loop(kb + 1, NB, trailing, 0)


def below_rows(portion, cols, inv_ref, lower_ref, keep_ref, my_col, below_ref, panel_ref, first_ref, wide):
    safe = jnp.minimum(my_col, NB - 1)
    dims = (((1,), (1,)), ((), ()))

    def rows(i, _):
        a = jnp.concatenate(
            [jnp.concatenate([portion[k, 2 * i + t // 2, t % 2] for k in range(8)], axis=1) for t in range(4)], axis=0
        )
        out = lax.dot_general(a, inv_ref[...], dims, preferred_element_type=F32)
        for t in range(4):
            l = 4 * i + t
            kept = out[t * B : (t + 1) * B, :] * keep_ref[l]
            wide[t * B : (t + 1) * B, :] = kept
            below_ref[pl.ds(pl.multiple_of(l * B, B), B), :] = kept.astype(BF)
        for t in range(4):
            first_ref[4 * i + t] = wide[t * B : (t + 1) * B, pl.ds(pl.multiple_of(safe * B, B), B)]
        return 0

    lax.fori_loop(0, 4, rows, 0)
    first_ref[0] = lower_ref[...]

    def more(i, _):
        a = jnp.concatenate(
            [jnp.concatenate([cols[k, 4 * i + t] for k in range(8)], axis=1) for t in range(4)], axis=0
        )
        out = lax.dot_general(a, inv_ref[...], dims, preferred_element_type=F32)
        for t in range(4):
            m = 4 * i + t
            kept = out[t * B : (t + 1) * B, :] * keep_ref[16 + m]
            panel_ref[pl.ds(pl.multiple_of(m * B, B), B), :] = kept.astype(BF)
        return 0

    lax.fori_loop(0, 2, more, 0)


def factor_kernel(piece, keep_ref, below_ref, panel_ref, first_ref, sq, portion, cols, inv_ref, lower_ref, work, left, right, wide, *sems):
    my_row, my_col = lax.axis_index("row"), lax.axis_index("col")
    gather = Gather(piece, sq, portion, cols, sems)
    gather.enter()
    gather.square()
    gather.second()
    factor_start(sq, lower_ref, work)

    def step(kb, _):
        @pl.when(kb == 6)
        def _():
            gather.third()

        factor_step(kb, my_row, my_col, inv_ref, lower_ref, work, left, right)
        return 0

    lax.fori_loop(0, NB, step, 0)
    gather.last()
    below_rows(portion, cols, inv_ref, lower_ref, keep_ref, my_col, below_ref, panel_ref, first_ref, wide)
    gather.finish()


FACTOR_OUT = (
    jax.ShapeDtypeStruct((16 * B, N), BF),
    jax.ShapeDtypeStruct((8 * B, N), BF),
    jax.ShapeDtypeStruct((16, B, B), F32),
)
FACTOR_SCRATCH = (
    ((8, 8, B, B), BF),
    ((8, 8, 2, B, B), BF),
    ((8, 8, B, B), BF),
    ((N, N), BF),
    ((B, B), F32),
    ((N, N), F32),
    ((6 * B, N), BF),
    ((6 * B, N), BF),
    ((4 * B, N), F32),
)


def factor(piece, keep):
    return pl.pallas_call(
        factor_kernel,
        out_shape=FACTOR_OUT,
        in_specs=[ANY, SM],
        out_specs=(VM, VM, VM),
        scratch_shapes=[pltpu.VMEM(s, d) for s, d in FACTOR_SCRATCH]
        + [pltpu.SemaphoreType.DMA((n,)) for n in Gather.SEMS],
        compiler_params=params(collective_id=2, has_side_effects=True),
    )(piece, keep)


def schur_kernel(tab, front, arrived, below, panel, first, out_ref):
    i = pl.program_id(0)
    my_col = lax.axis_index("col")
    product = lax.dot_general(below[...], panel[...], (((1,), (1,)), ((), ())), preferred_element_type=F32)
    for s in range(2):
        l = 2 * i + s
        initial = jnp.swapaxes(front[s], 0, 1)
        values = []
        for m in range(8):
            value = initial[m].astype(F32)
            for h in range(2):
                valid = tab[AT_RCH + h * 16 + l] == tab[AT_CCH + h * 8 + m]
                at = jnp.where(valid, tab[AT_RSRC + h * 16 + l] + tab[AT_CSRC + h * 8 + m], 0)
                value = value + jnp.where(valid, arrived[at].astype(F32), 0.0)
            value = value - product[s * B : (s + 1) * B, m * B : (m + 1) * B]
            if s == 0:
                value = jnp.where(l == 0, 0.0, value)
            if m == 0:
                value = jnp.where(my_col < NB, first[s], value)
            values.append(value)
        out_ref[s] = jnp.swapaxes(jnp.stack(values), 0, 1)


def schur(tab, front, arrived, below, panel, first):
    full = lambda shape: pl.BlockSpec(shape, lambda i, t: (0,) * len(shape))
    return pl.pallas_call(
        schur_kernel,
        out_shape=jax.ShapeDtypeStruct((16, B, 8, B), F32),
        grid_spec=pltpu.PrefetchScalarGridSpec(
            num_scalar_prefetch=1,
            grid=(8,),
            in_specs=[
                pl.BlockSpec((2, B, 8, B), lambda i, t: (i, 0, 0, 0)),
                full((256, B, B)),
                pl.BlockSpec((2 * B, N), lambda i, t: (i, 0)),
                full((N, N)),
                pl.BlockSpec((2, B, B), lambda i, t: (i, 0, 0)),
            ],
            out_specs=pl.BlockSpec((2, B, 8, B), lambda i, t: (i, 0, 0, 0)),
        ),
        compiler_params=params(),
    )(tab, front, arrived, below, panel, first)


def per_device(child_update_blocks, child_pivot_panel, child_map, coupled, parent_front):
    my_row, my_col = lax.axis_index("row"), lax.axis_index("col")
    front = parent_front.reshape(16, B, 8, B)
    out_tab = table(outgoing_kernel, 32, child_map)
    outgoing = contributions(out_tab, child_pivot_panel.reshape(8, 2, B, B), child_update_blocks.reshape(16, B, 8, B))
    incoming = lax.all_to_all(outgoing, ("row", "col"), split_axis=0, concat_axis=0, tiled=True)
    arrived = incoming.reshape(256, B, B)
    later_map, later_coupled, _ = lax.optimization_barrier((child_map, coupled, outgoing))
    in_tab = table(incoming_kernel, 96, later_map)
    kept = jnp.concatenate([jnp.ones((NB,), F32), later_coupled.astype(F32)])
    keep = jnp.concatenate(
        [
            lax.dynamic_index_in_dim(kept.reshape(16, 8), my_row, 1, keepdims=False),
            lax.dynamic_index_in_dim(kept.reshape(8, 16), my_col, 1, keepdims=False),
        ]
    )
    pivots = pivot_columns(in_tab, arrived, front[:, :, 0, :])
    below, panel, first = factor(pivots.reshape(8, 2, B, B), keep)
    out = schur(in_tab, front, arrived, below, panel, first)
    return out.reshape(1, 16, B, 1, 8, B)


def solution(mesh):
    in_specs = (
        P("row", None, None, "col", None, None),
        P("row", None, None, "col", None),
        P(),
        P(),
        P("row", None, None, "col", None, None),
    )
    out_specs = P("row", None, None, "col", None, None)
    return jax.shard_map(per_device, mesh=mesh, in_specs=in_specs, out_specs=out_specs, check_vma=False)
```

```python
import functools

import jax
import jax.numpy as jnp
from jax import lax
from jax.experimental import pallas as pl
from jax.experimental.pallas import tpu as pltpu
from jax.sharding import PartitionSpec as P

B = 128
NB = 8
N = NB * B
F32 = jnp.float32
BF = jnp.bfloat16
MESH = pl.DeviceIdType.MESH
ANY = pl.BlockSpec(memory_space=pl.ANY)
VM = pl.BlockSpec(memory_space=pltpu.VMEM)
SM = pl.BlockSpec(memory_space=pltpu.SMEM)
MIB = 1024 * 1024


def params(mib, **kw):
    return pltpu.CompilerParams(vmem_limit_bytes=mib * MIB, **kw)


OUT_ROW, OUT_COL = 0, 16
AT_RSRC, AT_RCH, AT_CSRC, AT_CCH = 0, 32, 64, 80


def clear(count):
    def one(i, _):
        count[i] = 0
        return 0

    lax.fori_loop(0, 16, one, 0)


def outgoing_kernel(map_ref, tab_ref, count):
    my_row, my_col = lax.axis_index("row"), lax.axis_index("col")
    row_rank, col_rank = my_row % 4, my_col % 8
    child = 2 * (my_row // 4) + my_col // 8
    clear(count)
    for l in range(16):
        owner = map_ref[child, l * 4 + row_rank] % 8
        tab_ref[OUT_ROW + owner * 2 + count[owner]] = l
        count[owner] = count[owner] + 1
    for c in range(16):
        tab_ref[OUT_COL + c] = 0
    for m in range(8):
        tab_ref[OUT_COL + map_ref[child, m * 8 + col_rank] % 16] = m


def incoming_kernel(map_ref, tab_ref, count):
    my_row, my_col = lax.axis_index("row"), lax.axis_index("col")
    clear(count)

    def arrive(q, _):
        h, g = q // 2, q % 2

        def one(b, _):
            target = map_ref[q, b]

            @pl.when(target % 8 == my_row)
            def _():
                slot = q * 4 + b % 4
                at = h * 16 + target // 8
                tab_ref[AT_RSRC + at] = (h * 4 + b % 4) * 32 + count[slot]
                tab_ref[AT_RCH + at] = g
                count[slot] = count[slot] + 1

            @pl.when(target % 16 == my_col)
            def _():
                at = h * 8 + target // 16
                tab_ref[AT_CSRC + at] = (g * 8 + b % 8) * 2
                tab_ref[AT_CCH + at] = g

            return 0

        lax.fori_loop(0, 64, one, 0)
        return 0

    lax.fori_loop(0, 4, arrive, 0)


def table(kernel, size, child_map):
    return pl.pallas_call(
        kernel,
        out_shape=jax.ShapeDtypeStruct((size,), jnp.int32),
        in_specs=[SM],
        out_specs=SM,
        scratch_shapes=[pltpu.SMEM((16,), jnp.int32)],
        cost_estimate=pl.CostEstimate(flops=20000, bytes_accessed=2048, transcendentals=0),
    )(child_map)


def remote(src, dst, s, r, row, col):
    return pltpu.make_async_remote_copy(
        src_ref=src, dst_ref=dst, send_sem=s, recv_sem=r, device_id=(row, col), device_id_type=MESH
    )


def contribution_kernel(tab, p_ref, u_hbm, out_hbm, row_ref, col_ref, total, u_ref, block, slots, local, s_chip, s_sib, s_col, r_row, r_col):
    my_row, my_col = lax.axis_index("row"), lax.axis_index("col")
    base, y = my_row // 4 * 4, my_row % 4
    half, cc = my_col // 8 * 8, my_col % 8
    core, pair, parity = cc % 2, cc // 2, cc // 4
    sibling = half + pair * 2 + 1 - core
    y0 = cc % 4
    step = jnp.where(y0 % 2 == 0, 3, 1)
    outer = (y0 + step) % 4
    inner = y0 + 1 - 2 * (y0 % 2)
    last = outer + 1 - 2 * (outer % 2)
    is_source, is_relay = y == y0, y == outer
    fetch = pltpu.make_async_copy(u_hbm, u_ref, local.at[2])
    fetch.start()
    barrier = pltpu.get_barrier_semaphore()

    def greet(row, col):
        pl.semaphore_signal(barrier, inc=1, device_id=(row, col), device_id_type=MESH)

    others = [half + (pair + d) % 4 * 2 + core for d in (2, 1, 3)]
    for col in others:
        greet(my_row, col)
    greet(my_row, sibling)

    @pl.when(jnp.logical_not(is_source))
    def _():
        greet(base + jnp.where(y == last, outer, y0), my_col)

    pl.semaphore_wait(barrier, 4 + jnp.where(is_source, 2, jnp.where(is_relay, 1, 0)))

    order = [cc, pair * 2 + 1 - core] + [(pair + d) % 4 * 2 + core for d in (2, 1, 3)]
    order += [(pair + d) % 4 * 2 + 1 - core for d in (2, 1, 3)]


    def chip_send(i, late):
        col = others[i]
        p = (col % 8 // 4 + late) % 2
        return remote(p_ref.at[:, p], row_ref.at[cc, :, p], s_chip.at[i, late], r_row.at[cc, late], my_row, col)

    def sib_send(e, late):
        p, j = (parity + late) % 2, order[e]
        src = p_ref.at[:, p] if e == 0 else row_ref.at[j, :, p]
        return remote(src, row_ref.at[j, :, p], s_sib.at[max(e - 1, 0), late], r_row.at[j, late], my_row, sibling)

    def row_wait(e, late):
        p, j = (parity + late) % 2, order[e]
        remote(p_ref.at[:, p], row_ref.at[j, :, p], s_sib.at[0, 0], r_row.at[j, late], my_row, sibling).wait_recv()

    def col_send(e, t):
        src = p_ref.at[:, parity] if e == 0 else row_ref.at[order[e], :, parity]
        return remote(src, col_ref.at[order[e]], s_col.at[e, t], r_col.at[order[e]], base + (outer, inner)[t], my_col)

    def pass_on(e):
        j = order[e]
        return remote(col_ref.at[j], col_ref.at[j], s_col.at[e, 0], r_col.at[j], base + last, my_col)

    def relay(*events):
        @pl.when(is_relay)
        def _():
            for e in events:
                pass_on(e).wait_recv()
                pass_on(e).start()

    def product(t):
        pairs = (order[2 * t], order[2 * t + 1])

        @pl.when(is_source)
        def _():
            for i in pairs:
                col_ref[i] = row_ref[i, :, parity]

        @pl.when(jnp.logical_not(is_source | is_relay))
        def _():
            pass_on(2 * t).wait_recv()
            pass_on(2 * t + 1).wait_recv()

        def some(i, _):
            left = [row_ref[f, pl.ds(2 * i, 2)].reshape(4 * B, B) for f in pairs]
            right = [col_ref[f].reshape(8 * B, B) for f in pairs]
            more = lax.dot_general(
                jnp.concatenate(left, axis=1), jnp.concatenate(right, axis=1), (((1,), (1,)), ((), ())),
                preferred_element_type=F32,
            )
            at = pl.ds(4 * i, 4)
            if t == 0:
                update = [jnp.swapaxes(u_ref[4 * i + r], 0, 1) for r in range(4)]
            for m in range(8):
                part = more[:, m * B : (m + 1) * B].reshape(4, B, B)
                if t == 0:
                    for r in range(4):
                        total[m, 4 * i + r] = update[r][m].astype(F32) - part[r]
                elif t < 3:
                    total[m, at] = total[m, at] - part
                else:
                    block[m, at] = (total[m, at] - part).astype(BF)
            return 0

        lax.fori_loop(0, 4, some, 0)

    for late in range(2):
        for i in range(3):
            chip_send(i, late).start()
        sib_send(0, late).start()
        if late == 0:

            @pl.when(is_source)
            def _():
                col_send(0, 0).start()
                col_send(0, 1).start()

    row_ref[cc] = p_ref[...]
    for e in range(1, 8):
        row_wait(e, 0)
        if 2 <= e < 5:
            sib_send(e, 0).start()

        @pl.when(is_source)
        def _():
            col_send(e, 0).start()
            col_send(e, 1).start()

        if e == 1:
            row_wait(1, 1)
            relay(0, 1)
            fetch.wait()
            product(0)
    relay(2, 3, 4)
    for e in (2, 3, 4):
        row_wait(e, 1)
        sib_send(e, 1).start()
    relay(5)
    product(1)
    relay(6, 7)
    for e in (5, 6, 7):
        row_wait(e, 1)
    product(2)
    product(3)

    def emit(owner, slot):
        return pltpu.make_async_copy(slots.at[slot], out_hbm.at[pl.ds(owner * 16, 16)], local.at[slot])

    def lay_out(owner, _):
        slot = owner % 2

        @pl.when(owner >= 2)
        def _():
            emit(owner - 2, slot).wait()

        for s in range(2):
            l = tab[OUT_ROW + owner * 2 + s]
            for c in range(16):
                slots[slot, c, s * B : (s + 1) * B, :] = block[tab[OUT_COL + c], l]
        emit(owner, slot).start()
        return 0

    lax.fori_loop(0, 8, lay_out, 0)
    for slot in range(2):
        emit(6 + slot, slot).wait()
    for late in range(2):
        for i in range(3):
            chip_send(i, late).wait_send()
        for e in (0, 2, 3, 4):
            sib_send(e, late).wait_send()

    @pl.when(is_source)
    def _():
        for e in range(8):
            col_send(e, 0).wait_send()
            col_send(e, 1).wait_send()

    @pl.when(is_relay)
    def _():
        for e in range(8):
            pass_on(e).wait_send()


def contributions(tab, piece, update):
    dma = pltpu.SemaphoreType.DMA
    return pl.pallas_call(
        contribution_kernel,
        out_shape=jax.ShapeDtypeStruct((128, 2 * B, B), BF),
        in_specs=[SM, VM, ANY],
        out_specs=ANY,
        scratch_shapes=[
            pltpu.VMEM((8, 8, 2, B, B), BF),
            pltpu.VMEM((8, 8, B, B), BF),
            pltpu.VMEM((8, 16, B, B), F32),
            pltpu.VMEM((16, B, 8, B), BF),
            pltpu.VMEM((8, 16, B, B), BF),
            pltpu.VMEM((2, 16, 2 * B, B), BF),
            dma((3,)),
            dma((3, 2)),
            dma((4, 2)),
            dma((8, 2)),
            dma((8, 2)),
            dma((8,)),
        ],
        compiler_params=params(56, collective_id=1, has_side_effects=True),
    )(tab, piece, update)


def pivot_kernel(tab, arrived, front, out_ref, block, sem):
    def fits(l, h):
        return tab[AT_RCH + h * 16 + l] == tab[AT_CCH + h * 8]

    def fetch(l, h):
        at = jnp.where(fits(l, h), tab[AT_RSRC + h * 16 + l] + tab[AT_CSRC + h * 8], 0)
        return pltpu.make_async_copy(arrived.at[at], block.at[h, l], sem.at[h, l])

    for l in range(16):
        for h in range(2):
            fetch(l, h).start()
    for l in range(16):
        value = front[l].astype(F32)
        for h in range(2):
            valid = fits(l, h)
            fetch(l, h).wait()
            value = value + jnp.where(valid, block[h, l].astype(F32), 0.0)
        out_ref[l] = value.astype(BF)


def pivot_columns(tab, arrived, front):
    return pl.pallas_call(
        pivot_kernel,
        out_shape=jax.ShapeDtypeStruct((16, B, B), BF),
        in_specs=[SM, ANY, VM],
        out_specs=VM,
        scratch_shapes=[pltpu.VMEM((2, 16, B, B), BF), pltpu.SemaphoreType.DMA((2, 16))],
        compiler_params=params(8),
    )(tab, arrived, front)


class Gather:
    SEMS = (3, 3, 3, 3, 3, 3, 4, 4, 1, 2, 1, 8, 2, 2, 4, 4, 4, 4, 4, 4, 1, 2, 4, 4)

    def __init__(self, piece, sq, portion, cols, sems):
        self.piece, self.sq, self.portion, self.cols = piece, sq, portion, cols
        (self.s_zq, self.s_zp, self.s_y2, self.s_x2, self.s_x3, self.s_y3, self.s_bx, self.s_by) = sems[:8]
        (self.s_px, self.s_ps, self.s_f, self.s_c) = sems[8:12]
        (self.r_zq, self.r_zp, self.r_y2, self.r_x2, self.r_x3, self.r_y3, self.r_bx, self.r_by) = sems[12:20]
        (self.r_px, self.r_ps, self.r_f, self.r_c) = sems[20:]
        row, col = lax.axis_index("row"), lax.axis_index("col")
        self.xl, self.y, self.z, self.xh, self.k = row // 4, row % 4, col // 4, col // 2 % 2, col % 2
        self.x = self.xh * 2 + self.xl
        self.zh, self.zl = self.z // 2, self.z % 2
        self.owner = self.z < 2
        y0 = self.xh * 2 + self.k
        outer = (y0 + jnp.where(y0 % 2 == 0, 3, 1)) % 4
        self.y0, self.outer, self.inner = y0, outer, y0 + 1 - 2 * (y0 % 2)
        self.last_y = outer + 1 - 2 * (outer % 2)
        self.is_source, self.is_relay = self.y == y0, self.y == outer
        self.straight = self.xl == self.zl
        self.groups = [(self.xh, self.k), (self.xh, 1 - self.k), (1 - self.xh, self.k), (1 - self.xh, 1 - self.k)]

    def at(self, xl=None, y=None, z=None, xh=None, k=None):
        pick = lambda new, old: old if new is None else new
        return pick(xl, self.xl) * 4 + pick(y, self.y), pick(z, self.z) * 4 + pick(xh, self.xh) * 2 + pick(k, self.k)

    def xs(self):
        return [((self.x + d) % 4 % 2, (self.x + d) % 4 // 2) for d in (1, 3, 2)]

    def ys(self):
        return [(self.y + d) % 4 for d in (1, 3, 2)]

    def zs(self):
        return [(self.z + d) % 4 for d in (1, 3, 2)]

    def send(self, src, dst, s, r, to):
        return remote(src, dst, s, r, to[0], to[1])

    def arrived(self, ref, sem):
        to = self.at(k=1 - self.k)
        remote(ref, ref, self.s_zq.at[0], sem, to[0], to[1]).wait_recv()

    def enter(self):
        barrier = pltpu.get_barrier_semaphore()

        def greet(to):
            pl.semaphore_signal(barrier, inc=1, device_id=to, device_id_type=MESH)

        for z in self.zs():
            greet(self.at(z=z))
        for y in self.ys():
            greet(self.at(y=y))
        for xl, xh in self.xs():
            greet(self.at(xl=xl, xh=xh))
        greet(self.at(k=1 - self.k))

        @pl.when(self.is_source & jnp.logical_not(self.straight))
        def _():
            for xh, k in self.groups:
                greet(self.at(xl=self.zl, xh=xh, k=k))

        pl.semaphore_wait(barrier, 10 + jnp.where(self.straight, 1, 0))


    def mine(self, zp):
        return self.sq.at[zp, self.xh, self.k, self.xl, self.y]

    def zq_sends(self):
        src = self.piece.at[0, 0]
        return [
            self.send(src, self.mine(self.z), self.s_zq.at[i], self.r_zq.at[self.z], self.at(z=z))
            for i, z in enumerate(self.zs())
        ]

    def zp_sends(self):
        dst = self.portion.at[self.z, self.xh, self.k]
        return [
            self.send(self.piece, dst, self.s_zp.at[i], self.r_zp.at[self.z], self.at(z=z)) for i, z in enumerate(self.zs())
        ]

    def y2_sends(self):
        c = self.mine(0)
        return [self.send(c, c, self.s_y2.at[i], self.r_y2.at[self.y], self.at(y=y)) for i, y in enumerate(self.ys())]

    def x2_sends(self):
        c = self.mine(1)
        return [
            self.send(c, c, self.s_x2.at[i], self.r_x2.at[self.x], self.at(xl=xl, xh=xh))
            for i, (xl, xh) in enumerate(self.xs())
        ]

    def along_y(self, xl, xh, k):
        return self.sq.at[0, xh, k, xl]

    def along_x(self, y, k):
        return self.sq.at[1, :, k, :, y]

    def x3_sends(self):
        c = self.along_y(self.xl, self.xh, self.k)
        return [
            self.send(c, c, self.s_x3.at[i], self.r_x3.at[self.x], self.at(xl=xl, xh=xh))
            for i, (xl, xh) in enumerate(self.xs())
        ]

    def y3_sends(self):
        c = self.along_x(self.y, self.k)
        return [self.send(c, c, self.s_y3.at[i], self.r_y3.at[self.y], self.at(y=y)) for i, y in enumerate(self.ys())]

    def bx_send(self, xl, xh):
        c, x = self.along_y(xl, xh, self.k), xh * 2 + xl
        return self.send(c, c, self.s_bx.at[x], self.r_bx.at[x], self.at(k=1 - self.k))

    def by_send(self, y):
        c = self.along_x(y, self.k)
        return self.send(c, c, self.s_by.at[y], self.r_by.at[y], self.at(k=1 - self.k))

    def square(self):
        @pl.when(self.owner)
        def _():
            for s in self.zq_sends() + self.zp_sends():
                s.start()
            self.sq[self.z, self.xh, self.k, self.xl, self.y] = self.piece[0, 0]
            self.portion[self.z, self.xh, self.k] = self.piece[...]

        for zp, sends in ((0, self.y2_sends), (1, self.x2_sends)):

            @pl.when(self.z != zp)
            def _():
                self.arrived(self.mine(zp), self.r_zq.at[zp])

            for s in sends():
                s.start()
        for y in self.ys():
            self.arrived(self.sq.at[0, self.xh, self.k, self.xl, y], self.r_y2.at[y])
        for s in self.x3_sends():
            s.start()
        self.bx_send(self.xl, self.xh).start()
        for xl, xh in self.xs():
            self.arrived(self.sq.at[1, xh, self.k, xl, self.y], self.r_x2.at[xh * 2 + xl])
        for s in self.y3_sends():
            s.start()
        self.by_send(self.y).start()
        for (xl, xh), y in zip(self.xs(), self.ys()):
            self.arrived(self.along_y(xl, xh, self.k), self.r_x3.at[xh * 2 + xl])
            self.bx_send(xl, xh).start()
            self.arrived(self.along_x(y, self.k), self.r_y3.at[y])
            self.by_send(y).start()
        for i in range(4):
            self.arrived(self.along_y(i % 2, i // 2, 1 - self.k), self.r_bx.at[i])
            self.arrived(self.along_x(i, 1 - self.k), self.r_by.at[i])


    def two(self, xh, k):
        return self.portion.at[:, xh, k]

    def px_send(self):
        c = self.two(self.xh, self.k)
        return self.send(c, c, self.s_px.at[0], self.r_px.at[0], self.at(xh=1 - self.xh))

    def ps_send(self, i):
        c = self.two(self.xh if i == 0 else 1 - self.xh, self.k)
        return self.send(c, c, self.s_ps.at[i], self.r_ps.at[i], self.at(k=1 - self.k))

    def f_send(self):
        src = self.portion.at[:, self.xh, self.k, :, self.zh]
        dst = self.cols.at[:, self.xh, self.k]
        to = self.at(xl=1 - self.xl, xh=self.y // 2, k=self.y % 2)
        return self.send(src, dst, self.s_f.at[0], self.r_f.at[self.xh * 2 + self.k], to)

    def group(self, i):
        xh, k = self.groups[i]
        return self.cols.at[:, xh, k]

    def c_send(self, i, t):
        c = self.group(i)
        return self.send(c, c, self.s_c.at[2 * i + t], self.r_c.at[i], self.at(y=(self.outer, self.inner)[t]))

    def pass_send(self, i):
        c = self.group(i)
        return self.send(c, c, self.s_c.at[2 * i], self.r_c.at[i], self.at(y=self.last_y))

    def spread(self, i):
        @pl.when(self.is_source & self.straight)
        def _():
            xh, k = self.groups[i]
            for zp in range(2):
                self.cols[zp, xh, k] = self.portion[zp, xh, k, :, self.zh]
            self.c_send(i, 0).start()
            self.c_send(i, 1).start()

    def turn(self, i):
        @pl.when(self.is_source & jnp.logical_not(self.straight))
        def _():
            xh, k = self.groups[i]
            self.arrived(self.group(i), self.r_f.at[xh * 2 + k])
            self.c_send(i, 0).start()
            self.c_send(i, 1).start()

    def relay(self, i):
        @pl.when(self.is_relay)
        def _():
            self.arrived(self.group(i), self.r_c.at[i])
            self.pass_send(i).start()

    def begin(self):
        for zp in range(2):

            @pl.when(self.z != zp)
            def _():
                self.arrived(self.portion.at[zp, self.xh, self.k], self.r_zp.at[zp])

        @pl.when(self.straight)
        def _():
            self.f_send().start()

        self.ps_send(0).start()
        self.spread(0)

    def during(self, kb):
        straight, turned = self.straight, jnp.logical_not(self.straight)

        @pl.when(kb == 1)
        def _():
            self.arrived(self.two(self.xh, 1 - self.k), self.r_ps.at[0])
            self.spread(1)

        @pl.when(kb == 2)
        def _():
            self.px_send().start()

        for step, i in ((3, 0), (3, 1), (3, 2), (3, 3)):

            @pl.when(kb == step)
            def _():
                self.turn(i)

        for step, i in ((4, 0), (5, 1), (6, 2), (7, 3)):

            @pl.when((kb == step) & turned)
            def _():
                self.relay(i)

        for step, i in ((2, 0), (3, 1), (7, 2)):

            @pl.when((kb == step) & straight)
            def _():
                self.relay(i)

        @pl.when(kb == 6)
        def _():
            self.arrived(self.two(1 - self.xh, self.k), self.r_px.at[0])
            self.ps_send(1).start()
            self.spread(2)

        @pl.when(kb == 7)
        def _():
            self.arrived(self.two(1 - self.xh, 1 - self.k), self.r_ps.at[1])
            self.spread(3)

    def after(self):
        @pl.when(self.straight)
        def _():
            self.relay(3)

    def end(self):
        @pl.when(jnp.logical_not(self.is_source | self.is_relay))
        def _():
            for i in range(4):
                self.arrived(self.group(i), self.r_c.at[i])

    def finish(self):
        @pl.when(self.owner)
        def _():
            for s in self.zq_sends() + self.zp_sends():
                s.wait_send()

        for s in self.y2_sends() + self.x2_sends() + self.x3_sends() + self.y3_sends():
            s.wait_send()
        for i in range(4):
            self.bx_send(i % 2, i // 2).wait_send()
            self.by_send(i).wait_send()
        self.px_send().wait_send()
        self.ps_send(0).wait_send()
        self.ps_send(1).wait_send()

        @pl.when(self.straight)
        def _():
            self.f_send().wait_send()

        @pl.when(self.is_source)
        def _():
            for i in range(4):
                self.c_send(i, 0).wait_send()
                self.c_send(i, 1).wait_send()

        @pl.when(self.is_relay)
        def _():
            for i in range(4):
                self.pass_send(i).wait_send()


def splits(a, n):
    parts = []
    for i in range(n):
        h = a.astype(BF)
        parts.append(h)
        if i < n - 1:
            a = a - h.astype(F32)
    return parts


LEFT = {2: (0, 0, 1), 3: (0, 0, 1, 1, 0, 2)}
RIGHT = {2: (0, 1, 0), 3: (0, 1, 0, 1, 2, 0)}


def dot_f32(a, b, dims, n=3):
    sa, sb = splits(a, n), splits(b, n)
    left = jnp.concatenate([sa[i] for i in LEFT[n]], axis=dims[0][0])
    right = jnp.concatenate([sb[i] for i in RIGHT[n]], axis=dims[1][0])
    return lax.dot_general(left, right, (dims, ((), ())), preferred_element_type=F32)


def diagonal_factor(square):
    group = 16
    lane = lax.broadcasted_iota(jnp.int32, (8, B), 1)
    sub = lax.broadcasted_iota(jnp.int32, (8, B), 0)
    spread = lambda x, s: jnp.broadcast_to(x[s : s + 1, :], (8, B))
    rest, upper, lower = square, [], []
    for g in range(B // group):
        r0 = group * g
        p = [rest[8 * v : 8 * v + 8, :] for v in range(2)]
        column = [[jnp.broadcast_to(p[v][:, r0 + j : r0 + j + 1], (8, B)) for v in range(2)] for j in range(group)]
        root = [jnp.zeros((8, B), F32) for _ in range(2)]
        for k in range(group):
            at, s = divmod(k, 8)
            r = lax.rsqrt(spread(column[k][at], s))
            root[at] = jnp.where(sub == s, r, root[at])
            if k == group - 1:
                break
            here = lane == r0 + k
            row = jnp.where(here, 1.0, spread(p[at], s))
            for v in range(at, 2):
                if v == at and s == 7:
                    continue
                factor = column[k][v] * (r * r)
                if v == at:
                    factor = jnp.where(sub > s, factor, 0.0)
                    p[v] = jnp.where(here & (sub > s), 0.0, p[v]) - factor * row
                else:
                    p[v] = jnp.where(here, 0.0, p[v]) - factor * row
                for j in range(k + 1, group):
                    column[j][v] = column[j][v] - factor * spread(column[j][at], s)
        panel = jnp.concatenate([p[v] * root[v] for v in range(2)], axis=0)
        roots = jnp.concatenate(root, axis=0)
        ln = lax.broadcasted_iota(jnp.int32, (group, B), 1) - r0
        sb = lax.broadcasted_iota(jnp.int32, (group, B), 0)
        eliminated = jnp.where(ln == sb, roots, jnp.where((ln > sb) & (ln < group), 0.0, panel))
        upper.append(panel)
        lower.append(jnp.where(ln > sb, 0.0, eliminated))
        if g < B // group - 1:
            change = dot_f32(jnp.where(ln >= group, panel, 0.0), eliminated, ((0,), (0,)))
            lt = lax.broadcasted_iota(jnp.int32, (B - r0 - group, B), 1)
            rest = jnp.where((lt >= r0) & (lt < r0 + group), 0.0, rest[group:, :]) - change[r0 + group :, :]
    return jnp.concatenate(upper, axis=0), jnp.concatenate(lower, axis=0)


def factor_start(sq_ref, lower_ref, work):
    for i in range(NB):
        for j in range(NB):
            at = (slice(i * B, (i + 1) * B), slice(j * B, (j + 1) * B))
            if j < i:
                work[at] = jnp.zeros((B, B), F32)
            else:
                block = lambda r, c: sq_ref[c // 4, c // 2 % 2, c % 2, r // 4, r % 4].astype(F32)
                work[at] = 0.5 * (block(i, j) + block(j, i).T)
    lower_ref[...] = jnp.zeros((B, B), F32)


def factor_step(kb, my_row, my_col, inv_ref, lower_ref, work, left, right):
    lane = lax.broadcasted_iota(jnp.int32, (B, B), 1)
    sub = lax.broadcasted_iota(jnp.int32, (B, B), 0)
    d0 = pl.multiple_of(kb * B, B)
    upper, lower = diagonal_factor(work[pl.ds(d0, B), pl.ds(d0, B)])
    work[pl.ds(d0, B), pl.ds(d0, B)] = jnp.where(lane == sub, 1.0, 0.0)
    panel = dot_f32(lower, work[pl.ds(d0, B), :], ((1,), (0,)), 2)
    col = lax.broadcasted_iota(jnp.int32, (B, N), 1)
    inv_ref[pl.ds(d0, B), :] = jnp.where(col < d0 + B, panel, 0.0).astype(BF)

    @pl.when(kb == my_col)
    def _():
        @pl.when(kb == my_row)
        def _():
            lower_ref[...] = jnp.where(lane >= sub, upper, 0.0).T

        @pl.when(kb < my_row)
        def _():
            work[pl.ds(d0, B), :] = panel
            lower_ref[...] = work[pl.ds(d0, B), pl.ds(pl.multiple_of(my_row * B, B), B)].T

    parts = splits(panel, 2)
    for t in range(3):
        left[t * B : (t + 1) * B, :] = parts[LEFT[2][t]]
        right[t * B : (t + 1) * B, :] = parts[RIGHT[2][t]]

    def trailing(i, _):
        i0 = pl.multiple_of(i * B, B)
        work[pl.ds(i0, B), pl.ds(d0, B)] = jnp.zeros((B, B), F32)
        work[pl.ds(i0, B), :] = work[pl.ds(i0, B), :] - lax.dot_general(
            left[:, pl.ds(i0, B)], right[...], (((0,), (0,)), ((), ())), preferred_element_type=F32
        )
        return 0

    lax.fori_loop(kb + 1, NB, trailing, 0)


def below_rows(portion, inv_ref, lower_ref, keep_ref, my_col, below_ref, first_ref, wide, write):
    safe = jnp.minimum(my_col, NB - 1)

    def rows(i, _):
        a = jnp.concatenate(
            [
                jnp.concatenate([portion[k // 4, k // 2 % 2, k % 2, 2 * i + t // 2, t % 2] for k in range(8)], axis=1)
                for t in range(4)
            ],
            axis=0,
        )
        out = lax.dot_general(a, inv_ref[...], (((1,), (1,)), ((), ())), preferred_element_type=F32)
        for t in range(4):
            l = 4 * i + t
            kept = out[t * B : (t + 1) * B, :] * keep_ref[l]
            wide[t * B : (t + 1) * B, :] = kept
            below_ref[pl.ds(pl.multiple_of(l * B, B), B), :] = kept.astype(BF)
        for t in range(4):
            first_ref[4 * i + t] = wide[t * B : (t + 1) * B, pl.ds(pl.multiple_of(safe * B, B), B)]
        write(i).start()
        return 0

    lax.fori_loop(0, 4, rows, 0)
    first_ref[0] = lower_ref[...]


def below_columns(cols, inv_ref, keep_ref, panel_ref, write):
    def some(i, _):
        a = jnp.concatenate(
            [
                jnp.concatenate([cols[k // 4, k // 2 % 2, k % 2, 4 * i + t] for k in range(8)], axis=1)
                for t in range(4)
            ],
            axis=0,
        )
        out = lax.dot_general(a, inv_ref[...], (((1,), (1,)), ((), ())), preferred_element_type=F32)
        for t in range(4):
            m = 4 * i + t
            kept = out[t * B : (t + 1) * B, :] * keep_ref[16 + m]
            panel_ref[pl.ds(pl.multiple_of(m * B, B), B), :] = kept.astype(BF)
        write(i).start()
        return 0

    lax.fori_loop(0, 2, some, 0)


def factor_kernel(piece, keep_ref, below_hbm, panel_hbm, first_hbm, sq, portion, cols, inv_ref, lower_ref, work, left, right, wide, below_ref, panel_ref, first_ref, out_sem, *sems):
    my_row, my_col = lax.axis_index("row"), lax.axis_index("col")

    def write(i):
        rows = pl.ds(4 * B * i, 4 * B)
        return pltpu.make_async_copy(below_ref.at[rows], below_hbm.at[rows], out_sem.at[i])

    def write_first():
        return pltpu.make_async_copy(first_ref, first_hbm, out_sem.at[4])

    def write_panel(i):
        rows = pl.ds(4 * B * i, 4 * B)
        return pltpu.make_async_copy(panel_ref.at[rows], panel_hbm.at[rows], out_sem.at[5 + i])

    gather = Gather(piece, sq, portion, cols, sems)
    gather.enter()
    gather.square()
    gather.begin()
    factor_start(sq, lower_ref, work)

    def step(kb, _):
        gather.during(kb)
        factor_step(kb, my_row, my_col, inv_ref, lower_ref, work, left, right)
        return 0

    lax.fori_loop(0, NB, step, 0)
    gather.after()
    below_rows(portion, inv_ref, lower_ref, keep_ref, my_col, below_ref, first_ref, wide, write)
    write_first().start()
    gather.end()
    below_columns(cols, inv_ref, keep_ref, panel_ref, write_panel)
    gather.finish()
    for i in range(4):
        write(i).wait()
    write_first().wait()
    for i in range(2):
        write_panel(i).wait()


FACTOR_OUT = (
    jax.ShapeDtypeStruct((16 * B, N), BF),
    jax.ShapeDtypeStruct((8 * B, N), BF),
    jax.ShapeDtypeStruct((16, B, B), F32),
)
FACTOR_SCRATCH = (
    ((2, 2, 2, 2, 4, B, B), BF),
    ((2, 2, 2, 8, 2, B, B), BF),
    ((2, 2, 2, 8, B, B), BF),
    ((N, N), BF),
    ((B, B), F32),
    ((N, N), F32),
    ((3 * B, N), BF),
    ((3 * B, N), BF),
    ((4 * B, N), F32),
)


def factor(piece, keep):
    return pl.pallas_call(
        factor_kernel,
        out_shape=FACTOR_OUT,
        in_specs=[VM, SM],
        out_specs=(ANY, ANY, ANY),
        scratch_shapes=[pltpu.VMEM(s, d) for s, d in FACTOR_SCRATCH]
        + [pltpu.VMEM(o.shape, o.dtype) for o in FACTOR_OUT]
        + [pltpu.SemaphoreType.DMA((7,))]
        + [pltpu.SemaphoreType.DMA((n,)) for n in Gather.SEMS],
        compiler_params=params(32, collective_id=2, has_side_effects=True),
    )(piece, keep)


def schur_kernel(tab, front, arrived, below, panel, first, out_ref):
    i = pl.program_id(0)
    my_col = lax.axis_index("col")
    product = lax.dot_general(below[...], panel[...], (((1,), (1,)), ((), ())), preferred_element_type=F32)
    sub = lax.broadcasted_iota(jnp.int32, (B, 8, B), 1)
    taken = (sub == 0) & (my_col < NB)
    for s in range(2):
        l = 2 * i + s
        values = []
        for m in range(8):
            value = -product[s * B : (s + 1) * B, m * B : (m + 1) * B]
            for h in range(2):
                valid = tab[AT_RCH + h * 16 + l] == tab[AT_CCH + h * 8 + m]
                at = jnp.where(valid, tab[AT_RSRC + h * 16 + l] + tab[AT_CSRC + h * 8 + m], 0)
                value = value + jnp.where(valid, arrived[at].astype(F32), 0.0)
            if s == 0:
                value = jnp.where(l == 0, 0.0, value)
            if m == 0:
                value = jnp.where(my_col < NB, first[s], value)
            values.append(value)
        drop = taken | (l == 0) if s == 0 else taken
        out_ref[s] = jnp.swapaxes(jnp.stack(values), 0, 1) + jnp.where(drop, 0.0, front[s].astype(F32))


def schur(tab, front, arrived, below, panel, first):
    full = lambda shape: pl.BlockSpec(shape, lambda i, t: (0,) * len(shape))
    return pl.pallas_call(
        schur_kernel,
        out_shape=jax.ShapeDtypeStruct((16, B, 8, B), F32),
        grid_spec=pltpu.PrefetchScalarGridSpec(
            num_scalar_prefetch=1,
            grid=(8,),
            in_specs=[
                pl.BlockSpec((2, B, 8, B), lambda i, t: (i, 0, 0, 0)),
                full((256, B, B)),
                pl.BlockSpec((2 * B, N), lambda i, t: (i, 0)),
                full((N, N)),
                pl.BlockSpec((2, B, B), lambda i, t: (i, 0, 0)),
            ],
            out_specs=pl.BlockSpec((2, B, 8, B), lambda i, t: (i, 0, 0, 0)),
        ),
        compiler_params=params(28),
    )(tab, front, arrived, below, panel, first)


def per_device(child_update_blocks, child_pivot_panel, child_map, coupled, parent_front):
    my_row, my_col = lax.axis_index("row"), lax.axis_index("col")
    front = parent_front.reshape(16, B, 8, B)
    out_tab = table(outgoing_kernel, 32, child_map)
    outgoing = contributions(out_tab, child_pivot_panel.reshape(8, 2, B, B), child_update_blocks.reshape(16, B, 8, B))
    incoming = lax.all_to_all(outgoing, ("row", "col"), split_axis=0, concat_axis=0, tiled=True)
    arrived = incoming.reshape(256, B, B)
    later_map, later_coupled, _ = lax.optimization_barrier((child_map, coupled, outgoing))
    in_tab = table(incoming_kernel, 96, later_map)
    kept = jnp.concatenate([jnp.ones((NB,), F32), later_coupled.astype(F32)])
    keep = jnp.concatenate(
        [
            lax.dynamic_index_in_dim(kept.reshape(16, 8), my_row, 1, keepdims=False),
            lax.dynamic_index_in_dim(kept.reshape(8, 16), my_col, 1, keepdims=False),
        ]
    )
    pivots = pivot_columns(in_tab, arrived, front[:, :, 0, :])
    below, panel, first = factor(pivots.reshape(8, 2, B, B), keep)
    out = schur(in_tab, front, arrived, below, panel, first)
    return out.reshape(1, 16, B, 1, 8, B)


def solution(mesh):
    in_specs = (
        P("row", None, None, "col", None, None),
        P("row", None, None, "col", None),
        P(),
        P(),
        P("row", None, None, "col", None, None),
    )
    out_specs = P("row", None, None, "col", None, None)
    return jax.shard_map(per_device, mesh=mesh, in_specs=in_specs, out_specs=out_specs, check_vma=False)
```

```python
import functools

import jax
import jax.numpy as jnp
from jax import lax
from jax.experimental import pallas as pl
from jax.experimental.pallas import tpu as pltpu
from jax.sharding import PartitionSpec as P

B = 128
NB = 8
N = NB * B
F32 = jnp.float32
BF = jnp.bfloat16
MESH = pl.DeviceIdType.MESH
ANY = pl.BlockSpec(memory_space=pl.ANY)
VM = pl.BlockSpec(memory_space=pltpu.VMEM)
SM = pl.BlockSpec(memory_space=pltpu.SMEM)
MIB = 1024 * 1024


def params(mib, **kw):
    return pltpu.CompilerParams(vmem_limit_bytes=mib * MIB, **kw)


AT_RSRC, AT_RCH, AT_CSRC, AT_CCH = 0, 32, 64, 80


def incoming_kernel(map_ref, tab_ref, count):
    my_row, my_col = lax.axis_index("row"), lax.axis_index("col")
    for i in range(16):
        count[i] = 0

    def arrive(q, _):
        h, g = q // 2, q % 2

        def one(b, _):
            target = map_ref[q, b]

            @pl.when(target % 8 == my_row)
            def _():
                slot = q * 4 + b % 4
                at = h * 16 + target // 8
                tab_ref[AT_RSRC + at] = (h * 4 + b % 4) * 32 + count[slot]
                tab_ref[AT_RCH + at] = g
                count[slot] = count[slot] + 1

            @pl.when(target % 16 == my_col)
            def _():
                at = h * 8 + target // 16
                tab_ref[AT_CSRC + at] = (g * 8 + b % 8) * 2
                tab_ref[AT_CCH + at] = g

            return 0

        lax.fori_loop(0, 64, one, 0)
        return 0

    lax.fori_loop(0, 4, arrive, 0)


def table(kernel, size, child_map):
    return pl.pallas_call(
        kernel,
        out_shape=jax.ShapeDtypeStruct((size,), jnp.int32),
        in_specs=[SM],
        out_specs=SM,
        scratch_shapes=[pltpu.SMEM((16,), jnp.int32)],
        cost_estimate=pl.CostEstimate(flops=20000, bytes_accessed=2048, transcendentals=0),
    )(child_map)


def remote(src, dst, s, r, row, col):
    return pltpu.make_async_remote_copy(
        src_ref=src, dst_ref=dst, send_sem=s, recv_sem=r, device_id=(row, col), device_id_type=MESH
    )


def contribution_kernel(map_ref, p_ref, u_hbm, out_hbm, row_ref, col_ref, total, u_ref, block, slots, goes, local, s_chip, s_sib, s_col, r_row, r_col):
    my_row, my_col = lax.axis_index("row"), lax.axis_index("col")
    base, y = my_row // 4 * 4, my_row % 4
    half, cc = my_col // 8 * 8, my_col % 8
    core, pair, parity = cc % 2, cc // 2, cc // 4
    sibling = half + pair * 2 + 1 - core
    y0 = cc % 4
    step = jnp.where(y0 % 2 == 0, 3, 1)
    outer = (y0 + step) % 4
    inner = y0 + 1 - 2 * (y0 % 2)
    last = outer + 1 - 2 * (outer % 2)
    is_source, is_relay = y == y0, y == outer
    fetch = pltpu.make_async_copy(u_hbm, u_ref, local.at[2])
    fetch.start()
    barrier = pltpu.get_barrier_semaphore()

    def greet(row, col):
        pl.semaphore_signal(barrier, inc=1, device_id=(row, col), device_id_type=MESH)

    others = [half + (pair + d) % 4 * 2 + core for d in (2, 1, 3)]
    for col in others:
        greet(my_row, col)
    greet(my_row, sibling)

    @pl.when(jnp.logical_not(is_source))
    def _():
        greet(base + jnp.where(y == last, outer, y0), my_col)

    pl.semaphore_wait(barrier, 4 + jnp.where(is_source, 2, jnp.where(is_relay, 1, 0)))

    order = [cc, pair * 2 + 1 - core] + [(pair + d) % 4 * 2 + core for d in (2, 1, 3)]
    order += [(pair + d) % 4 * 2 + 1 - core for d in (2, 1, 3)]


    def chip_send(i, late):
        col = others[i]
        p = (col % 8 // 4 + late) % 2
        return remote(p_ref.at[:, p], row_ref.at[cc, :, p], s_chip.at[i, late], r_row.at[cc, late], my_row, col)

    def sib_send(e, late):
        p, j = (parity + late) % 2, order[e]
        src = p_ref.at[:, p] if e == 0 else row_ref.at[j, :, p]
        return remote(src, row_ref.at[j, :, p], s_sib.at[max(e - 1, 0), late], r_row.at[j, late], my_row, sibling)

    def row_wait(e, late):
        p, j = (parity + late) % 2, order[e]
        remote(p_ref.at[:, p], row_ref.at[j, :, p], s_sib.at[0, 0], r_row.at[j, late], my_row, sibling).wait_recv()

    def col_send(e, t):
        src = p_ref.at[:, parity] if e == 0 else row_ref.at[order[e], :, parity]
        return remote(src, col_ref.at[order[e]], s_col.at[e, t], r_col.at[order[e]], base + (outer, inner)[t], my_col)

    def pass_on(e):
        j = order[e]
        return remote(col_ref.at[j], col_ref.at[j], s_col.at[e, 0], r_col.at[j], base + last, my_col)

    def relay(*events):
        @pl.when(is_relay)
        def _():
            for e in events:
                pass_on(e).wait_recv()
                pass_on(e).start()

    def product(t):
        pairs = (order[2 * t], order[2 * t + 1])

        @pl.when(is_source)
        def _():
            for i in pairs:
                col_ref[i] = row_ref[i, :, parity]

        @pl.when(jnp.logical_not(is_source | is_relay))
        def _():
            pass_on(2 * t).wait_recv()
            pass_on(2 * t + 1).wait_recv()

        def some(i, _):
            left = [row_ref[f, pl.ds(2 * i, 2)].reshape(4 * B, B) for f in pairs]
            right = [col_ref[f].reshape(8 * B, B) for f in pairs]
            more = lax.dot_general(
                jnp.concatenate(left, axis=1), jnp.concatenate(right, axis=1), (((1,), (1,)), ((), ())),
                preferred_element_type=F32,
            )
            at = pl.ds(4 * i, 4)
            if t == 0:
                update = [jnp.swapaxes(u_ref[4 * i + r], 0, 1) for r in range(4)]
            for m in range(8):
                part = more[:, m * B : (m + 1) * B].reshape(4, B, B)
                if t == 0:
                    for r in range(4):
                        total[m, 4 * i + r] = update[r][m].astype(F32) - part[r]
                elif t < 3:
                    total[m, at] = total[m, at] - part
                else:
                    block[m, at] = (total[m, at] - part).astype(BF)
            return 0

        lax.fori_loop(0, 4, some, 0)

    for late in range(2):
        for i in range(3):
            chip_send(i, late).start()
        sib_send(0, late).start()
        if late == 0:

            @pl.when(is_source)
            def _():
                col_send(0, 0).start()
                col_send(0, 1).start()

    row_ref[cc] = p_ref[...]
    child = 2 * (my_row // 4) + my_col // 8
    targets = [map_ref[child, m * 8 + cc] % 16 for m in range(8)]
    for c in range(16):
        at = 0
        for m in range(1, 8):
            at = jnp.where(targets[m] == c, m, at)
        goes[c] = at
    for e in range(1, 8):
        row_wait(e, 0)
        if 2 <= e < 5:
            sib_send(e, 0).start()

        @pl.when(is_source)
        def _():
            col_send(e, 0).start()
            col_send(e, 1).start()

        if e == 1:
            row_wait(1, 1)
            relay(0, 1)
            fetch.wait()
            product(0)
    relay(2, 3, 4)
    for e in (2, 3, 4):
        row_wait(e, 1)
        sib_send(e, 1).start()
    relay(5)
    product(1)
    relay(6, 7)
    for e in (5, 6, 7):
        row_wait(e, 1)
    product(2)
    product(3)

    def emit(owner, slot):
        return pltpu.make_async_copy(slots.at[slot], out_hbm.at[pl.ds(owner * 16, 16)], local.at[slot])

    def lay_out(owner, _):
        slot = owner % 2

        @pl.when(owner >= 2)
        def _():
            emit(owner - 2, slot).wait()

        pair = [0, 0]
        for l in range(15, -1, -1):
            here = map_ref[child, l * 4 + y] % 8 == owner
            pair = [jnp.where(here, l, pair[0]), jnp.where(here, pair[0], pair[1])]
        for s, l in enumerate(pair):
            for c in range(16):
                slots[slot, c, s * B : (s + 1) * B, :] = block[goes[c], l]
        emit(owner, slot).start()
        return 0

    lax.fori_loop(0, 8, lay_out, 0)
    for slot in range(2):
        emit(6 + slot, slot).wait()
    for late in range(2):
        for i in range(3):
            chip_send(i, late).wait_send()
        for e in (0, 2, 3, 4):
            sib_send(e, late).wait_send()

    @pl.when(is_source)
    def _():
        for e in range(8):
            col_send(e, 0).wait_send()
            col_send(e, 1).wait_send()

    @pl.when(is_relay)
    def _():
        for e in range(8):
            pass_on(e).wait_send()


def contributions(child_map, piece, update):
    dma = pltpu.SemaphoreType.DMA
    return pl.pallas_call(
        contribution_kernel,
        out_shape=jax.ShapeDtypeStruct((128, 2 * B, B), BF),
        in_specs=[SM, VM, ANY],
        out_specs=ANY,
        scratch_shapes=[
            pltpu.VMEM((8, 8, 2, B, B), BF),
            pltpu.VMEM((8, 8, B, B), BF),
            pltpu.VMEM((8, 16, B, B), F32),
            pltpu.VMEM((16, B, 8, B), BF),
            pltpu.VMEM((8, 16, B, B), BF),
            pltpu.VMEM((2, 16, 2 * B, B), BF),
            pltpu.SMEM((16,), jnp.int32),
            dma((3,)),
            dma((3, 2)),
            dma((4, 2)),
            dma((8, 2)),
            dma((8, 2)),
            dma((8,)),
        ],
        compiler_params=params(56, collective_id=1, has_side_effects=True),
    )(child_map, piece, update)


def pivot_kernel(tab, arrived, front, out_ref, block, sem):
    def fits(l, h):
        return tab[AT_RCH + h * 16 + l] == tab[AT_CCH + h * 8]

    def fetch(l, h):
        at = jnp.where(fits(l, h), tab[AT_RSRC + h * 16 + l] + tab[AT_CSRC + h * 8], 0)
        return pltpu.make_async_copy(arrived.at[at], block.at[h, l], sem.at[h, l])

    for l in range(16):
        for h in range(2):
            fetch(l, h).start()
    for l in range(16):
        value = front[l].astype(F32)
        for h in range(2):
            valid = fits(l, h)
            fetch(l, h).wait()
            value = value + jnp.where(valid, block[h, l].astype(F32), 0.0)
        out_ref[l] = value.astype(BF)


def pivot_columns(tab, arrived, front):
    return pl.pallas_call(
        pivot_kernel,
        out_shape=jax.ShapeDtypeStruct((16, B, B), BF),
        in_specs=[SM, ANY, VM],
        out_specs=VM,
        scratch_shapes=[pltpu.VMEM((2, 16, B, B), BF), pltpu.SemaphoreType.DMA((2, 16))],
        compiler_params=params(8),
    )(tab, arrived, front)


class Gather:
    SEMS = (3, 3, 3, 3, 3, 3, 4, 4, 1, 2, 1, 8, 2, 2, 4, 4, 4, 4, 4, 4, 1, 2, 4, 4)

    def __init__(self, piece, sq, portion, cols, sems):
        self.piece, self.sq, self.portion, self.cols = piece, sq, portion, cols
        (self.s_zq, self.s_zp, self.s_y2, self.s_x2, self.s_x3, self.s_y3, self.s_bx, self.s_by) = sems[:8]
        (self.s_px, self.s_ps, self.s_f, self.s_c) = sems[8:12]
        (self.r_zq, self.r_zp, self.r_y2, self.r_x2, self.r_x3, self.r_y3, self.r_bx, self.r_by) = sems[12:20]
        (self.r_px, self.r_ps, self.r_f, self.r_c) = sems[20:]
        row, col = lax.axis_index("row"), lax.axis_index("col")
        self.xl, self.y, self.z, self.xh, self.k = row // 4, row % 4, col // 4, col // 2 % 2, col % 2
        self.x = self.xh * 2 + self.xl
        self.zh, self.zl = self.z // 2, self.z % 2
        self.owner = self.z < 2
        y0 = self.xh * 2 + self.k
        outer = (y0 + jnp.where(y0 % 2 == 0, 3, 1)) % 4
        self.y0, self.outer, self.inner = y0, outer, y0 + 1 - 2 * (y0 % 2)
        self.last_y = outer + 1 - 2 * (outer % 2)
        self.is_source, self.is_relay = self.y == y0, self.y == outer
        self.straight = self.xl == self.zl
        self.groups = [(self.xh, self.k), (self.xh, 1 - self.k), (1 - self.xh, self.k), (1 - self.xh, 1 - self.k)]

    def at(self, xl=None, y=None, z=None, xh=None, k=None):
        pick = lambda new, old: old if new is None else new
        return pick(xl, self.xl) * 4 + pick(y, self.y), pick(z, self.z) * 4 + pick(xh, self.xh) * 2 + pick(k, self.k)

    def xs(self):
        return [((self.x + d) % 4 % 2, (self.x + d) % 4 // 2) for d in (1, 3, 2)]

    def ys(self):
        return [(self.y + d) % 4 for d in (1, 3, 2)]

    def zs(self):
        return [(self.z + d) % 4 for d in (1, 3, 2)]

    def send(self, src, dst, s, r, to):
        return remote(src, dst, s, r, to[0], to[1])

    def arrived(self, ref, sem):
        to = self.at(k=1 - self.k)
        remote(ref, ref, self.s_zq.at[0], sem, to[0], to[1]).wait_recv()

    def enter(self):
        barrier = pltpu.get_barrier_semaphore()

        def greet(to):
            pl.semaphore_signal(barrier, inc=1, device_id=to, device_id_type=MESH)

        for z in self.zs():
            greet(self.at(z=z))
        for y in self.ys():
            greet(self.at(y=y))
        for xl, xh in self.xs():
            greet(self.at(xl=xl, xh=xh))
        greet(self.at(k=1 - self.k))

        @pl.when(self.is_source & jnp.logical_not(self.straight))
        def _():
            for xh, k in self.groups:
                greet(self.at(xl=self.zl, xh=xh, k=k))

        pl.semaphore_wait(barrier, 10 + jnp.where(self.straight, 1, 0))


    def mine(self, zp):
        return self.sq.at[zp, self.xh, self.k, self.xl, self.y]

    def zq_sends(self):
        src = self.piece.at[0, 0]
        return [
            self.send(src, self.mine(self.z), self.s_zq.at[i], self.r_zq.at[self.z], self.at(z=z))
            for i, z in enumerate(self.zs())
        ]

    def zp_sends(self):
        dst = self.portion.at[self.z, self.xh, self.k]
        return [
            self.send(self.piece, dst, self.s_zp.at[i], self.r_zp.at[self.z], self.at(z=z)) for i, z in enumerate(self.zs())
        ]

    def y2_sends(self):
        c = self.mine(0)
        return [self.send(c, c, self.s_y2.at[i], self.r_y2.at[self.y], self.at(y=y)) for i, y in enumerate(self.ys())]

    def x2_sends(self):
        c = self.mine(1)
        return [
            self.send(c, c, self.s_x2.at[i], self.r_x2.at[self.x], self.at(xl=xl, xh=xh))
            for i, (xl, xh) in enumerate(self.xs())
        ]

    def along_y(self, xl, xh, k):
        return self.sq.at[0, xh, k, xl]

    def along_x(self, y, k):
        return self.sq.at[1, :, k, :, y]

    def x3_sends(self):
        c = self.along_y(self.xl, self.xh, self.k)
        return [
            self.send(c, c, self.s_x3.at[i], self.r_x3.at[self.x], self.at(xl=xl, xh=xh))
            for i, (xl, xh) in enumerate(self.xs())
        ]

    def y3_sends(self):
        c = self.along_x(self.y, self.k)
        return [self.send(c, c, self.s_y3.at[i], self.r_y3.at[self.y], self.at(y=y)) for i, y in enumerate(self.ys())]

    def bx_send(self, xl, xh):
        c, x = self.along_y(xl, xh, self.k), xh * 2 + xl
        return self.send(c, c, self.s_bx.at[x], self.r_bx.at[x], self.at(k=1 - self.k))

    def by_send(self, y):
        c = self.along_x(y, self.k)
        return self.send(c, c, self.s_by.at[y], self.r_by.at[y], self.at(k=1 - self.k))

    def square(self):
        @pl.when(self.owner)
        def _():
            for s in self.zq_sends() + self.zp_sends():
                s.start()
            self.sq[self.z, self.xh, self.k, self.xl, self.y] = self.piece[0, 0]
            self.portion[self.z, self.xh, self.k] = self.piece[...]

        for zp, sends in ((0, self.y2_sends), (1, self.x2_sends)):

            @pl.when(self.z != zp)
            def _():
                self.arrived(self.mine(zp), self.r_zq.at[zp])

            for s in sends():
                s.start()
        for y in self.ys():
            self.arrived(self.sq.at[0, self.xh, self.k, self.xl, y], self.r_y2.at[y])
        for s in self.x3_sends():
            s.start()
        self.bx_send(self.xl, self.xh).start()
        for xl, xh in self.xs():
            self.arrived(self.sq.at[1, xh, self.k, xl, self.y], self.r_x2.at[xh * 2 + xl])
        for s in self.y3_sends():
            s.start()
        self.by_send(self.y).start()
        for (xl, xh), y in zip(self.xs(), self.ys()):
            self.arrived(self.along_y(xl, xh, self.k), self.r_x3.at[xh * 2 + xl])
            self.bx_send(xl, xh).start()
            self.arrived(self.along_x(y, self.k), self.r_y3.at[y])
            self.by_send(y).start()
        for i in range(4):
            self.arrived(self.along_y(i % 2, i // 2, 1 - self.k), self.r_bx.at[i])
            self.arrived(self.along_x(i, 1 - self.k), self.r_by.at[i])


    def two(self, xh, k):
        return self.portion.at[:, xh, k]

    def px_send(self):
        c = self.two(self.xh, self.k)
        return self.send(c, c, self.s_px.at[0], self.r_px.at[0], self.at(xh=1 - self.xh))

    def ps_send(self, i):
        c = self.two(self.xh if i == 0 else 1 - self.xh, self.k)
        return self.send(c, c, self.s_ps.at[i], self.r_ps.at[i], self.at(k=1 - self.k))

    def f_send(self):
        src = self.portion.at[:, self.xh, self.k, :, self.zh]
        dst = self.cols.at[:, self.xh, self.k]
        to = self.at(xl=1 - self.xl, xh=self.y // 2, k=self.y % 2)
        return self.send(src, dst, self.s_f.at[0], self.r_f.at[self.xh * 2 + self.k], to)

    def group(self, i):
        xh, k = self.groups[i]
        return self.cols.at[:, xh, k]

    def c_send(self, i, t):
        c = self.group(i)
        return self.send(c, c, self.s_c.at[2 * i + t], self.r_c.at[i], self.at(y=(self.outer, self.inner)[t]))

    def pass_send(self, i):
        c = self.group(i)
        return self.send(c, c, self.s_c.at[2 * i], self.r_c.at[i], self.at(y=self.last_y))

    def spread(self, i):
        @pl.when(self.is_source & self.straight)
        def _():
            xh, k = self.groups[i]
            for zp in range(2):
                self.cols[zp, xh, k] = self.portion[zp, xh, k, :, self.zh]
            self.c_send(i, 0).start()
            self.c_send(i, 1).start()

    def turn(self, i):
        @pl.when(self.is_source & jnp.logical_not(self.straight))
        def _():
            xh, k = self.groups[i]
            self.arrived(self.group(i), self.r_f.at[xh * 2 + k])
            self.c_send(i, 0).start()
            self.c_send(i, 1).start()

    def relay(self, i):
        @pl.when(self.is_relay)
        def _():
            self.arrived(self.group(i), self.r_c.at[i])
            self.pass_send(i).start()

    def begin(self):
        for zp in range(2):

            @pl.when(self.z != zp)
            def _():
                self.arrived(self.portion.at[zp, self.xh, self.k], self.r_zp.at[zp])

        @pl.when(self.straight)
        def _():
            self.f_send().start()

        self.ps_send(0).start()
        self.spread(0)

    def during(self, kb):
        straight, turned = self.straight, jnp.logical_not(self.straight)

        @pl.when(kb == 1)
        def _():
            self.arrived(self.two(self.xh, 1 - self.k), self.r_ps.at[0])
            self.spread(1)

        @pl.when(kb == 2)
        def _():
            self.px_send().start()

        for step, i in ((4, 0), (4, 1), (4, 2), (4, 3)):

            @pl.when(kb == step)
            def _():
                self.turn(i)

        for step, i in ((5, 0), (6, 1), (7, 2)):

            @pl.when((kb == step) & turned)
            def _():
                self.relay(i)

        for step, i in ((2, 0), (3, 1), (7, 2)):

            @pl.when((kb == step) & straight)
            def _():
                self.relay(i)

        @pl.when(kb == 6)
        def _():
            self.arrived(self.two(1 - self.xh, self.k), self.r_px.at[0])
            self.ps_send(1).start()
            self.spread(2)

        @pl.when(kb == 7)
        def _():
            self.arrived(self.two(1 - self.xh, 1 - self.k), self.r_ps.at[1])
            self.spread(3)

    def after(self):
        self.relay(3)

    def end(self):
        @pl.when(jnp.logical_not(self.is_source | self.is_relay))
        def _():
            for i in range(4):
                self.arrived(self.group(i), self.r_c.at[i])

    def finish(self):
        @pl.when(self.owner)
        def _():
            for s in self.zq_sends() + self.zp_sends():
                s.wait_send()

        for s in self.y2_sends() + self.x2_sends() + self.x3_sends() + self.y3_sends():
            s.wait_send()
        for i in range(4):
            self.bx_send(i % 2, i // 2).wait_send()
            self.by_send(i).wait_send()
        self.px_send().wait_send()
        self.ps_send(0).wait_send()
        self.ps_send(1).wait_send()

        @pl.when(self.straight)
        def _():
            self.f_send().wait_send()

        @pl.when(self.is_source)
        def _():
            for i in range(4):
                self.c_send(i, 0).wait_send()
                self.c_send(i, 1).wait_send()

        @pl.when(self.is_relay)
        def _():
            for i in range(4):
                self.pass_send(i).wait_send()


def splits(a, n):
    parts = []
    for i in range(n):
        h = a.astype(BF)
        parts.append(h)
        if i < n - 1:
            a = a - h.astype(F32)
    return parts


LEFT = {2: (0, 0, 1), 3: (0, 0, 1, 1, 0, 2)}
RIGHT = {2: (0, 1, 0), 3: (0, 1, 0, 1, 2, 0)}


def dot_f32(a, b, dims, n=3):
    sa, sb = splits(a, n), splits(b, n)
    left = jnp.concatenate([sa[i] for i in LEFT[n]], axis=dims[0][0])
    right = jnp.concatenate([sb[i] for i in RIGHT[n]], axis=dims[1][0])
    return lax.dot_general(left, right, (dims, ((), ())), preferred_element_type=F32)


POS = 3


def diagonal_factor(square, beside):
    group = 16
    lane = lax.broadcasted_iota(jnp.int32, (8, B), 1)
    sub = lax.broadcasted_iota(jnp.int32, (8, B), 0)
    spread = lambda x, s: jnp.broadcast_to(x[s : s + 1, :], (8, B))
    rest, upper, lower = square, [], []
    for g in range(B // group):
        r0 = group * g
        p = [rest[8 * v : 8 * v + 8, :] for v in range(2)]
        column = [[jnp.broadcast_to(p[v][:, r0 + j : r0 + j + 1], (8, B)) for v in range(2)] for j in range(group)]
        root = [jnp.zeros((8, B), F32) for _ in range(2)]
        for k in range(group):
            if k % 8 == POS and beside:
                beside.pop(0)()
            at, s = divmod(k, 8)
            r = lax.rsqrt(spread(column[k][at], s))
            root[at] = jnp.where(sub == s, r, root[at])
            if k == group - 1:
                break
            here = lane == r0 + k
            row = jnp.where(here, 1.0, spread(p[at], s))
            for v in range(at, 2):
                if v == at and s == 7:
                    continue
                factor = column[k][v] * (r * r)
                if v == at:
                    factor = jnp.where(sub > s, factor, 0.0)
                    p[v] = jnp.where(here & (sub > s), 0.0, p[v]) - factor * row
                else:
                    p[v] = jnp.where(here, 0.0, p[v]) - factor * row
                for j in range(k + 1, group):
                    column[j][v] = column[j][v] - factor * spread(column[j][at], s)
        panel = jnp.concatenate([p[v] * root[v] for v in range(2)], axis=0)
        roots = jnp.concatenate(root, axis=0)
        ln = lax.broadcasted_iota(jnp.int32, (group, B), 1) - r0
        sb = lax.broadcasted_iota(jnp.int32, (group, B), 0)
        eliminated = jnp.where(ln == sb, roots, jnp.where((ln > sb) & (ln < group), 0.0, panel))
        upper.append(panel)
        lower.append(jnp.where(ln > sb, 0.0, eliminated))
        if g < B // group - 1:
            change = dot_f32(jnp.where(ln >= group, panel, 0.0), eliminated, ((0,), (0,)))
            lt = lax.broadcasted_iota(jnp.int32, (B - r0 - group, B), 1)
            rest = jnp.where((lt >= r0) & (lt < r0 + group), 0.0, rest[group:, :]) - change[r0 + group :, :]
    return jnp.concatenate(upper, axis=0), jnp.concatenate(lower, axis=0)


def factor_start(sq_ref, lower_ref, work, left, right):
    for i in range(NB):
        for j in range(NB):
            at = (slice(i * B, (i + 1) * B), slice(j * B, (j + 1) * B))
            if j < i:
                work[at] = jnp.zeros((B, B), F32)
            else:
                block = lambda r, c: sq_ref[c // 4, c // 2 % 2, c % 2, r // 4, r % 4].astype(F32)
                work[at] = 0.5 * (block(i, j) + block(j, i).T)
    lower_ref[...] = jnp.zeros((B, B), F32)
    left[...] = jnp.zeros_like(left)
    right[...] = jnp.zeros_like(right)


def trailing(i, k0, work, left, right, half=None):
    cols = slice(0, N) if half is None else slice(half * N // 2, (half + 1) * N // 2)
    i0 = pl.multiple_of(jnp.minimum(i, NB) * B, B)
    part = left[:, pl.ds(pl.multiple_of(jnp.minimum(i, NB - 1) * B, B), B)]
    if not half:
        work[pl.ds(i0, B), pl.ds(k0, B)] = jnp.zeros((B, B), F32)
    work[pl.ds(i0, B), cols] = work[pl.ds(i0, B), cols] - lax.dot_general(
        part, right[:, cols], (((0,), (0,)), ((), ())), preferred_element_type=F32
    )


def factor_step(kb, my_row, my_col, inv_ref, lower_ref, work, left, right):
    lane = lax.broadcasted_iota(jnp.int32, (B, B), 1)
    sub = lax.broadcasted_iota(jnp.int32, (B, B), 0)
    d0 = pl.multiple_of(kb * B, B)
    before = pl.multiple_of(jnp.maximum(kb - 1, 0) * B, B)
    beside = [
        functools.partial(trailing, kb + t, before, work, left, right, half) for t in range(1, NB - 1) for half in range(2)
    ]
    upper, lower = diagonal_factor(work[pl.ds(d0, B), pl.ds(d0, B)], beside)
    for piece in beside:
        piece()
    work[pl.ds(d0, B), pl.ds(d0, B)] = jnp.where(lane == sub, 1.0, 0.0)
    panel = dot_f32(lower, work[pl.ds(d0, B), :], ((1,), (0,)), 2)
    col = lax.broadcasted_iota(jnp.int32, (B, N), 1)
    inv_ref[pl.ds(d0, B), :] = jnp.where(col < d0 + B, panel, 0.0).astype(BF)
    parts = splits(panel, 2)
    for t in range(3):
        left[t * B : (t + 1) * B, :] = parts[LEFT[2][t]]
        right[t * B : (t + 1) * B, :] = parts[RIGHT[2][t]]
    trailing(kb + 1, d0, work, left, right)

    @pl.when(kb == my_col)
    def _():
        @pl.when(kb == my_row)
        def _():
            lower_ref[...] = jnp.where(lane >= sub, upper, 0.0).T

        @pl.when(kb < my_row)
        def _():
            work[pl.ds(d0, B), :] = panel
            lower_ref[...] = work[pl.ds(d0, B), pl.ds(pl.multiple_of(my_row * B, B), B)].T


def below_tiles(a, inv_ref):
    tiles = []
    for c in range(0, N, 2 * B):
        end = c + 2 * B
        tiles.append(
            lax.dot_general(
                a[:, :end], inv_ref[c:end, :end], (((1,), (1,)), ((), ())), preferred_element_type=F32
            )
        )
    return tiles


def below_rows(portion, inv_ref, lower_ref, keep_ref, my_col, below_ref, first_ref, wide, write):
    safe = jnp.minimum(my_col, NB - 1)

    def rows(i, _):
        a = jnp.concatenate(
            [
                jnp.concatenate([portion[k // 4, k // 2 % 2, k % 2, 2 * i + t // 2, t % 2] for k in range(8)], axis=1)
                for t in range(4)
            ],
            axis=0,
        )
        for c, out in enumerate(below_tiles(a, inv_ref)):
            cols = slice(2 * B * c, 2 * B * (c + 1))
            for t in range(4):
                l = 4 * i + t
                kept = out[t * B : (t + 1) * B, :] * keep_ref[l]
                wide[t * B : (t + 1) * B, cols] = kept
                below_ref[pl.ds(pl.multiple_of(l * B, B), B), cols] = kept.astype(BF)
        for t in range(4):
            first_ref[4 * i + t] = wide[t * B : (t + 1) * B, pl.ds(pl.multiple_of(safe * B, B), B)]
        write(i).start()
        return 0

    lax.fori_loop(0, 4, rows, 0)
    first_ref[0] = lower_ref[...]


def below_columns(cols, inv_ref, keep_ref, panel_ref, write):
    def some(i, _):
        a = jnp.concatenate(
            [
                jnp.concatenate([cols[k // 4, k // 2 % 2, k % 2, 4 * i + t] for k in range(8)], axis=1)
                for t in range(4)
            ],
            axis=0,
        )
        for c, out in enumerate(below_tiles(a, inv_ref)):
            for t in range(4):
                m = 4 * i + t
                kept = out[t * B : (t + 1) * B, :] * keep_ref[16 + m]
                panel_ref[pl.ds(pl.multiple_of(m * B, B), B), 2 * B * c : 2 * B * (c + 1)] = kept.astype(BF)
        write(i).start()
        return 0

    lax.fori_loop(0, 2, some, 0)


def factor_kernel(piece, keep_ref, below_hbm, panel_hbm, first_hbm, sq, portion, cols, inv_ref, lower_ref, work, left, right, wide, below_ref, panel_ref, first_ref, out_sem, *sems):
    my_row, my_col = lax.axis_index("row"), lax.axis_index("col")

    def write(i):
        rows = pl.ds(4 * B * i, 4 * B)
        return pltpu.make_async_copy(below_ref.at[rows], below_hbm.at[rows], out_sem.at[i])

    def write_first():
        return pltpu.make_async_copy(first_ref, first_hbm, out_sem.at[4])

    def write_panel(i):
        rows = pl.ds(4 * B * i, 4 * B)
        return pltpu.make_async_copy(panel_ref.at[rows], panel_hbm.at[rows], out_sem.at[5 + i])

    gather = Gather(piece, sq, portion, cols, sems)
    gather.enter()
    gather.square()
    gather.begin()
    factor_start(sq, lower_ref, work, left, right)

    def step(kb, _):
        gather.during(kb)
        factor_step(kb, my_row, my_col, inv_ref, lower_ref, work, left, right)
        return 0

    lax.fori_loop(0, NB, step, 0)
    gather.after()
    below_rows(portion, inv_ref, lower_ref, keep_ref, my_col, below_ref, first_ref, wide, write)
    write_first().start()
    gather.end()
    below_columns(cols, inv_ref, keep_ref, panel_ref, write_panel)
    gather.finish()
    for i in range(4):
        write(i).wait()
    write_first().wait()
    for i in range(2):
        write_panel(i).wait()


FACTOR_OUT = (
    jax.ShapeDtypeStruct((16 * B, N), BF),
    jax.ShapeDtypeStruct((8 * B, N), BF),
    jax.ShapeDtypeStruct((16, B, B), F32),
)
FACTOR_SCRATCH = (
    ((2, 2, 2, 2, 4, B, B), BF),
    ((2, 2, 2, 8, 2, B, B), BF),
    ((2, 2, 2, 8, B, B), BF),
    ((N, N), BF),
    ((B, B), F32),
    ((N + B, N), F32),
    ((3 * B, N), BF),
    ((3 * B, N), BF),
    ((4 * B, N), F32),
)


def factor(piece, keep):
    return pl.pallas_call(
        factor_kernel,
        out_shape=FACTOR_OUT,
        in_specs=[VM, SM],
        out_specs=(ANY, ANY, ANY),
        scratch_shapes=[pltpu.VMEM(s, d) for s, d in FACTOR_SCRATCH]
        + [pltpu.VMEM(o.shape, o.dtype) for o in FACTOR_OUT]
        + [pltpu.SemaphoreType.DMA((7,))]
        + [pltpu.SemaphoreType.DMA((n,)) for n in Gather.SEMS],
        compiler_params=params(32, collective_id=2, has_side_effects=True),
    )(piece, keep)


def schur_kernel(tab, front, arrived, below, panel, first, out_ref):
    i = pl.program_id(0)
    my_col = lax.axis_index("col")
    product = lax.dot_general(below[...], panel[...], (((1,), (1,)), ((), ())), preferred_element_type=F32)
    sub = lax.broadcasted_iota(jnp.int32, (B, 8, B), 1)
    taken = (sub == 0) & (my_col < NB)
    for s in range(2):
        l = 2 * i + s
        values = []
        for m in range(8):
            value = -product[s * B : (s + 1) * B, m * B : (m + 1) * B]
            for h in range(2):
                valid = tab[AT_RCH + h * 16 + l] == tab[AT_CCH + h * 8 + m]
                at = jnp.where(valid, tab[AT_RSRC + h * 16 + l] + tab[AT_CSRC + h * 8 + m], 0)
                value = value + jnp.where(valid, arrived[at].astype(F32), 0.0)
            if s == 0:
                value = jnp.where(l == 0, 0.0, value)
            if m == 0:
                value = jnp.where(my_col < NB, first[s], value)
            values.append(value)
        drop = taken | (l == 0) if s == 0 else taken
        out_ref[s] = jnp.swapaxes(jnp.stack(values), 0, 1) + jnp.where(drop, 0.0, front[s].astype(F32))


def schur(tab, front, arrived, below, panel, first):
    full = lambda shape: pl.BlockSpec(shape, lambda i, t: (0,) * len(shape))
    return pl.pallas_call(
        schur_kernel,
        out_shape=jax.ShapeDtypeStruct((16, B, 8, B), F32),
        grid_spec=pltpu.PrefetchScalarGridSpec(
            num_scalar_prefetch=1,
            grid=(8,),
            in_specs=[
                pl.BlockSpec((2, B, 8, B), lambda i, t: (i, 0, 0, 0)),
                full((256, B, B)),
                pl.BlockSpec((2 * B, N), lambda i, t: (i, 0)),
                full((N, N)),
                pl.BlockSpec((2, B, B), lambda i, t: (i, 0, 0)),
            ],
            out_specs=pl.BlockSpec((2, B, 8, B), lambda i, t: (i, 0, 0, 0)),
        ),
        compiler_params=params(28),
    )(tab, front, arrived, below, panel, first)


def per_device(child_update_blocks, child_pivot_panel, child_map, coupled, parent_front):
    my_row, my_col = lax.axis_index("row"), lax.axis_index("col")
    front = parent_front.reshape(16, B, 8, B)
    outgoing = contributions(child_map, child_pivot_panel.reshape(8, 2, B, B), child_update_blocks.reshape(16, B, 8, B))
    incoming = lax.all_to_all(outgoing, ("row", "col"), split_axis=0, concat_axis=0, tiled=True)
    arrived = incoming.reshape(256, B, B)
    later_map, later_coupled, _ = lax.optimization_barrier((child_map, coupled, outgoing))
    in_tab = table(incoming_kernel, 96, later_map)
    kept = jnp.concatenate([jnp.ones((NB,), F32), later_coupled.astype(F32)])
    keep = jnp.concatenate(
        [
            lax.dynamic_index_in_dim(kept.reshape(16, 8), my_row, 1, keepdims=False),
            lax.dynamic_index_in_dim(kept.reshape(8, 16), my_col, 1, keepdims=False),
        ]
    )
    pivots = pivot_columns(in_tab, arrived, front[:, :, 0, :])
    below, panel, first = factor(pivots.reshape(8, 2, B, B), keep)
    out = schur(in_tab, front, arrived, below, panel, first)
    return out.reshape(1, 16, B, 1, 8, B)


def solution(mesh):
    in_specs = (
        P("row", None, None, "col", None, None),
        P("row", None, None, "col", None),
        P(),
        P(),
        P("row", None, None, "col", None, None),
    )
    out_specs = P("row", None, None, "col", None, None)
    return jax.shard_map(per_device, mesh=mesh, in_specs=in_specs, out_specs=out_specs, check_vma=False)
```

```python
import functools

import jax
import jax.numpy as jnp
from jax import lax
from jax.experimental import pallas as pl
from jax.experimental.pallas import tpu as pltpu
from jax.sharding import PartitionSpec as P

B = 128
NB = 8
N = NB * B
F32 = jnp.float32
BF = jnp.bfloat16
MESH = pl.DeviceIdType.MESH
ANY = pl.BlockSpec(memory_space=pl.ANY)
VM = pl.BlockSpec(memory_space=pltpu.VMEM)
SM = pl.BlockSpec(memory_space=pltpu.SMEM)
MIB = 1024 * 1024


def params(mib, **kw):
    return pltpu.CompilerParams(vmem_limit_bytes=mib * MIB, **kw)


AT_RSRC, AT_RCH, AT_CSRC, AT_CCH = 0, 32, 64, 80


def incoming_kernel(map_ref, tab_ref, count):
    my_row, my_col = lax.axis_index("row"), lax.axis_index("col")
    for i in range(16):
        count[i] = 0

    def arrive(q, _):
        h, g = q // 2, q % 2

        def one(b, _):
            target = map_ref[q, b]

            @pl.when(target % 8 == my_row)
            def _():
                slot = q * 4 + b % 4
                at = h * 16 + target // 8
                tab_ref[AT_RSRC + at] = (h * 4 + b % 4) * 32 + count[slot]
                tab_ref[AT_RCH + at] = g
                count[slot] = count[slot] + 1

            @pl.when(target % 16 == my_col)
            def _():
                at = h * 8 + target // 16
                tab_ref[AT_CSRC + at] = (g * 8 + b % 8) * 2
                tab_ref[AT_CCH + at] = g

            return 0

        lax.fori_loop(0, 64, one, 0)
        return 0

    lax.fori_loop(0, 4, arrive, 0)


def table(kernel, size, child_map):
    return pl.pallas_call(
        kernel,
        out_shape=jax.ShapeDtypeStruct((size,), jnp.int32),
        in_specs=[SM],
        out_specs=SM,
        scratch_shapes=[pltpu.SMEM((16,), jnp.int32)],
        cost_estimate=pl.CostEstimate(flops=20000, bytes_accessed=2048, transcendentals=0),
    )(child_map)


def remote(src, dst, s, r, row, col):
    return pltpu.make_async_remote_copy(
        src_ref=src, dst_ref=dst, send_sem=s, recv_sem=r, device_id=(row, col), device_id_type=MESH
    )


def contribution_kernel(map_ref, p_ref, u_hbm, out_hbm, row_ref, col_ref, total, u_ref, block, slots, goes, local, s_chip, s_sib, s_col, r_row, r_col):
    my_row, my_col = lax.axis_index("row"), lax.axis_index("col")
    base, y = my_row // 4 * 4, my_row % 4
    half, cc = my_col // 8 * 8, my_col % 8
    core, pair, parity = cc % 2, cc // 2, cc // 4
    sibling = half + pair * 2 + 1 - core
    y0 = cc % 4
    step = jnp.where(y0 % 2 == 0, 3, 1)
    outer = (y0 + step) % 4
    inner = y0 + 1 - 2 * (y0 % 2)
    last = outer + 1 - 2 * (outer % 2)
    is_source, is_relay = y == y0, y == outer
    fetch = pltpu.make_async_copy(u_hbm, u_ref, local.at[2])
    fetch.start()
    barrier = pltpu.get_barrier_semaphore()

    def greet(row, col):
        pl.semaphore_signal(barrier, inc=1, device_id=(row, col), device_id_type=MESH)

    others = [half + (pair + d) % 4 * 2 + core for d in (2, 1, 3)]
    for col in others:
        greet(my_row, col)
    greet(my_row, sibling)

    @pl.when(jnp.logical_not(is_source))
    def _():
        greet(base + jnp.where(y == last, outer, y0), my_col)

    pl.semaphore_wait(barrier, 4 + jnp.where(is_source, 2, jnp.where(is_relay, 1, 0)))

    order = [cc, pair * 2 + 1 - core] + [(pair + d) % 4 * 2 + core for d in (2, 1, 3)]
    order += [(pair + d) % 4 * 2 + 1 - core for d in (2, 1, 3)]


    def chip_send(i, late):
        col = others[i]
        p = (col % 8 // 4 + late) % 2
        return remote(p_ref.at[:, p], row_ref.at[cc, :, p], s_chip.at[i, late], r_row.at[cc, late], my_row, col)

    def sib_send(e, late):
        p, j = (parity + late) % 2, order[e]
        src = p_ref.at[:, p] if e == 0 else row_ref.at[j, :, p]
        return remote(src, row_ref.at[j, :, p], s_sib.at[max(e - 1, 0), late], r_row.at[j, late], my_row, sibling)

    def row_wait(e, late):
        p, j = (parity + late) % 2, order[e]
        remote(p_ref.at[:, p], row_ref.at[j, :, p], s_sib.at[0, 0], r_row.at[j, late], my_row, sibling).wait_recv()

    def col_send(e, t):
        src = p_ref.at[:, parity] if e == 0 else row_ref.at[order[e], :, parity]
        return remote(src, col_ref.at[order[e]], s_col.at[e, t], r_col.at[order[e]], base + (outer, inner)[t], my_col)

    def pass_on(e):
        j = order[e]
        return remote(col_ref.at[j], col_ref.at[j], s_col.at[e, 0], r_col.at[j], base + last, my_col)

    def relay(*events):
        @pl.when(is_relay)
        def _():
            for e in events:
                pass_on(e).wait_recv()
                pass_on(e).start()

    def product(t):
        pairs = (order[2 * t], order[2 * t + 1])

        @pl.when(is_source)
        def _():
            for i in pairs:
                col_ref[i] = row_ref[i, :, parity]

        @pl.when(jnp.logical_not(is_source | is_relay))
        def _():
            pass_on(2 * t).wait_recv()
            pass_on(2 * t + 1).wait_recv()

        def some(i, _):
            left = [row_ref[f, pl.ds(2 * i, 2)].reshape(4 * B, B) for f in pairs]
            right = [col_ref[f].reshape(8 * B, B) for f in pairs]
            more = lax.dot_general(
                jnp.concatenate(left, axis=1), jnp.concatenate(right, axis=1), (((1,), (1,)), ((), ())),
                preferred_element_type=F32,
            )
            at = pl.ds(4 * i, 4)
            if t == 0:
                update = [jnp.swapaxes(u_ref[4 * i + r], 0, 1) for r in range(4)]
            for m in range(8):
                part = more[:, m * B : (m + 1) * B].reshape(4, B, B)
                if t == 0:
                    for r in range(4):
                        total[m, 4 * i + r] = update[r][m].astype(F32) - part[r]
                elif t < 3:
                    total[m, at] = total[m, at] - part
                else:
                    block[m, at] = (total[m, at] - part).astype(BF)
            return 0

        lax.fori_loop(0, 4, some, 0)

    for late in range(2):
        for i in range(3):
            chip_send(i, late).start()
        sib_send(0, late).start()
        if late == 0:

            @pl.when(is_source)
            def _():
                col_send(0, 0).start()
                col_send(0, 1).start()

    row_ref[cc] = p_ref[...]
    child = 2 * (my_row // 4) + my_col // 8
    targets = [map_ref[child, m * 8 + cc] % 16 for m in range(8)]
    for c in range(16):
        at = 0
        for m in range(1, 8):
            at = jnp.where(targets[m] == c, m, at)
        goes[c] = at
    for e in range(1, 8):
        row_wait(e, 0)
        if 2 <= e < 5:
            sib_send(e, 0).start()

        @pl.when(is_source)
        def _():
            col_send(e, 0).start()
            col_send(e, 1).start()

        if e == 1:
            row_wait(1, 1)
            relay(0, 1)
            fetch.wait()
            product(0)
    relay(2, 3, 4)
    for e in (2, 3, 4):
        row_wait(e, 1)
        sib_send(e, 1).start()
    relay(5)
    product(1)
    relay(6, 7)
    for e in (5, 6, 7):
        row_wait(e, 1)
    product(2)
    product(3)

    def emit(owner, slot):
        return pltpu.make_async_copy(slots.at[slot], out_hbm.at[pl.ds(owner * 16, 16)], local.at[slot])

    def lay_out(owner, _):
        slot = owner % 2

        @pl.when(owner >= 2)
        def _():
            emit(owner - 2, slot).wait()

        pair = [0, 0]
        for l in range(15, -1, -1):
            here = map_ref[child, l * 4 + y] % 8 == owner
            pair = [jnp.where(here, l, pair[0]), jnp.where(here, pair[0], pair[1])]
        for s, l in enumerate(pair):
            for c in range(16):
                slots[slot, c, s * B : (s + 1) * B, :] = block[goes[c], l]
        emit(owner, slot).start()
        return 0

    lax.fori_loop(0, 8, lay_out, 0)
    for slot in range(2):
        emit(6 + slot, slot).wait()
    for late in range(2):
        for i in range(3):
            chip_send(i, late).wait_send()
        for e in (0, 2, 3, 4):
            sib_send(e, late).wait_send()

    @pl.when(is_source)
    def _():
        for e in range(8):
            col_send(e, 0).wait_send()
            col_send(e, 1).wait_send()

    @pl.when(is_relay)
    def _():
        for e in range(8):
            pass_on(e).wait_send()


def contributions(child_map, piece, update):
    dma = pltpu.SemaphoreType.DMA
    return pl.pallas_call(
        contribution_kernel,
        out_shape=jax.ShapeDtypeStruct((128, 2 * B, B), BF),
        in_specs=[SM, VM, ANY],
        out_specs=ANY,
        scratch_shapes=[
            pltpu.VMEM((8, 8, 2, B, B), BF),
            pltpu.VMEM((8, 8, B, B), BF),
            pltpu.VMEM((8, 16, B, B), F32),
            pltpu.VMEM((16, B, 8, B), BF),
            pltpu.VMEM((8, 16, B, B), BF),
            pltpu.VMEM((2, 16, 2 * B, B), BF),
            pltpu.SMEM((16,), jnp.int32),
            dma((3,)),
            dma((3, 2)),
            dma((4, 2)),
            dma((8, 2)),
            dma((8, 2)),
            dma((8,)),
        ],
        compiler_params=params(56, collective_id=1, has_side_effects=True),
    )(child_map, piece, update)


def pivot_kernel(tab, arrived, front, out_ref, block, sem):
    def fits(l, h):
        return tab[AT_RCH + h * 16 + l] == tab[AT_CCH + h * 8]

    def fetch(l, h):
        at = jnp.where(fits(l, h), tab[AT_RSRC + h * 16 + l] + tab[AT_CSRC + h * 8], 0)
        return pltpu.make_async_copy(arrived.at[at], block.at[h, l], sem.at[h, l])

    for l in range(16):
        for h in range(2):
            fetch(l, h).start()
    for l in range(16):
        value = front[l].astype(F32)
        for h in range(2):
            valid = fits(l, h)
            fetch(l, h).wait()
            value = value + jnp.where(valid, block[h, l].astype(F32), 0.0)
        out_ref[l] = value.astype(BF)


def pivot_columns(tab, arrived, front):
    return pl.pallas_call(
        pivot_kernel,
        out_shape=jax.ShapeDtypeStruct((16, B, B), BF),
        in_specs=[SM, ANY, VM],
        out_specs=VM,
        scratch_shapes=[pltpu.VMEM((2, 16, B, B), BF), pltpu.SemaphoreType.DMA((2, 16))],
        compiler_params=params(8),
    )(tab, arrived, front)


class Gather:
    SEMS = (3, 3, 3, 3, 3, 3, 4, 4, 1, 2, 1, 8, 2, 2, 4, 4, 4, 4, 4, 4, 1, 2, 4, 4)

    def __init__(self, piece, sq, portion, cols, sems):
        self.piece, self.sq, self.portion, self.cols = piece, sq, portion, cols
        (self.s_zq, self.s_zp, self.s_y2, self.s_x2, self.s_x3, self.s_y3, self.s_bx, self.s_by) = sems[:8]
        (self.s_px, self.s_ps, self.s_f, self.s_c) = sems[8:12]
        (self.r_zq, self.r_zp, self.r_y2, self.r_x2, self.r_x3, self.r_y3, self.r_bx, self.r_by) = sems[12:20]
        (self.r_px, self.r_ps, self.r_f, self.r_c) = sems[20:]
        row, col = lax.axis_index("row"), lax.axis_index("col")
        self.xl, self.y, self.z, self.xh, self.k = row // 4, row % 4, col // 4, col // 2 % 2, col % 2
        self.x = self.xh * 2 + self.xl
        self.zh, self.zl = self.z // 2, self.z % 2
        self.owner = self.z < 2
        y0 = self.xh * 2 + self.k
        outer = (y0 + jnp.where(y0 % 2 == 0, 3, 1)) % 4
        self.y0, self.outer, self.inner = y0, outer, y0 + 1 - 2 * (y0 % 2)
        self.last_y = outer + 1 - 2 * (outer % 2)
        self.is_source, self.is_relay = self.y == y0, self.y == outer
        self.straight = self.xl == self.zl
        self.groups = [(self.xh, self.k), (self.xh, 1 - self.k), (1 - self.xh, self.k), (1 - self.xh, 1 - self.k)]

    def at(self, xl=None, y=None, z=None, xh=None, k=None):
        pick = lambda new, old: old if new is None else new
        return pick(xl, self.xl) * 4 + pick(y, self.y), pick(z, self.z) * 4 + pick(xh, self.xh) * 2 + pick(k, self.k)

    def xs(self):
        return [((self.x + d) % 4 % 2, (self.x + d) % 4 // 2) for d in (1, 3, 2)]

    def ys(self):
        return [(self.y + d) % 4 for d in (1, 3, 2)]

    def zs(self):
        return [(self.z + d) % 4 for d in (1, 3, 2)]

    def send(self, src, dst, s, r, to):
        return remote(src, dst, s, r, to[0], to[1])

    def arrived(self, ref, sem):
        to = self.at(k=1 - self.k)
        remote(ref, ref, self.s_zq.at[0], sem, to[0], to[1]).wait_recv()

    def enter(self):
        barrier = pltpu.get_barrier_semaphore()

        def greet(to):
            pl.semaphore_signal(barrier, inc=1, device_id=to, device_id_type=MESH)

        for z in self.zs():
            greet(self.at(z=z))
        for y in self.ys():
            greet(self.at(y=y))
        for xl, xh in self.xs():
            greet(self.at(xl=xl, xh=xh))
        greet(self.at(k=1 - self.k))

        @pl.when(self.is_source & jnp.logical_not(self.straight))
        def _():
            for xh, k in self.groups:
                greet(self.at(xl=self.zl, xh=xh, k=k))

        pl.semaphore_wait(barrier, 10 + jnp.where(self.straight, 1, 0))


    def mine(self, zp):
        return self.sq.at[zp, self.xh, self.k, self.xl, self.y]

    def zq_sends(self):
        src = self.piece.at[0, 0]
        return [
            self.send(src, self.mine(self.z), self.s_zq.at[i], self.r_zq.at[self.z], self.at(z=z))
            for i, z in enumerate(self.zs())
        ]

    def zp_sends(self):
        dst = self.portion.at[self.z, self.xh, self.k]
        return [
            self.send(self.piece, dst, self.s_zp.at[i], self.r_zp.at[self.z], self.at(z=z)) for i, z in enumerate(self.zs())
        ]

    def y2_sends(self):
        c = self.mine(0)
        return [self.send(c, c, self.s_y2.at[i], self.r_y2.at[self.y], self.at(y=y)) for i, y in enumerate(self.ys())]

    def x2_sends(self):
        c = self.mine(1)
        return [
            self.send(c, c, self.s_x2.at[i], self.r_x2.at[self.x], self.at(xl=xl, xh=xh))
            for i, (xl, xh) in enumerate(self.xs())
        ]

    def along_y(self, xl, xh, k):
        return self.sq.at[0, xh, k, xl]

    def along_x(self, y, k):
        return self.sq.at[1, :, k, :, y]

    def x3_sends(self):
        c = self.along_y(self.xl, self.xh, self.k)
        return [
            self.send(c, c, self.s_x3.at[i], self.r_x3.at[self.x], self.at(xl=xl, xh=xh))
            for i, (xl, xh) in enumerate(self.xs())
        ]

    def y3_sends(self):
        c = self.along_x(self.y, self.k)
        return [self.send(c, c, self.s_y3.at[i], self.r_y3.at[self.y], self.at(y=y)) for i, y in enumerate(self.ys())]

    def bx_send(self, xl, xh):
        c, x = self.along_y(xl, xh, self.k), xh * 2 + xl
        return self.send(c, c, self.s_bx.at[x], self.r_bx.at[x], self.at(k=1 - self.k))

    def by_send(self, y):
        c = self.along_x(y, self.k)
        return self.send(c, c, self.s_by.at[y], self.r_by.at[y], self.at(k=1 - self.k))

    def square(self):
        @pl.when(self.owner)
        def _():
            for s in self.zq_sends() + self.zp_sends():
                s.start()
            self.sq[self.z, self.xh, self.k, self.xl, self.y] = self.piece[0, 0]
            self.portion[self.z, self.xh, self.k] = self.piece[...]

        for zp, sends in ((0, self.y2_sends), (1, self.x2_sends)):

            @pl.when(self.z != zp)
            def _():
                self.arrived(self.mine(zp), self.r_zq.at[zp])

            for s in sends():
                s.start()
        for y in self.ys():
            self.arrived(self.sq.at[0, self.xh, self.k, self.xl, y], self.r_y2.at[y])
        for s in self.x3_sends():
            s.start()
        self.bx_send(self.xl, self.xh).start()
        for xl, xh in self.xs():
            self.arrived(self.sq.at[1, xh, self.k, xl, self.y], self.r_x2.at[xh * 2 + xl])
        for s in self.y3_sends():
            s.start()
        self.by_send(self.y).start()
        for (xl, xh), y in zip(self.xs(), self.ys()):
            self.arrived(self.along_y(xl, xh, self.k), self.r_x3.at[xh * 2 + xl])
            self.bx_send(xl, xh).start()
            self.arrived(self.along_x(y, self.k), self.r_y3.at[y])
            self.by_send(y).start()
        self.early()
        for i in range(4):
            self.arrived(self.along_y(i % 2, i // 2, 1 - self.k), self.r_bx.at[i])
            self.arrived(self.along_x(i, 1 - self.k), self.r_by.at[i])


    def two(self, xh, k):
        return self.portion.at[:, xh, k]

    def px_send(self):
        c = self.two(self.xh, self.k)
        return self.send(c, c, self.s_px.at[0], self.r_px.at[0], self.at(xh=1 - self.xh))

    def ps_send(self, i):
        c = self.two(self.xh if i == 0 else 1 - self.xh, self.k)
        return self.send(c, c, self.s_ps.at[i], self.r_ps.at[i], self.at(k=1 - self.k))

    def f_send(self):
        src = self.portion.at[:, self.xh, self.k, :, self.zh]
        dst = self.cols.at[:, self.xh, self.k]
        to = self.at(xl=1 - self.xl, xh=self.y // 2, k=self.y % 2)
        return self.send(src, dst, self.s_f.at[0], self.r_f.at[self.xh * 2 + self.k], to)

    def group(self, i):
        xh, k = self.groups[i]
        return self.cols.at[:, xh, k]

    def c_send(self, i, t):
        c = self.group(i)
        return self.send(c, c, self.s_c.at[2 * i + t], self.r_c.at[i], self.at(y=(self.outer, self.inner)[t]))

    def pass_send(self, i):
        c = self.group(i)
        return self.send(c, c, self.s_c.at[2 * i], self.r_c.at[i], self.at(y=self.last_y))

    def spread(self, i):
        @pl.when(self.is_source & self.straight)
        def _():
            xh, k = self.groups[i]
            for zp in range(2):
                self.cols[zp, xh, k] = self.portion[zp, xh, k, :, self.zh]
            self.c_send(i, 0).start()
            self.c_send(i, 1).start()

    def turn(self, i):
        @pl.when(self.is_source & jnp.logical_not(self.straight))
        def _():
            xh, k = self.groups[i]
            self.arrived(self.group(i), self.r_f.at[xh * 2 + k])
            self.c_send(i, 0).start()
            self.c_send(i, 1).start()

    def relay(self, i):
        @pl.when(self.is_relay)
        def _():
            self.arrived(self.group(i), self.r_c.at[i])
            self.pass_send(i).start()

    def early(self):
        for zp in range(2):

            @pl.when(self.z != zp)
            def _():
                self.arrived(self.portion.at[zp, self.xh, self.k], self.r_zp.at[zp])

        @pl.when(self.straight)
        def _():
            self.f_send().start()

    def begin(self):
        self.ps_send(0).start()
        self.spread(0)

    def during(self, kb):
        straight, turned = self.straight, jnp.logical_not(self.straight)

        @pl.when(kb == 1)
        def _():
            self.px_send().start()
            self.arrived(self.two(self.xh, 1 - self.k), self.r_ps.at[0])
            self.spread(1)

        for step, i in ((4, 0), (4, 1), (4, 2), (4, 3)):

            @pl.when(kb == step)
            def _():
                self.turn(i)

        for step, i in ((5, 0), (6, 1), (7, 2)):

            @pl.when((kb == step) & turned)
            def _():
                self.relay(i)

        for step, i in ((2, 0), (3, 1), (7, 2)):

            @pl.when((kb == step) & straight)
            def _():
                self.relay(i)

        @pl.when(kb == 6)
        def _():
            self.arrived(self.two(1 - self.xh, self.k), self.r_px.at[0])
            self.ps_send(1).start()
            self.spread(2)

        @pl.when(kb == 7)
        def _():
            self.arrived(self.two(1 - self.xh, 1 - self.k), self.r_ps.at[1])
            self.spread(3)

    def after(self):
        self.relay(3)

    def end(self):
        @pl.when(jnp.logical_not(self.is_source | self.is_relay))
        def _():
            for i in range(4):
                self.arrived(self.group(i), self.r_c.at[i])

    def finish(self):
        @pl.when(self.owner)
        def _():
            for s in self.zq_sends() + self.zp_sends():
                s.wait_send()

        for s in self.y2_sends() + self.x2_sends() + self.x3_sends() + self.y3_sends():
            s.wait_send()
        for i in range(4):
            self.bx_send(i % 2, i // 2).wait_send()
            self.by_send(i).wait_send()
        self.px_send().wait_send()
        self.ps_send(0).wait_send()
        self.ps_send(1).wait_send()

        @pl.when(self.straight)
        def _():
            self.f_send().wait_send()

        @pl.when(self.is_source)
        def _():
            for i in range(4):
                self.c_send(i, 0).wait_send()
                self.c_send(i, 1).wait_send()

        @pl.when(self.is_relay)
        def _():
            for i in range(4):
                self.pass_send(i).wait_send()


def splits(a, n):
    parts = []
    for i in range(n):
        h = a.astype(BF)
        parts.append(h)
        if i < n - 1:
            a = a - h.astype(F32)
    return parts


LEFT = {2: (0, 0, 1), 3: (0, 0, 1, 1, 0, 2)}
RIGHT = {2: (0, 1, 0), 3: (0, 1, 0, 1, 2, 0)}


def dot_f32(a, b, dims, n=3):
    sa, sb = splits(a, n), splits(b, n)
    left = jnp.concatenate([sa[i] for i in LEFT[n]], axis=dims[0][0])
    right = jnp.concatenate([sb[i] for i in RIGHT[n]], axis=dims[1][0])
    return lax.dot_general(left, right, (dims, ((), ())), preferred_element_type=F32)


POS = 3


def diagonal_factor(square, beside):
    group = 16
    lane = lax.broadcasted_iota(jnp.int32, (8, B), 1)
    sub = lax.broadcasted_iota(jnp.int32, (8, B), 0)
    spread = lambda x, s: jnp.broadcast_to(x[s : s + 1, :], (8, B))
    rest, upper, lower = square, [], []
    for g in range(B // group):
        r0 = group * g
        p = [rest[8 * v : 8 * v + 8, :] for v in range(2)]
        column = [[jnp.broadcast_to(p[v][:, r0 + j : r0 + j + 1], (8, B)) for v in range(2)] for j in range(group)]
        root = [jnp.zeros((8, B), F32) for _ in range(2)]
        for k in range(group):
            if k % 8 == POS and beside:
                beside.pop(0)()
            at, s = divmod(k, 8)
            r = lax.rsqrt(spread(column[k][at], s))
            root[at] = jnp.where(sub == s, r, root[at])
            if k == group - 1:
                break
            here = lane == r0 + k
            row = jnp.where(here, 1.0, spread(p[at], s))
            for v in range(at, 2):
                if v == at and s == 7:
                    continue
                factor = column[k][v] * (r * r)
                if v == at:
                    factor = jnp.where(sub > s, factor, 0.0)
                    p[v] = jnp.where(here & (sub > s), 0.0, p[v]) - factor * row
                else:
                    p[v] = jnp.where(here, 0.0, p[v]) - factor * row
                for j in range(k + 1, group):
                    column[j][v] = column[j][v] - factor * spread(column[j][at], s)
        panel = jnp.concatenate([p[v] * root[v] for v in range(2)], axis=0)
        roots = jnp.concatenate(root, axis=0)
        ln = lax.broadcasted_iota(jnp.int32, (group, B), 1) - r0
        sb = lax.broadcasted_iota(jnp.int32, (group, B), 0)
        eliminated = jnp.where(ln == sb, roots, jnp.where((ln > sb) & (ln < group), 0.0, panel))
        upper.append(panel)
        lower.append(jnp.where(ln > sb, 0.0, eliminated))
        if g < B // group - 1:
            change = dot_f32(jnp.where(ln >= group, panel, 0.0), eliminated, ((0,), (0,)))
            lt = lax.broadcasted_iota(jnp.int32, (B - r0 - group, B), 1)
            rest = jnp.where((lt >= r0) & (lt < r0 + group), 0.0, rest[group:, :]) - change[r0 + group :, :]
    return jnp.concatenate(upper, axis=0), jnp.concatenate(lower, axis=0)


def factor_start(sq_ref, lower_ref, work, left, right):
    for i in range(NB):
        for j in range(NB):
            at = (slice(i * B, (i + 1) * B), slice(j * B, (j + 1) * B))
            if j < i:
                work[at] = jnp.zeros((B, B), F32)
            else:
                block = lambda r, c: sq_ref[c // 4, c // 2 % 2, c % 2, r // 4, r % 4].astype(F32)
                work[at] = 0.5 * (block(i, j) + block(j, i).T)
    lower_ref[...] = jnp.zeros((B, B), F32)
    left[...] = jnp.zeros_like(left)
    right[...] = jnp.zeros_like(right)


def trailing(i, k0, work, left, right, half=None):
    cols = slice(0, N) if half is None else slice(half * N // 2, (half + 1) * N // 2)
    i0 = pl.multiple_of(jnp.minimum(i, NB) * B, B)
    part = left[:, pl.ds(pl.multiple_of(jnp.minimum(i, NB - 1) * B, B), B)]
    if not half:
        work[pl.ds(i0, B), pl.ds(k0, B)] = jnp.zeros((B, B), F32)
    work[pl.ds(i0, B), cols] = work[pl.ds(i0, B), cols] - lax.dot_general(
        part, right[:, cols], (((0,), (0,)), ((), ())), preferred_element_type=F32
    )


def factor_step(kb, my_row, my_col, inv_ref, lower_ref, work, left, right):
    lane = lax.broadcasted_iota(jnp.int32, (B, B), 1)
    sub = lax.broadcasted_iota(jnp.int32, (B, B), 0)
    d0 = pl.multiple_of(kb * B, B)
    before = pl.multiple_of(jnp.maximum(kb - 1, 0) * B, B)
    beside = [
        functools.partial(trailing, kb + t, before, work, left, right, half) for t in range(1, NB - 1) for half in range(2)
    ]
    upper, lower = diagonal_factor(work[pl.ds(d0, B), pl.ds(d0, B)], beside)
    for piece in beside:
        piece()
    work[pl.ds(d0, B), pl.ds(d0, B)] = jnp.where(lane == sub, 1.0, 0.0)
    panel = dot_f32(lower, work[pl.ds(d0, B), :], ((1,), (0,)), 2)
    col = lax.broadcasted_iota(jnp.int32, (B, N), 1)
    inv_ref[pl.ds(d0, B), :] = jnp.where(col < d0 + B, panel, 0.0).astype(BF)
    parts = splits(panel, 2)
    for t in range(3):
        left[t * B : (t + 1) * B, :] = parts[LEFT[2][t]]
        right[t * B : (t + 1) * B, :] = parts[RIGHT[2][t]]
    trailing(kb + 1, d0, work, left, right)

    @pl.when(kb == my_col)
    def _():
        @pl.when(kb == my_row)
        def _():
            lower_ref[...] = jnp.where(lane >= sub, upper, 0.0).T

        @pl.when(kb < my_row)
        def _():
            work[pl.ds(d0, B), :] = panel
            lower_ref[...] = work[pl.ds(d0, B), pl.ds(pl.multiple_of(my_row * B, B), B)].T


def below_tiles(a, inv_ref):
    tiles = []
    for c in range(0, N, 2 * B):
        end = c + 2 * B
        tiles.append(
            lax.dot_general(
                a[:, :end], inv_ref[c:end, :end], (((1,), (1,)), ((), ())), preferred_element_type=F32
            )
        )
    return tiles


def below_rows(portion, inv_ref, lower_ref, keep_ref, my_col, below_ref, first_ref, wide, write):
    safe = jnp.minimum(my_col, NB - 1)

    def rows(i, _):
        a = jnp.concatenate(
            [
                jnp.concatenate([portion[k // 4, k // 2 % 2, k % 2, 2 * i + t // 2, t % 2] for k in range(8)], axis=1)
                for t in range(4)
            ],
            axis=0,
        )
        for c, out in enumerate(below_tiles(a, inv_ref)):
            cols = slice(2 * B * c, 2 * B * (c + 1))
            for t in range(4):
                l = 4 * i + t
                kept = out[t * B : (t + 1) * B, :] * keep_ref[l]
                wide[t * B : (t + 1) * B, cols] = kept
                below_ref[pl.ds(pl.multiple_of(l * B, B), B), cols] = kept.astype(BF)
        for t in range(4):
            first_ref[4 * i + t] = wide[t * B : (t + 1) * B, pl.ds(pl.multiple_of(safe * B, B), B)]
        write(i).start()
        return 0

    lax.fori_loop(0, 4, rows, 0)
    first_ref[0] = lower_ref[...]


def below_columns(cols, inv_ref, keep_ref, panel_ref, write):
    def some(i, _):
        a = jnp.concatenate(
            [
                jnp.concatenate([cols[k // 4, k // 2 % 2, k % 2, 4 * i + t] for k in range(8)], axis=1)
                for t in range(4)
            ],
            axis=0,
        )
        for c, out in enumerate(below_tiles(a, inv_ref)):
            for t in range(4):
                m = 4 * i + t
                kept = out[t * B : (t + 1) * B, :] * keep_ref[16 + m]
                panel_ref[pl.ds(pl.multiple_of(m * B, B), B), 2 * B * c : 2 * B * (c + 1)] = kept.astype(BF)
        write(i).start()
        return 0

    lax.fori_loop(0, 2, some, 0)


def factor_kernel(piece, keep_ref, below_hbm, panel_hbm, first_hbm, sq, portion, cols, inv_ref, lower_ref, work, left, right, wide, below_ref, panel_ref, first_ref, out_sem, *sems):
    my_row, my_col = lax.axis_index("row"), lax.axis_index("col")

    def write(i):
        rows = pl.ds(4 * B * i, 4 * B)
        return pltpu.make_async_copy(below_ref.at[rows], below_hbm.at[rows], out_sem.at[i])

    def write_first():
        return pltpu.make_async_copy(first_ref, first_hbm, out_sem.at[4])

    def write_panel(i):
        rows = pl.ds(4 * B * i, 4 * B)
        return pltpu.make_async_copy(panel_ref.at[rows], panel_hbm.at[rows], out_sem.at[5 + i])

    gather = Gather(piece, sq, portion, cols, sems)
    gather.enter()
    gather.square()
    gather.begin()
    factor_start(sq, lower_ref, work, left, right)

    def step(kb, _):
        gather.during(kb)
        factor_step(kb, my_row, my_col, inv_ref, lower_ref, work, left, right)
        return 0

    lax.fori_loop(0, NB, step, 0)
    gather.after()
    below_rows(portion, inv_ref, lower_ref, keep_ref, my_col, below_ref, first_ref, wide, write)
    write_first().start()
    gather.end()
    below_columns(cols, inv_ref, keep_ref, panel_ref, write_panel)
    gather.finish()
    for i in range(4):
        write(i).wait()
    write_first().wait()
    for i in range(2):
        write_panel(i).wait()


FACTOR_OUT = (
    jax.ShapeDtypeStruct((16 * B, N), BF),
    jax.ShapeDtypeStruct((8 * B, N), BF),
    jax.ShapeDtypeStruct((16, B, B), F32),
)
FACTOR_SCRATCH = (
    ((2, 2, 2, 2, 4, B, B), BF),
    ((2, 2, 2, 8, 2, B, B), BF),
    ((2, 2, 2, 8, B, B), BF),
    ((N, N), BF),
    ((B, B), F32),
    ((N + B, N), F32),
    ((3 * B, N), BF),
    ((3 * B, N), BF),
    ((4 * B, N), F32),
)


def factor(piece, keep):
    return pl.pallas_call(
        factor_kernel,
        out_shape=FACTOR_OUT,
        in_specs=[VM, SM],
        out_specs=(ANY, ANY, ANY),
        scratch_shapes=[pltpu.VMEM(s, d) for s, d in FACTOR_SCRATCH]
        + [pltpu.VMEM(o.shape, o.dtype) for o in FACTOR_OUT]
        + [pltpu.SemaphoreType.DMA((7,))]
        + [pltpu.SemaphoreType.DMA((n,)) for n in Gather.SEMS],
        compiler_params=params(32, collective_id=2, has_side_effects=True),
    )(piece, keep)


def schur_kernel(tab, front, arrived, below, panel, first, out_ref):
    i = pl.program_id(0)
    my_col = lax.axis_index("col")
    product = lax.dot_general(below[...], panel[...], (((1,), (1,)), ((), ())), preferred_element_type=F32)
    sub = lax.broadcasted_iota(jnp.int32, (B, 8, B), 1)
    taken = (sub == 0) & (my_col < NB)
    for s in range(2):
        l = 2 * i + s
        values = []
        for m in range(8):
            value = -product[s * B : (s + 1) * B, m * B : (m + 1) * B]
            for h in range(2):
                valid = tab[AT_RCH + h * 16 + l] == tab[AT_CCH + h * 8 + m]
                at = jnp.where(valid, tab[AT_RSRC + h * 16 + l] + tab[AT_CSRC + h * 8 + m], 0)
                value = value + jnp.where(valid, arrived[at].astype(F32), 0.0)
            if s == 0:
                value = jnp.where(l == 0, 0.0, value)
            if m == 0:
                value = jnp.where(my_col < NB, first[s], value)
            values.append(value)
        drop = taken | (l == 0) if s == 0 else taken
        out_ref[s] = jnp.swapaxes(jnp.stack(values), 0, 1) + jnp.where(drop, 0.0, front[s].astype(F32))


def schur(tab, front, arrived, below, panel, first):
    full = lambda shape: pl.BlockSpec(shape, lambda i, t: (0,) * len(shape))
    return pl.pallas_call(
        schur_kernel,
        out_shape=jax.ShapeDtypeStruct((16, B, 8, B), F32),
        grid_spec=pltpu.PrefetchScalarGridSpec(
            num_scalar_prefetch=1,
            grid=(8,),
            in_specs=[
                pl.BlockSpec((2, B, 8, B), lambda i, t: (i, 0, 0, 0)),
                full((256, B, B)),
                pl.BlockSpec((2 * B, N), lambda i, t: (i, 0)),
                full((N, N)),
                pl.BlockSpec((2, B, B), lambda i, t: (i, 0, 0)),
            ],
            out_specs=pl.BlockSpec((2, B, 8, B), lambda i, t: (i, 0, 0, 0)),
        ),
        compiler_params=params(28),
    )(tab, front, arrived, below, panel, first)


def per_device(child_update_blocks, child_pivot_panel, child_map, coupled, parent_front):
    my_row, my_col = lax.axis_index("row"), lax.axis_index("col")
    front = parent_front.reshape(16, B, 8, B)
    outgoing = contributions(child_map, child_pivot_panel.reshape(8, 2, B, B), child_update_blocks.reshape(16, B, 8, B))
    incoming = lax.all_to_all(outgoing, ("row", "col"), split_axis=0, concat_axis=0, tiled=True)
    arrived = incoming.reshape(256, B, B)
    later_map, later_coupled, _ = lax.optimization_barrier((child_map, coupled, outgoing))
    in_tab = table(incoming_kernel, 96, later_map)
    kept = jnp.concatenate([jnp.ones((NB,), F32), later_coupled.astype(F32)])
    keep = jnp.concatenate(
        [
            lax.dynamic_index_in_dim(kept.reshape(16, 8), my_row, 1, keepdims=False),
            lax.dynamic_index_in_dim(kept.reshape(8, 16), my_col, 1, keepdims=False),
        ]
    )
    pivots = pivot_columns(in_tab, arrived, front[:, :, 0, :])
    below, panel, first = factor(pivots.reshape(8, 2, B, B), keep)
    out = schur(in_tab, front, arrived, below, panel, first)
    return out.reshape(1, 16, B, 1, 8, B)


def solution(mesh):
    in_specs = (
        P("row", None, None, "col", None, None),
        P("row", None, None, "col", None),
        P(),
        P(),
        P("row", None, None, "col", None, None),
    )
    out_specs = P("row", None, None, "col", None, None)
    return jax.shard_map(per_device, mesh=mesh, in_specs=in_specs, out_specs=out_specs, check_vma=False)
```
